256 devices in a mesh: tm: 64 (over y, z, core), space: 4 (over x).
Axes of the slice: x: 4, y: 4, z: 8, core: 2. Of those that a mesh axis runs over, the one named last changes fastest.
Arguments:
- latents: bfloat16 [1024, 2, 256, 128], P('tm', None, 'space'), may hold values from -6 to 6
- cotangent: bfloat16 [1024, 2, 256, 128], P('tm', None, 'space'), may hold values from -6 to 6
- clip_lengths: int32 [32], replicated, may hold values from 1 to 64, 1024 in all
- context_offset: int32 [32], replicated, may hold values from 0 to 63
- conv_weight: bfloat16 [3, 3, 128, 128], replicated, may hold values from -0.1875 to 0.1875
- w_query: bfloat16 [128, 128], replicated, may hold values from -0.5 to 0.5
- w_key: bfloat16 [128, 128], replicated, may hold values from -0.5 to 0.5
- w_value: bfloat16 [128, 128], replicated, may hold values from -0.5 to 0.5
- w_out: bfloat16 [128, 128], replicated, may hold values from -0.5 to 0.5
- query_gain: float32 [128], replicated, may hold values from 0.5 to 2
- key_gain: float32 [128], replicated, may hold values from 0.5 to 2
Outputs:
- outputs: bfloat16 [1024, 2, 256, 128], P('tm', None, 'space')
- latent_grad: bfloat16 [1024, 2, 256, 128], P('tm', None, 'space')
The draws below stay inside these ranges and needn't reach their ends.
Inputs may be any that keep to these rules, and one draw needn't show every extreme that they name: `clip_lengths`: the clips cover the 1024 frames in order, one after another; some clip has exactly 64 frames.
All inputs are finite; a program needn't handle non-finite values.
Results may differ from the reference program's by a relative error of at most 0.0095.
Values may be sent and summed in bfloat16 or wider, within the bound.
A program may use at most 128 MiB of HBM per device.

```python
import math
import jax
import jax.numpy as jnp
import numpy as np
from jax import lax

C = 128
HEAD = 64
ROWS = 2
TILE_W = 64
FRAMES = 1024
WIDTH = 256
CLIP_MAX = 64
CLIPS = 32
N_SPACE = 4


def draw_query_gain(key, part):
    key = jax.random.fold_in(key, 11)
    return jax.random.uniform(key, (C,), jnp.float32, 0.5, 1.5)


def draw_key_gain(key, part):
    key = jax.random.fold_in(key, 12)
    return jax.random.uniform(key, (C,), jnp.float32, 0.5, 1.5)


def touch_ends(values, stream_key, smallest, high):
    extent = values.shape
    place = [jax.random.randint(jax.random.fold_in(stream_key, axis), (), 0, extent[axis]) for axis in range(len(extent))]
    values = values.at[tuple(place)].set(smallest)
    longest = extent.index(max(extent))
    place[longest] = (place[longest] + 1) % extent[longest]
    return values.at[tuple(place)].set(high)


def block_levels(key, shape, shards, low, top_value):
    loudness, own = 1.0, jax.random.fold_in(key, 6)
    for axis_at, parts in shards:
        steps = jnp.exp(jax.random.uniform(jax.random.fold_in(own, axis_at), (parts,), jnp.float32, low / len(shards), top_value / len(shards)))
        loudness = loudness * jnp.repeat(steps, shape[axis_at] // parts).reshape([-1 if axis == axis_at else 1 for axis in range(len(shape))])
    return loudness


def profile(count, total, limit, lean):
    portions = [(1 << 20) // math.isqrt(rank ** lean) + 1 for rank in range(2, count + 1)]
    spare, holding = total - limit - (count - 1), [1] * (count - 1)
    while spare > 0:
        movable = [i for i in range(count - 1) if holding[i] < limit]
        mass, remaining = sum([portions[i] for i in movable]), spare
        for i in movable:
            more = min(limit - holding[i], max(1, remaining * portions[i] // mass), spare)
            holding[i] = holding[i] + more
            spare = spare - more
    return np.array([limit] + holding)


def ragged_sizes(stream_key, number_of, total, most, lean):
    if number_of == 2:
        one = jax.random.randint(stream_key, (), max(1, total - most), min(most, total - 1) + 1)
        return jnp.stack([one, total - one])
    sizes = jnp.asarray(profile(number_of, total, most, lean), jnp.int32)
    twos = (number_of - 1) // 2
    giver, sink = sizes[1:1 + 2 * twos:2], sizes[2:2 + 2 * twos:2]
    slack = jnp.minimum(giver - 1, most - sink)
    shifted = jax.random.randint(jax.random.fold_in(stream_key, 1), (twos,), 0, 1 << 20) % (slack + 1)
    sizes = sizes.at[1:1 + 2 * twos:2].set(giver - shifted).at[2:2 + 2 * twos:2].set(sink + shifted)
    return sizes[jax.random.permutation(jax.random.fold_in(stream_key, 2), number_of)]


def centred(rng, dims, scale, most, shards=(), kind=jnp.bfloat16):
    values = scale * jax.random.normal(rng, dims, jnp.float32)
    if shards:
        values = values * block_levels(rng, dims, shards, -0.22, 0.18)
    return jnp.clip(values, -most, most).astype(kind)


def setup_inputs(seed: int = 0) -> dict:
    key_list = jax.random.split(jax.random.key(seed), 12)
    return {
        "latents": centred(key_list[0], (FRAMES, ROWS, WIDTH, C), 1.0, 6.0, ((0, 64), (2, 4))),
        "cotangent": centred(key_list[1], (FRAMES, ROWS, WIDTH, C), 1.0, 6.0, ((0, 64), (2, 4))),
        "clip_lengths": ragged_sizes(key_list[2], CLIPS, FRAMES, CLIP_MAX, 2).astype(jnp.int32),
        "context_offset": touch_ends(jax.random.randint(key_list[3], (CLIPS,), 0, CLIP_MAX), jax.random.fold_in(key_list[3], 1), 0, CLIP_MAX - 1).astype(jnp.int32),
        "conv_weight": centred(key_list[4], (3, 3, C, C), (9 * C) ** -0.5, 0.1875),
        "w_query": centred(key_list[5], (C, C), C ** -0.5, 0.5),
        "w_key": centred(key_list[6], (C, C), C ** -0.5, 0.5),
        "w_value": centred(key_list[7], (C, C), C ** -0.5, 0.5),
        "w_out": centred(key_list[8], (C, C), C ** -0.5, 0.5),
        "query_gain": draw_query_gain(jax.random.fold_in(key_list[11], 71), 0),
        "key_gain": draw_key_gain(jax.random.fold_in(key_list[11], 71), 0),
    }


highest = lax.Precision.HIGHEST
epsilon = 1e-06

def to_bf16(tensor):
    return lax.optimization_barrier(tensor.astype(jnp.bfloat16))

def clip_context(clip_lengths, context_offset, frame_ids):
    clip_end = jnp.cumsum(clip_lengths).astype(jnp.int32)
    clip_start = clip_end - clip_lengths
    targets = clip_start + context_offset % clip_lengths
    inside = (frame_ids[:, None] >= clip_start[None, :]) & (frame_ids[:, None] < clip_end[None, :])
    return lax.optimization_barrier(jnp.sum(jnp.where(inside, targets[None, :], 0), axis=1)).astype(jnp.int32)

def matmul(left_side, right_side):
    return jnp.einsum('...c,cd->...d', left_side.astype(jnp.float32), right_side.astype(jnp.float32), precision=highest)

def matmul_back(left_side, right_side):
    return jnp.einsum('...d,cd->...c', left_side.astype(jnp.float32), right_side.astype(jnp.float32), precision=highest)

def head_split(tensor):
    batch_count, tokens, width_count = tensor.shape
    return tensor.reshape(batch_count, tokens, width_count // HEAD, HEAD).transpose(0, 2, 1, 3)

def head_join(tensor):
    batch_count, head_count, tokens, head_size = tensor.shape
    return tensor.transpose(0, 2, 1, 3).reshape(batch_count, tokens, head_count * head_size)

def head_norm(raw_proj, gain_vector):
    shaped = raw_proj.reshape(raw_proj.shape[:-1] + (raw_proj.shape[-1] // HEAD, HEAD))
    factor = lax.rsqrt(lax.optimization_barrier(jnp.mean(shaped * shaped, axis=-1, keepdims=True)) + epsilon)
    return (shaped * factor).reshape(raw_proj.shape) * gain_vector

def head_norm_back(raw_proj, gain_vector, grad_in):
    new_shape = raw_proj.shape[:-1] + (raw_proj.shape[-1] // HEAD, HEAD)
    shaped = raw_proj.reshape(new_shape)
    scaled = (grad_in * gain_vector).reshape(new_shape)
    factor = lax.rsqrt(lax.optimization_barrier(jnp.mean(shaped * shaped, axis=-1, keepdims=True)) + epsilon)
    inner_mean = lax.optimization_barrier(jnp.mean(shaped * scaled, axis=-1, keepdims=True))
    return (factor * scaled - shaped * factor * factor * factor * inner_mean).reshape(raw_proj.shape)

def conv_sum(padded, conv_weight, transpose_it):
    row_span = padded.shape[1] - 2
    col_span = padded.shape[2] - 2
    result = jnp.zeros(padded.shape[:1] + (row_span, col_span, padded.shape[3]), jnp.float32)
    for row_at in range(3):
        for col_at in range(3):
            if transpose_it:
                window_piece = padded[:, 2 - row_at:2 - row_at + row_span, 2 - col_at:2 - col_at + col_span]
                result = result + matmul_back(window_piece, conv_weight[row_at, col_at])
            else:
                window_piece = padded[:, row_at:row_at + row_span, col_at:col_at + col_span]
                result = result + matmul(window_piece, conv_weight[row_at, col_at])
    return result

def to_windows(tensor):
    frame_total = tensor.shape[0]
    shaped = tensor.reshape(frame_total, ROWS, N_SPACE, TILE_W, C).transpose(0, 2, 1, 3, 4)
    return shaped.reshape(frame_total * N_SPACE, ROWS * TILE_W, C)

def from_windows(tensor):
    frame_total = tensor.shape[0] // N_SPACE
    shaped = tensor.reshape(frame_total, N_SPACE, ROWS, TILE_W, C).transpose(0, 2, 1, 3, 4)
    return shaped.reshape(frame_total, ROWS, WIDTH, C)

def pad_frame(tensor):
    return jnp.pad(tensor, ((0, 0), (1, 1), (1, 1), (0, 0)))

def reference(latents, cotangent, clip_lengths, context_offset, conv_weight, w_query, w_key, w_value, w_out, query_gain, key_gain):
    frame_total = latents.shape[0]
    block_size = 2
    block_count = frame_total // block_size
    token_count = ROWS * TILE_W
    score_scale = 1.0 / math.sqrt(HEAD)
    context = clip_context(clip_lengths, context_offset, jnp.arange(frame_total, dtype=jnp.int32))

    def hidden_of(frames):
        return to_bf16(frames.astype(jnp.float32) + conv_sum(pad_frame(frames), conv_weight, False))

    def first_pass(frames):
        hidden = to_windows(hidden_of(frames))
        key_tiles = to_bf16(head_norm(matmul(hidden, w_key), key_gain))
        value_tiles = to_bf16(matmul(hidden, w_value))
        return (key_tiles, value_tiles)
    latent_blocks = latents.reshape(block_count, block_size, ROWS, WIDTH, C)
    grad_blocks = cotangent.reshape(block_count, block_size, ROWS, WIDTH, C)
    context_blocks = context.reshape(block_count, block_size)
    key_all, value_all = lax.map(first_pass, latent_blocks)
    key_all = key_all.reshape(frame_total, N_SPACE, token_count, C)
    value_all = value_all.reshape(frame_total, N_SPACE, token_count, C)

    def second_pass(inputs):
        frames, grad_frames, targets = inputs
        hidden = to_windows(hidden_of(frames))
        query_raw = matmul(hidden, w_query)
        queries = to_bf16(head_norm(query_raw, query_gain))
        context_keys = key_all[targets].reshape(block_size * N_SPACE, token_count, C)
        context_values = value_all[targets].reshape(block_size * N_SPACE, token_count, C)
        query_heads = head_split(queries).astype(jnp.float32)
        key_heads = head_split(context_keys).astype(jnp.float32)
        value_heads = head_split(context_values).astype(jnp.float32)
        scores = jnp.einsum('bhqd,bhkd->bhqk', query_heads, key_heads, precision=highest) * score_scale
        row_top = lax.optimization_barrier(jnp.max(scores, axis=-1, keepdims=True))
        raised = jnp.exp(scores - row_top)
        probabilities = raised / lax.optimization_barrier(jnp.sum(raised, axis=-1, keepdims=True))
        weights = to_bf16(probabilities).astype(jnp.float32)
        attended = to_bf16(head_join(jnp.einsum('bhqk,bhkd->bhqd', weights, value_heads, precision=highest)))
        outputs = to_bf16(hidden.astype(jnp.float32) + matmul(attended, w_out))
        grad_out = to_windows(grad_frames)
        grad_attended = to_bf16(matmul_back(grad_out, w_out))
        grad_heads = head_split(grad_attended).astype(jnp.float32)
        grad_probs = jnp.einsum('bhqd,bhkd->bhqk', grad_heads, value_heads, precision=highest)
        row_sum = lax.optimization_barrier(jnp.sum(grad_probs * probabilities, axis=-1, keepdims=True))
        grad_scores = to_bf16(probabilities * (grad_probs - row_sum) * score_scale).astype(jnp.float32)
        grad_queries = head_join(jnp.einsum('bhqk,bhkd->bhqd', grad_scores, key_heads, precision=highest))
        key_terms = head_join(jnp.einsum('bhqk,bhqd->bhkd', grad_scores, query_heads, precision=highest))
        value_terms = head_join(jnp.einsum('bhqk,bhqd->bhkd', weights, grad_heads, precision=highest))
        grad_query_raw = to_bf16(head_norm_back(query_raw, query_gain, grad_queries))
        return (from_windows(outputs), grad_query_raw, key_terms, value_terms)
    outputs, grad_query_raw, key_terms, value_terms = lax.map(second_pass, (latent_blocks, grad_blocks, context_blocks))
    key_terms = key_terms.reshape(frame_total, N_SPACE, token_count, C)
    value_terms = value_terms.reshape(frame_total, N_SPACE, token_count, C)
    grad_keys = jax.ops.segment_sum(key_terms, context, num_segments=frame_total)
    grad_values = jax.ops.segment_sum(value_terms, context, num_segments=frame_total)
    grad_keys = grad_keys.reshape(block_count, block_size * N_SPACE, token_count, C)
    grad_values = grad_values.reshape(block_count, block_size * N_SPACE, token_count, C)

    def third_pass(inputs):
        frames, grad_frames, grad_query_block, grad_key_block, grad_value_block = inputs
        hidden = to_windows(hidden_of(frames))
        key_raw = matmul(hidden, w_key)
        grad_key_raw = to_bf16(head_norm_back(key_raw, key_gain, grad_key_block))
        grad_values_low = to_bf16(grad_value_block)
        grad_hidden = to_windows(grad_frames).astype(jnp.float32) + matmul_back(grad_query_block, w_query)
        grad_hidden = grad_hidden + matmul_back(grad_key_raw, w_key) + matmul_back(grad_values_low, w_value)
        grad_hidden = to_bf16(from_windows(grad_hidden))
        return to_bf16(grad_hidden.astype(jnp.float32) + conv_sum(pad_frame(grad_hidden), conv_weight, True))
    latent_grad = lax.map(third_pass, (latent_blocks, grad_blocks, grad_query_raw, grad_keys, grad_values))
    outputs = outputs.reshape(frame_total, ROWS, WIDTH, C)
    latent_grad = latent_grad.reshape(frame_total, ROWS, WIDTH, C)
    return (outputs, latent_grad)
```

```python
import functools

import jax
import jax.numpy as jnp
from jax import lax
from jax.experimental import pallas as pl
from jax.experimental.pallas import tpu as pltpu
from jax.sharding import PartitionSpec as P

HEAD = 64
SPAN = 4
GROUP = 4
EPS = 1e-6
MESH = pl.DeviceIdType.MESH
VMEM = pltpu.VMEM
BF = jnp.bfloat16
F32 = jnp.float32
NT = (((1,), (1,)), ((), ()))
TN = (((0,), (0,)), ((), ()))


def dot(a, b):
    return jnp.dot(a, b, preferred_element_type=F32)


def dot_nt(a, b):
    return lax.dot_general(a, b, NT, preferred_element_type=F32)


def dot_tn(a, b):
    return lax.dot_general(a, b, TN, preferred_element_type=F32)


def partners():
    x, t = lax.axis_index("space"), lax.axis_index("tm")
    nx, nt = lax.axis_size("space"), lax.axis_size("tm")
    sides = [lax.rem(x + 1, nx), lax.rem(x + nx - 1, nx)]
    ups = [lax.rem(t + k, nt) for k in range(1, SPAN + 1)]
    downs = [lax.rem(t + nt - k, nt) for k in range(1, SPAN + 1)]
    return sides, ups, downs


def enter():
    sides, ups, downs = partners()
    barrier = pltpu.get_barrier_semaphore()
    for s in sides:
        pl.semaphore_signal(barrier, inc=1, device_id={"space": s}, device_id_type=MESH)
    for t in ups + downs:
        pl.semaphore_signal(barrier, inc=1, device_id={"tm": t}, device_id_type=MESH)
    return lambda: pl.semaphore_wait(barrier, len(sides) + len(ups) + len(downs))


def remote(src, dst, send, recv, device):
    return pltpu.make_async_remote_copy(
        src_ref=src, dst_ref=dst, send_sem=send, recv_sem=recv, device_id=device, device_id_type=MESH
    )


def over_clips(lens, offs, body, init):
    def step(j, carry):
        start, rest = carry[0], carry[1:]
        length = lens[j]
        end = start + length
        target = start + lax.rem(offs[j], length)
        return (end,) + tuple(body(rest, start, end, target))

    return lax.fori_loop(0, lens.shape[0], step, (jnp.int32(0),) + tuple(init))[1:]


def build_conv(cw_ref, w3):
    for b in range(3):
        for rin in range(2):
            for rout in range(2):
                w3[
                    b * 256 + rin * 128 : b * 256 + rin * 128 + 128, rout * 128 : rout * 128 + 128
                ] = cw_ref[rin - rout + 1, b]


def joined(ref, f):
    return jnp.concatenate([ref[f, 0:64, :], ref[f, 64:128, :]], axis=1).astype(F32)


def shifted(x, left, right):
    row = lax.broadcasted_iota(jnp.int32, (64, 1), 0)
    before = jnp.where(row == 0, left, pltpu.roll(x, 1, 0))
    after = jnp.where(row == 63, right, pltpu.roll(x, 63, 0))
    return before.astype(BF), x.astype(BF), after.astype(BF)


def conv(xs, w3):
    taps = [jnp.concatenate(shifted(*x), axis=1) for x in xs]
    taps = jnp.concatenate(taps, axis=0) if len(taps) > 1 else taps[0]
    whole = jnp.concatenate([x[0] for x in xs], axis=0) if len(xs) > 1 else xs[0][0]
    return whole + dot(taps, w3[...])


def conv_back(xs, w3):
    parts = [shifted(*x) for x in xs]
    cat = lambda i: jnp.concatenate([p[i] for p in parts], axis=0) if len(parts) > 1 else parts[0][i]
    whole = jnp.concatenate([x[0] for x in xs], axis=0) if len(xs) > 1 else xs[0][0]
    out = dot_nt(cat(0), w3[512:768, :])
    out = out + dot_nt(cat(1), w3[256:512, :])
    out = out + dot_nt(cat(2), w3[0:256, :])
    return whole + out


def put(ref, f, y):
    ref[f, 0:64, :] = y[:, :128].astype(ref.dtype)
    ref[f, 64:128, :] = y[:, 128:].astype(ref.dtype)


def edges_out(ref, f, edges, at):
    x = joined(ref, f)
    edges[0, pl.ds(at, 1), :] = x[63:64]
    edges[1, pl.ds(at, 1), :] = x[0:1]


def mask_edges(halo):
    x, nx = lax.axis_index("space"), lax.axis_size("space")
    halo[0] = jnp.where(x > 0, halo[0], 0.0)
    halo[1] = jnp.where(x < nx - 1, halo[1], 0.0)


def with_halo(ref, halo, f):
    return joined(ref, f), halo[0, pl.ds(f, 1), :], halo[1, pl.ds(f, 1), :]


def forward_kernel(
    lens, offs, lat, cw, hid, far, w3, edges, halo, ctx, got, side_send, side_recv, ctx_send, ctx_recv
):
    frames = lat.shape[0]
    ready = enter()
    sides, ups, downs = partners()
    first = lax.axis_index("tm") * frames
    last = first + frames - 1
    for f in range(frames):
        edges_out(lat, f, edges, f)
    build_conv(cw, w3)

    def scan(c, start, end, target):
        top, low, below, above = c
        inside = (target >= first) & (target <= last)
        top = jnp.where(inside, jnp.maximum(top, target), top)
        low = jnp.where(inside, jnp.minimum(low, target), low)
        below = jnp.where((start <= first) & (first < end), target, below)
        above = jnp.where((start <= last) & (last < end), target, above)
        return top, low, below, above

    top, low, below, above = over_clips(lens, offs, scan, (first, last, first, last))
    top, low = top - first, low - first
    up_at = jnp.clip((first - below + frames - 1) // frames, 1, SPAN) - 1
    down_at = jnp.clip((above - first) // frames, 1, SPAN) - 1 + SPAN

    ready()
    halos = [
        remote(edges.at[i], halo.at[i], side_send.at[i], side_recv.at[i], {"space": sides[i]})
        for i in range(2)
    ]
    for c in halos:
        c.start()
    for c in halos:
        c.wait()
    mask_edges(halo)
    pair = conv([with_halo(lat, halo, top), with_halo(lat, halo, low)], w3)
    put(ctx, 0, pair[:64])
    put(ctx, 1, pair[64:])
    sends = []
    for k in range(SPAN):
        sends.append(remote(ctx.at[0], got.at[k], ctx_send.at[k], ctx_recv.at[k], {"tm": ups[k]}))
        j = SPAN + k
        sends.append(remote(ctx.at[1], got.at[j], ctx_send.at[j], ctx_recv.at[j], {"tm": downs[k]}))
    for c in sends:
        c.start()

    @pl.loop(0, frames // GROUP)
    def _(g):
        y = conv([with_halo(lat, halo, g * GROUP + i) for i in range(GROUP)], w3)
        for i in range(GROUP):
            put(hid, g * GROUP + i, y[i * 64 : i * 64 + 64])

    for c in sends:
        c.wait()
    far[0] = got[up_at]
    far[1] = got[down_at]


def block_ones(rows, cols, rblock, cblock, value):
    r = lax.broadcasted_iota(jnp.int32, (rows, cols), 0) // rblock
    c = lax.broadcasted_iota(jnp.int32, (rows, cols), 1) // cblock
    return jnp.where(r == c, value, 0.0).astype(BF)


def middle_kernel(
    lens, offs, hid, far, ct, wq, wk, wv, wo, qg, kg, out, gh, gfar,
    slots, qs, un, sc, kk, vv, ga, gq, att, dk, dv, wqk, wvo, wqkt, wvot,
):
    frames = hid.shape[0]
    first = lax.axis_index("tm") * frames
    last = first + frames - 1

    def assign(c, start, end, target):
        at = target - first
        slot = jnp.where(at < 0, frames, jnp.where(at >= frames, frames + 1, at))

        def one(f, _):
            slots[f] = slot
            return 0

        lax.fori_loop(jnp.maximum(start - first, 0), jnp.minimum(end - first, frames), one, 0)
        return c

    over_clips(lens, offs, assign, ())

    zero = jnp.zeros((128, 128), BF)
    wqk[:, :128] = wq[...]
    wqk[:, 128:] = wk[...]
    wvo[:128, :128] = wv[...]
    wvo[:128, 128:] = zero
    wvo[128:, :128] = zero
    wvo[128:, 128:] = wo[...].astype(F32).T.astype(BF)
    wqkt[:128, :] = wq[...].astype(F32).T.astype(BF)
    wqkt[128:, :] = wk[...].astype(F32).T.astype(BF)
    wvot[:128, :128] = wv[...].astype(F32).T.astype(BF)
    wvot[:128, 128:] = zero
    wvot[128:, :128] = zero
    wvot[128:, 128:] = wo[...]
    mean4 = block_ones(256, 256, HEAD, HEAD, 1.0 / HEAD)
    ones2 = block_ones(256, 256, 128, 128, 1.0)
    spread = block_ones(128, 256, HEAD, 128, 1.0)
    gains = jnp.concatenate([qg[...], kg[...]], axis=1)
    lane = lax.broadcasted_iota(jnp.int32, (1, 128), 1)
    head0 = lane < HEAD

    def project(h, c, at, real):
        qk = dot(h, wqk[...])
        vg = dot(jnp.concatenate([h, c], axis=1), wvo[...])
        s = lax.rsqrt(dot((qk * qk).astype(BF), mean4) + EPS)
        u = qk * s
        y = u * gains
        for i in range(2):
            rows = slice(i * 128, i * 128 + 128)
            f = at + i
            un[f] = u[rows]
            sc[f] = s[rows]
            key, val = y[rows, 128:], vg[rows, :128]
            kk[f, :128] = jnp.where(head0, key, 0.0).astype(BF)
            kk[f, 128:] = jnp.where(head0, 0.0, key).astype(BF)
            vv[f, :128] = jnp.where(head0, val, 0.0).astype(BF)
            vv[f, 128:] = jnp.where(head0, 0.0, val).astype(BF)
            if real:
                qs[f] = y[rows, :128].astype(BF)
                ga[f] = vg[rows, 128:].astype(BF)

    @pl.loop(0, frames // 2)
    def _(g):
        at = pl.ds(g * 2, 2)
        project(hid[at].reshape(256, 128), ct[at].reshape(256, 128), g * 2, True)

    both = far[...].reshape(256, 128)
    project(both, both, frames, False)

    dk[...] = jnp.zeros_like(dk)
    dv[...] = jnp.zeros_like(dv)

    @pl.loop(0, frames // GROUP)
    def _(g):
        at = [g * GROUP + i for i in range(GROUP)]
        slot = [slots[f] for f in at]
        n = range(GROUP)
        raised = [jnp.exp(dot_nt(qs[at[i]], kk[slot[i]]) * 0.125) for i in n]
        total = [dot(r.astype(BF), ones2) for r in raised]
        prob = [raised[i] / total[i] for i in n]
        low = [p.astype(BF) for p in prob]
        o = [dot(low[i], vv[slot[i]]) for i in n]
        gp = [dot_nt(ga[at[i]], vv[slot[i]]) for i in n]
        for i in n:
            att[at[i]] = o[i].astype(BF)
        delta = [dot((o[i] * ga[at[i]].astype(F32)).astype(BF), spread) for i in n]
        ds = [(prob[i] * (gp[i] - delta[i]) * 0.125).astype(BF) for i in n]
        for i in n:
            gq[at[i]] = dot(ds[i], kk[slot[i]])
        kt = [dot_tn(qs[at[i]], ds[i]) for i in n]
        vt = [dot_tn(ga[at[i]], low[i]) for i in n]
        for i in n:
            dk[slot[i], :64] += kt[i][:64, :128]
            dk[slot[i], 64:] += kt[i][64:, 128:]
            dv[slot[i], :64] += vt[i][:64, :128]
            dv[slot[i], 64:] += vt[i][64:, 128:]

    def finish(at, real):
        rows = []
        for i in range(2):
            f = at + i
            left = gq[f] if real else jnp.zeros((128, 128), F32)
            rows.append(jnp.concatenate([left, dk[f].T], axis=1))
        e = jnp.concatenate(rows, axis=0) * gains
        u = jnp.concatenate([un[at], un[at + 1]], axis=0)
        s = jnp.concatenate([sc[at], sc[at + 1]], axis=0)
        m = dot((e * u).astype(BF), mean4)
        raw = (s * (e - u * m)).astype(BF)
        val = jnp.concatenate([dv[at].T, dv[at + 1].T], axis=0).astype(BF)
        a = jnp.concatenate([att[at], att[at + 1]], axis=0) if real else val
        back = dot(raw, wqkt[...])
        vo = dot(jnp.concatenate([val, a], axis=1), wvot[...])
        return back + vo[:, :128], vo[:, 128:]

    @pl.loop(0, frames // 2)
    def _(g):
        back, o = finish(g * 2, True)
        at = pl.ds(g * 2, 2)
        out[at] = (hid[at].astype(F32) + o.reshape(2, 128, 128)).astype(BF)
        gh[at] = (ct[at].astype(F32) + back.reshape(2, 128, 128)).astype(BF)

    back, _ = finish(frames, False)
    gfar[...] = back.reshape(2, 128, 128).astype(BF)


def backward_kernel(
    lens, offs, gh, gfar, cw, lg, w3, base, edges, halo, ctx, got, side_send, side_recv, ctx_send, ctx_recv
):
    frames = gh.shape[0]
    ready = enter()
    sides, ups, downs = partners()
    first = lax.axis_index("tm") * frames
    last = first + frames - 1
    for f in range(frames):
        edges_out(gh, f, edges, f)
    for f in range(2):
        edges_out(gfar, f, edges, frames + f)
    build_conv(cw, w3)

    def scan(c, start, end, target):
        top, low = c[0], c[1]
        inside = (target >= first) & (target <= last)
        top = jnp.where(inside, jnp.maximum(top, target), top)
        low = jnp.where(inside, jnp.minimum(low, target), low)
        hits = []
        for k in range(1, SPAN + 1):
            f = first + k * frames
            hits.append(jnp.where(inside & (start <= f) & (f < end), 1, c[1 + k]))
        for k in range(1, SPAN + 1):
            f = last - k * frames
            hits.append(jnp.where(inside & (start <= f) & (f < end), 1, c[1 + SPAN + k]))
        return (top, low, *hits)

    top, low, *hits = over_clips(lens, offs, scan, (first, last) + (jnp.int32(0),) * (2 * SPAN))
    top, low = top - first, low - first

    ready()
    halos = [
        remote(edges.at[i], halo.at[i], side_send.at[i], side_recv.at[i], {"space": sides[i]})
        for i in range(2)
    ]
    for c in halos:
        c.start()
    for c in halos:
        c.wait()
    mask_edges(halo)
    pair = conv_back(
        [
            (joined(gfar, i), halo[0, frames + i : frames + i + 1, :], halo[1, frames + i : frames + i + 1, :])
            for i in range(2)
        ],
        w3,
    )
    put(ctx, 0, pair[:64])
    put(ctx, 1, pair[64:])
    sends = []
    for k in range(SPAN):
        sends.append(remote(ctx.at[0], got.at[k], ctx_send.at[k], ctx_recv.at[k], {"tm": downs[k]}))
        j = SPAN + k
        sends.append(remote(ctx.at[1], got.at[j], ctx_send.at[j], ctx_recv.at[j], {"tm": ups[k]}))
    for c in sends:
        c.start()

    @pl.loop(0, frames // GROUP)
    def _(g):
        y = conv_back([with_halo(gh, halo, g * GROUP + i) for i in range(GROUP)], w3)
        for i in range(GROUP):
            put(base, g * GROUP + i, y[i * 64 : i * 64 + 64])

    for c in sends:
        c.wait()
    for_top = jnp.zeros((128, 128), F32)
    for_low = jnp.zeros((128, 128), F32)
    for k in range(SPAN):
        for_top += jnp.where(hits[k] > 0, got[k].astype(F32), 0.0)
        for_low += jnp.where(hits[SPAN + k] > 0, got[SPAN + k].astype(F32), 0.0)

    @pl.loop(0, frames)
    def _(f):
        y = base[f] + jnp.where(f == top, for_top, 0.0) + jnp.where(f == low, for_low, 0.0)
        lg[f] = y.astype(BF)


def per_device(
    latents, cotangent, clip_lengths, context_offset, conv_weight, w_query, w_key, w_value, w_out, query_gain, key_gain
):
    frames, rows, width, channels = latents.shape
    cells = rows * width
    flat = (frames, cells, channels)
    lat, ct = latents.reshape(flat), cotangent.reshape(flat)
    smem = pl.BlockSpec(memory_space=pltpu.SMEM)
    vmem = pl.BlockSpec(memory_space=VMEM)
    edge_rows = frames + 8
    comm = lambda: [
        VMEM((2, edge_rows, 256), F32),
        VMEM((2, edge_rows, 256), F32),
        VMEM((2, cells, channels), BF),
        VMEM((2 * SPAN, cells, channels), BF),
        pltpu.SemaphoreType.DMA((2,)),
        pltpu.SemaphoreType.DMA((2,)),
        pltpu.SemaphoreType.DMA((2 * SPAN,)),
        pltpu.SemaphoreType.DMA((2 * SPAN,)),
    ]
    frames_shape = jax.ShapeDtypeStruct(flat, BF)
    pair_shape = jax.ShapeDtypeStruct((2, cells, channels), BF)
    with jax.named_scope("forward_conv_and_context"):
        hid, far = pl.pallas_call(
            forward_kernel,
            out_shape=(frames_shape, pair_shape),
            in_specs=[smem, smem, vmem, vmem],
            out_specs=(vmem, vmem),
            scratch_shapes=[VMEM((768, 256), BF)] + comm(),
            compiler_params=pltpu.CompilerParams(
                collective_id=0, has_side_effects=True, vmem_limit_bytes=32 << 20
            ),
        )(clip_lengths, context_offset, lat, conv_weight)
    with jax.named_scope("attention"):
        slots = frames + 2
        out, gh, gfar = pl.pallas_call(
            middle_kernel,
            out_shape=(frames_shape, frames_shape, pair_shape),
            in_specs=[smem, smem] + [vmem] * 9,
            out_specs=(vmem, vmem, vmem),
            scratch_shapes=[
                pltpu.SMEM((frames,), jnp.int32),
                VMEM((frames, 128, 128), BF),
                VMEM((slots, 128, 256), F32),
                VMEM((slots, 128, 256), F32),
                VMEM((slots, 256, 128), BF),
                VMEM((slots, 256, 128), BF),
                VMEM((frames, 128, 128), BF),
                VMEM((frames, 128, 128), F32),
                VMEM((frames, 128, 128), BF),
                VMEM((slots, 128, 128), F32),
                VMEM((slots, 128, 128), F32),
                VMEM((128, 256), BF),
                VMEM((256, 256), BF),
                VMEM((256, 128), BF),
                VMEM((256, 256), BF),
            ],
            compiler_params=pltpu.CompilerParams(vmem_limit_bytes=40 << 20),
        )(
            clip_lengths, context_offset, hid, far, ct, w_query, w_key, w_value, w_out,
            query_gain.reshape(1, channels), key_gain.reshape(1, channels),
        )
    with jax.named_scope("backward_conv_and_sums"):
        lg = pl.pallas_call(
            backward_kernel,
            out_shape=frames_shape,
            in_specs=[smem, smem, vmem, vmem, vmem],
            out_specs=vmem,
            scratch_shapes=[VMEM((768, 256), BF), VMEM(flat, F32)] + comm(),
            compiler_params=pltpu.CompilerParams(
                collective_id=1, has_side_effects=True, vmem_limit_bytes=32 << 20
            ),
        )(clip_lengths, context_offset, gh, gfar, conv_weight)
    return out.reshape(latents.shape), lg.reshape(latents.shape)


def solution(mesh):
    data = P("tm", None, "space", None)
    return jax.shard_map(
        per_device,
        mesh=mesh,
        in_specs=(data, data) + (P(),) * 9,
        out_specs=(data, data),
        check_vma=False,
    )
```

```python
import jax
import jax.numpy as jnp
from jax import lax
from jax.experimental import pallas as pl
from jax.experimental.pallas import tpu as pltpu
from jax.sharding import PartitionSpec as P

HEAD = 64
SPAN = 4
GROUP = 4
HOPS = (-1, -2, -3, -4, 1, 2, 3, 4)
EPS = 1e-6
MESH = pl.DeviceIdType.MESH
VMEM = pltpu.VMEM
BF = jnp.bfloat16
F32 = jnp.float32
NT = (((1,), (1,)), ((), ()))
TN = (((0,), (0,)), ((), ()))


def dot(a, b):
    return jnp.dot(a, b, preferred_element_type=F32)


def dot_nt(a, b):
    return lax.dot_general(a, b, NT, preferred_element_type=F32)


def dot_tn(a, b):
    return lax.dot_general(a, b, TN, preferred_element_type=F32)


def partners():
    x, t = lax.axis_index("space"), lax.axis_index("tm")
    nx, nt = lax.axis_size("space"), lax.axis_size("tm")
    sides = [({"space": lax.rem(x + 1, nx)}, x + 1 < nx), ({"space": lax.rem(x + nx - 1, nx)}, x >= 1)]
    ups = [({"tm": lax.rem(t + k, nt)}, t + k < nt) for k in range(1, SPAN + 1)]
    downs = [({"tm": lax.rem(t + nt - k, nt)}, t >= k) for k in range(1, SPAN + 1)]
    return sides, ups, downs


class Message:
    def __init__(self, src, dst, send, recv, to, source):
        self.copy = pltpu.make_async_remote_copy(
            src_ref=src, dst_ref=dst, send_sem=send, recv_sem=recv, device_id=to[0], device_id_type=MESH
        )
        self.to, self.source = to[1], source[1]

    def start(self):
        pl.when(self.to)(self.copy.start)

    def sent(self):
        pl.when(self.to)(self.copy.wait_send)

    def arrived(self):
        pl.when(self.source)(self.copy.wait_recv)


def to_sides(src, dst, send, recv):
    sides, _, _ = partners()
    return [Message(src.at[i], dst.at[i], send.at[i], recv.at[i], sides[i], sides[1 - i]) for i in range(2)]


def to_clip(rising, falling, dst, send, recv):
    _, ups, downs = partners()
    out = []
    for k in reversed(range(SPAN)):
        j = SPAN + k
        out.append(Message(rising, dst.at[k], send.at[k], recv.at[k], ups[k], downs[k]))
        out.append(Message(falling, dst.at[j], send.at[j], recv.at[j], downs[k], ups[k]))
    return out


def build_conv(cw_ref, w3):
    for b in range(3):
        for rin in range(2):
            for rout in range(2):
                w3[
                    b * 256 + rin * 128 : b * 256 + rin * 128 + 128, rout * 128 : rout * 128 + 128
                ] = cw_ref[rin - rout + 1, b]


def joined(ref, f):
    return jnp.concatenate([ref[f, 0:64, :], ref[f, 64:128, :]], axis=1).astype(F32)


def shifted(x, left, right):
    row = lax.broadcasted_iota(jnp.int32, (64, 1), 0)
    before = jnp.where(row == 0, left, pltpu.roll(x, 1, 0))
    after = jnp.where(row == 63, right, pltpu.roll(x, 63, 0))
    return before.astype(BF), x.astype(BF), after.astype(BF)


def conv(xs, w3):
    taps = [jnp.concatenate(shifted(*x), axis=1) for x in xs]
    taps = jnp.concatenate(taps, axis=0) if len(taps) > 1 else taps[0]
    whole = jnp.concatenate([x[0] for x in xs], axis=0) if len(xs) > 1 else xs[0][0]
    return whole + dot(taps, w3[...])


def conv_back(xs, w3):
    parts = [shifted(*x) for x in xs]
    cat = lambda i: jnp.concatenate([p[i] for p in parts], axis=0) if len(parts) > 1 else parts[0][i]
    whole = jnp.concatenate([x[0] for x in xs], axis=0) if len(xs) > 1 else xs[0][0]
    out = dot_nt(cat(0), w3[512:768, :])
    out = out + dot_nt(cat(1), w3[256:512, :])
    out = out + dot_nt(cat(2), w3[0:256, :])
    return whole + out


def put(ref, f, y):
    ref[f, 0:64, :] = y[:, :128].astype(ref.dtype)
    ref[f, 64:128, :] = y[:, 128:].astype(ref.dtype)


def edges_out(ref, f, edges, at):
    x = joined(ref, f)
    edges[0, pl.ds(at, 1), :] = x[63:64]
    edges[1, pl.ds(at, 1), :] = x[0:1]


def mask_edges(halo):
    x, nx = lax.axis_index("space"), lax.axis_size("space")
    halo[0] = jnp.where(x > 0, halo[0], 0.0)
    halo[1] = jnp.where(x < nx - 1, halo[1], 0.0)


def halo_rows(halo, f):
    return halo[0, pl.ds(f, 1), :], halo[1, pl.ds(f, 1), :]


def with_halo(ref, halo, f):
    return (joined(ref, f), *halo_rows(halo, f))


def cells(y):
    parts = []
    for i in range(y.shape[0] // 64):
        parts += [y[i * 64 : i * 64 + 64, :128], y[i * 64 : i * 64 + 64, 128:]]
    return jnp.concatenate(parts, axis=0)


def block_ones(rows, cols, rblock, cblock, value):
    r = lax.broadcasted_iota(jnp.int32, (rows, cols), 0) // rblock
    c = lax.broadcasted_iota(jnp.int32, (rows, cols), 1) // cblock
    return jnp.where(r == c, value, 0.0).astype(BF)


def kernel(
    lens_h, offs_h, lat_h, ct_h, cw_h, wq_h, wk_h, wv_h, wo_h, qg_h, kg_h, out, lg,
    lens, offs, starts, targets, slots, lastf,
    lat, ct, cw, wq, wk, wv, wo, qg, kg,
    w3, wqk, wvo, wqkt, wvot,
    hid, qs, un, sc, kk, vv, ga, gq, att, dk, dv, gh, base,
    edge_f, halo_f, ctx_f, rim_f, got_f, gotrim_f,
    edge_b, halo_b, edge_g, halo_g, ctx_b, rim_b, got_b, gotrim_b,
    load_sem, side_send, side_recv, clip_send, clip_recv,
):
    frames = lat.shape[0]
    t, nt = lax.axis_index("tm"), lax.axis_size("tm")
    first = t * frames
    last = first + frames - 1

    pairs = [
        (lens_h, lens), (offs_h, offs), (lat_h, lat), (cw_h, cw), (ct_h, ct), (wq_h, wq), (wk_h, wk),
        (wv_h, wv), (wo_h, wo), (qg_h, qg), (kg_h, kg),
    ]
    loads = [pltpu.make_async_copy(a, b, load_sem.at[i]) for i, (a, b) in enumerate(pairs)]
    for c in loads:
        c.start()
    sides, ups, downs = partners()
    barrier = pltpu.get_barrier_semaphore()
    for who, there in sides + ups + downs:

        @pl.when(there)
        def _(who=who):
            pl.semaphore_signal(barrier, inc=1, device_id=who, device_id_type=MESH)

    loads[0].wait()
    loads[1].wait()

    def scan(j, c):
        start, top, low, below, below_end, above = c
        length = lens[j]
        end = start + length
        target = start + lax.rem(offs[j], length)
        starts[j] = start
        targets[j] = target
        inside = (target >= first) & (target <= last)
        top = jnp.where(inside, target, top)
        low = jnp.where(inside, jnp.minimum(low, target), low)
        at_first = start <= first
        below = jnp.where(at_first, target, below)
        below_end = jnp.where(at_first, end, below_end)
        above = jnp.where(start <= last, target, above)
        return end, top, low, below, below_end, above

    init = (jnp.int32(0), first, last, first, first, last)
    _, top, low, below, below_end, above = lax.fori_loop(0, lens.shape[0], scan, init, unroll=4)
    top, low = top - first, low - first
    up_at = jnp.clip((first - below + frames - 1) // frames, 1, SPAN) - 1
    down_at = jnp.clip((above - first) // frames, 1, SPAN) - 1 + SPAN

    loads[2].wait()
    ctx_f[0] = lat[top]
    ctx_f[1] = lat[low]
    for f in range(frames):
        edges_out(lat, f, edge_f, f)
    pl.semaphore_wait(barrier, sum(there.astype(jnp.int32) for _, there in sides + ups + downs))

    halos_f = to_sides(edge_f, halo_f, side_send.at[0], side_recv.at[0])
    frames_f = to_clip(ctx_f.at[0], ctx_f.at[1], got_f, clip_send.at[0], clip_recv.at[0])
    rims_f = to_clip(rim_f.at[0], rim_f.at[1], gotrim_f, clip_send.at[1], clip_recv.at[1])
    for m in halos_f + frames_f:
        m.start()

    def scan2(j, c):
        slot, lastof, near = c
        start, target = starts[j], targets[j]
        at = target - first
        mine = jnp.where(at < 0, frames, jnp.where(at >= frames, frames + 1, at))
        end = jnp.minimum(start + lens[j] - 1, last) - first
        slot = [jnp.where(start - first <= f, mine, s) for f, s in enumerate(slot)]
        lastof = [jnp.where(at == f, end, s) for f, s in enumerate(lastof)]
        near = [
            jnp.where(start <= (first + k * frames if k > 0 else last + k * frames), target, s)
            for k, s in zip(HOPS, near)
        ]
        return slot, lastof, near

    zero = jnp.int32(0)
    slot, lastof, near = lax.fori_loop(
        0, lens.shape[0], scan2, ([zero] * frames, [zero - 1] * frames, [zero - 1] * len(HOPS)), unroll=2
    )
    for f in range(frames):
        slots[f] = slot[f]
        lastf[f] = lastof[f]
    lastf[frames] = jnp.where(below < first, jnp.minimum(below_end - 1, last) - first, -1)
    lastf[frames + 1] = jnp.where(above > last, frames - 1, -1)
    hits = [
        (near[i] >= first) & (near[i] <= last) & ((t + k < nt) if k > 0 else (t + k >= 0))
        for i, k in enumerate(HOPS)
    ]

    for c in loads[3:]:
        c.wait()
    build_conv(cw, w3)
    none = jnp.zeros((128, 128), BF)
    wqk[:, :128] = wq[...]
    wqk[:, 128:] = wk[...]
    wvo[:128, :128] = wv[...]
    wvo[:128, 128:] = none
    wvo[128:, :128] = none
    wvo[128:, 128:] = wo[...].astype(F32).T.astype(BF)
    wqkt[:128, :] = wq[...].astype(F32).T.astype(BF)
    wqkt[128:, :] = wk[...].astype(F32).T.astype(BF)
    wvot[:128, :128] = wv[...].astype(F32).T.astype(BF)
    wvot[:128, 128:] = none
    wvot[128:, :128] = none
    wvot[128:, 128:] = wo[...]
    mean4 = block_ones(256, 256, HEAD, HEAD, 1.0 / HEAD)
    ones2 = block_ones(256, 256, 128, 128, 1.0)
    spread = block_ones(128, 256, HEAD, 128, 1.0)
    gains = jnp.concatenate([qg[...], kg[...]], axis=1)
    head0 = lax.broadcasted_iota(jnp.int32, (1, 128), 1) < HEAD
    dk[0] = jnp.zeros((128, 128), F32)
    dv[0] = jnp.zeros((128, 128), F32)

    for m in halos_f:
        m.arrived()
    mask_edges(halo_f)
    for i, f in enumerate((top, low)):
        left, right = halo_rows(halo_f, f)
        rim_f[i, 0:1] = left
        rim_f[i, 1:2] = right
    for m in rims_f:
        m.start()

    def project(h, c, at, real):
        qk = dot(h, wqk[...])
        vg = dot(jnp.concatenate([h, c], axis=1), wvo[...])
        s = lax.rsqrt(dot((qk * qk).astype(BF), mean4) + EPS)
        u = qk * s
        y = u * gains
        for i in range(h.shape[0] // 128):
            rows = slice(i * 128, i * 128 + 128)
            f = at + i
            un[f] = u[rows]
            sc[f] = s[rows]
            key, val = y[rows, 128:], vg[rows, :128]
            kk[f, :128] = jnp.where(head0, key, 0.0).astype(BF)
            kk[f, 128:] = jnp.where(head0, 0.0, key).astype(BF)
            vv[f, :128] = jnp.where(head0, val, 0.0).astype(BF)
            vv[f, 128:] = jnp.where(head0, 0.0, val).astype(BF)
            if real:
                qs[f] = y[rows, :128].astype(BF)
                ga[f] = vg[rows, 128:].astype(BF)

    @pl.loop(0, frames // 2)
    def _(g):
        h = cells(conv([with_halo(lat, halo_f, g * 2 + i) for i in range(2)], w3).astype(BF))
        at = pl.ds(g * 2, 2)
        hid[at] = h.reshape(2, 128, 128)
        project(h, ct[at].reshape(256, 128), g * 2, True)

    for m in frames_f + rims_f:
        m.arrived()
    below_there, above_there = t > 0, t < nt - 1
    far = []
    for at, there in ((up_at, below_there), (down_at, above_there)):
        x = jnp.where(there, joined(got_f, at), 0.0)
        rim = jnp.where(there, gotrim_f[at], 0.0)
        far.append((x, rim[0:1], rim[1:2]))
    both = cells(conv(far, w3).astype(BF))
    project(both, both, frames, False)

    @pl.loop(0, frames // GROUP)
    def _(g):
        at = [g * GROUP + i for i in range(GROUP)]
        slot = [slots[f] for f in at]
        same = [slots[jnp.maximum(f - 1, 0)] == s for f, s in zip(at, slot)]
        n = range(GROUP)
        raised = [jnp.exp(dot_nt(qs[at[i]], kk[slot[i]]) * 0.125) for i in n]
        total = [dot(r.astype(BF), ones2) for r in raised]
        prob = [raised[i] / total[i] for i in n]
        low_p = [p.astype(BF) for p in prob]
        o = [dot(low_p[i], vv[slot[i]]) for i in n]
        gp = [dot_nt(ga[at[i]], vv[slot[i]]) for i in n]
        for i in n:
            att[at[i]] = o[i].astype(BF)
        delta = [dot((o[i] * ga[at[i]].astype(F32)).astype(BF), spread) for i in n]
        ds = [(prob[i] * (gp[i] - delta[i]) * 0.125).astype(BF) for i in n]
        for i in n:
            gq[at[i]] = dot(ds[i], kk[slot[i]])
        kt = [dot_tn(qs[at[i]], ds[i]) for i in n]
        vt = [dot_tn(ga[at[i]], low_p[i]) for i in n]
        for acc, terms in ((dk, kt), (dv, vt)):
            run = acc[g * GROUP]
            for i in n:
                term = jnp.concatenate([terms[i][:64, :128], terms[i][64:, 128:]], axis=0)
                run = jnp.where(same[i], run, 0.0) + term
                acc[at[i] + 1] = run

    def finish(at, real):
        rows, vals = [], []
        for i in range(2):
            f = at + i
            left = gq[f] if real else jnp.zeros((128, 128), F32)
            until = jnp.clip(lastf[f] + 1, 0, frames)
            rows.append(jnp.concatenate([left, dk[until].T], axis=1))
            vals.append(dv[until].T)
        e = jnp.concatenate(rows, axis=0) * gains
        u = jnp.concatenate([un[at], un[at + 1]], axis=0)
        s = jnp.concatenate([sc[at], sc[at + 1]], axis=0)
        m = dot((e * u).astype(BF), mean4)
        raw = (s * (e - u * m)).astype(BF)
        val = jnp.concatenate(vals, axis=0).astype(BF)
        a = jnp.concatenate([att[at], att[at + 1]], axis=0) if real else val
        back = dot(raw, wqkt[...])
        vo = dot(jnp.concatenate([val, a], axis=1), wvot[...])
        return back + vo[:, :128], vo[:, 128:]

    def finish_local(g):
        back, o = finish(g * 2, True)
        at = pl.ds(g * 2, 2)
        out[at] = (hid[at].astype(F32) + o.reshape(2, 128, 128)).astype(BF)
        gh[at] = (ct[at].astype(F32) + back.reshape(2, 128, 128)).astype(BF)

    owed, _ = finish(frames, False)
    ctx_b[...] = owed.reshape(2, 128, 128).astype(BF)
    for i in range(2):
        edges_out(ctx_b, i, edge_g, i)
    frames_b = to_clip(ctx_b.at[1], ctx_b.at[0], got_b, clip_send.at[2], clip_recv.at[2])
    rims_b = to_clip(rim_b.at[1], rim_b.at[0], gotrim_b, clip_send.at[3], clip_recv.at[3])
    halos_g = to_sides(edge_g, halo_g, side_send.at[1], side_recv.at[1])
    halos_b = to_sides(edge_b, halo_b, side_send.at[2], side_recv.at[2])
    for m in halos_g + frames_b:
        m.start()
    pl.loop(0, frames // 2)(finish_local)
    for f in range(frames):
        edges_out(gh, f, edge_b, f)
    for m in halos_b:
        m.start()
    for m in halos_g:
        m.arrived()
    mask_edges(halo_g)
    for i in range(2):
        left, right = halo_rows(halo_g, i)
        rim_b[i, 0:1] = left
        rim_b[i, 1:2] = right
    for m in rims_b:
        m.start()
    for m in halos_b:
        m.arrived()
    mask_edges(halo_b)

    @pl.loop(0, frames // GROUP)
    def _(g):
        y = conv_back([with_halo(gh, halo_b, g * GROUP + i) for i in range(GROUP)], w3)
        for i in range(GROUP):
            put(base, g * GROUP + i, y[i * 64 : i * 64 + 64])

    for m in frames_b + rims_b:
        m.arrived()
    sums = []
    for at in (SPAN, 0):
        x, rim = jnp.zeros((64, 256), F32), jnp.zeros((2, 256), F32)
        for k in range(SPAN):
            x += jnp.where(hits[at + k], joined(got_b, at + k), 0.0)
            rim += jnp.where(hits[at + k], gotrim_b[at + k], 0.0)
        sums.append((x, rim[0:1], rim[1:2]))
    pair = cells(conv_back(sums, w3))
    for_top, for_low = pair[:128], pair[128:]

    @pl.loop(0, frames)
    def _(f):
        y = base[f] + jnp.where(f == top, for_top, 0.0) + jnp.where(f == low, for_low, 0.0)
        lg[f] = y.astype(BF)

    for m in halos_f + frames_f + rims_f + halos_g + frames_b + rims_b + halos_b:
        m.sent()


def per_device(
    latents, cotangent, clip_lengths, context_offset, conv_weight, w_query, w_key, w_value, w_out, query_gain, key_gain
):
    frames, rows, width, channels = latents.shape
    flat = (frames, rows * width, channels)
    one = (rows * width, channels)
    square = (channels, channels)
    slots = frames + 2
    clips = clip_lengths.shape[0]
    smem = lambda n: pltpu.SMEM((n,), jnp.int32)
    edge, few = VMEM((2, frames, 256), F32), VMEM((2, 8, 256), F32)
    comm = lambda: [VMEM((2, *one), BF), VMEM((2, 2, 256), F32), VMEM((2 * SPAN, *one), BF), VMEM((2 * SPAN, 2, 256), F32)]
    result = jax.ShapeDtypeStruct(flat, BF)
    out, lg = pl.pallas_call(
        kernel,
        name="tokenizer_block",
        out_shape=(result, result),
        in_specs=[pl.BlockSpec(memory_space=pltpu.HBM)] * 11,
        out_specs=(pl.BlockSpec(memory_space=VMEM),) * 2,
        scratch_shapes=[smem(clips)] * 4
        + [smem(frames), smem(slots)]
        + [VMEM(flat, BF), VMEM(flat, BF), VMEM(conv_weight.shape, BF)]
        + [VMEM(square, BF)] * 4
        + [VMEM((1, channels), F32)] * 2
        + [VMEM((768, 256), BF), VMEM((128, 256), BF), VMEM((256, 256), BF), VMEM((256, 128), BF), VMEM((256, 256), BF)]
        + [
            VMEM(flat, BF),
            VMEM(flat, BF),
            VMEM((slots, 128, 256), F32),
            VMEM((slots, 128, 256), F32),
            VMEM((slots, 256, 128), BF),
            VMEM((slots, 256, 128), BF),
            VMEM(flat, BF),
            VMEM(flat, F32),
            VMEM(flat, BF),
            VMEM((frames + 1, 128, 128), F32),
            VMEM((frames + 1, 128, 128), F32),
            VMEM(flat, BF),
            VMEM(flat, F32),
        ]
        + [edge, edge]
        + comm()
        + [edge, edge, few, few]
        + comm()
        + [
            pltpu.SemaphoreType.DMA((11,)),
            pltpu.SemaphoreType.DMA((3, 2)),
            pltpu.SemaphoreType.DMA((3, 2)),
            pltpu.SemaphoreType.DMA((4, 2 * SPAN)),
            pltpu.SemaphoreType.DMA((4, 2 * SPAN)),
        ],
        compiler_params=pltpu.CompilerParams(
            collective_id=0, has_side_effects=True, vmem_limit_bytes=40 << 20
        ),
    )(
        clip_lengths, context_offset, latents.reshape(flat), cotangent.reshape(flat), conv_weight,
        w_query, w_key, w_value, w_out, query_gain.reshape(1, channels), key_gain.reshape(1, channels),
    )
    return out.reshape(latents.shape), lg.reshape(latents.shape)


def solution(mesh):
    data = P("tm", None, "space", None)
    return jax.shard_map(
        per_device,
        mesh=mesh,
        in_specs=(data, data) + (P(),) * 9,
        out_specs=(data, data),
        check_vma=False,
    )
```

```python
import jax
import jax.numpy as jnp
from jax import lax
from jax.experimental import pallas as pl
from jax.experimental.pallas import tpu as pltpu
from jax.sharding import PartitionSpec as P

HEAD = 64
SPAN = 4
GROUP = 4
HOPS = (-1, -2, -3, -4, 1, 2, 3, 4)
EPS = 1e-6
MESH = pl.DeviceIdType.MESH
VMEM = pltpu.VMEM
BF = jnp.bfloat16
F32 = jnp.float32
NT = (((1,), (1,)), ((), ()))
TN = (((0,), (0,)), ((), ()))


def dot(a, b):
    return jnp.dot(a, b, preferred_element_type=F32)


def dot_nt(a, b):
    return lax.dot_general(a, b, NT, preferred_element_type=F32)


def dot_tn(a, b):
    return lax.dot_general(a, b, TN, preferred_element_type=F32)


def partners():
    x, t = lax.axis_index("space"), lax.axis_index("tm")
    nx, nt = lax.axis_size("space"), lax.axis_size("tm")
    sides = [({"space": lax.rem(x + 1, nx)}, x + 1 < nx), ({"space": lax.rem(x + nx - 1, nx)}, x >= 1)]
    ups = [({"tm": lax.rem(t + k, nt)}, t + k < nt) for k in range(1, SPAN + 1)]
    downs = [({"tm": lax.rem(t + nt - k, nt)}, t >= k) for k in range(1, SPAN + 1)]
    return sides, ups, downs


class Message:
    def __init__(self, src, dst, send, recv, to, source):
        self.copy = pltpu.make_async_remote_copy(
            src_ref=src, dst_ref=dst, send_sem=send, recv_sem=recv, device_id=to[0], device_id_type=MESH
        )
        self.to, self.source = to[1], source[1]

    def start(self):
        pl.when(self.to)(self.copy.start)

    def sent(self):
        pl.when(self.to)(self.copy.wait_send)

    def arrived(self):
        pl.when(self.source)(self.copy.wait_recv)


def to_sides(src, dst, send, recv):
    sides, _, _ = partners()
    return [Message(src.at[i], dst.at[i], send.at[i], recv.at[i], sides[i], sides[1 - i]) for i in range(2)]


def to_clip(rising, falling, dst, send, recv):
    _, ups, downs = partners()
    out = []
    for k in reversed(range(SPAN)):
        j = SPAN + k
        out.append(Message(rising, dst.at[k], send.at[k], recv.at[k], ups[k], downs[k]))
        out.append(Message(falling, dst.at[j], send.at[j], recv.at[j], downs[k], ups[k]))
    return out


def build_conv(cw_ref, w3):
    for b in range(3):
        for rin in range(2):
            for rout in range(2):
                w3[
                    b * 256 + rin * 128 : b * 256 + rin * 128 + 128, rout * 128 : rout * 128 + 128
                ] = cw_ref[rin - rout + 1, b]


def joined(ref, f):
    return jnp.concatenate([ref[f, 0:64, :], ref[f, 64:128, :]], axis=1).astype(F32)


def shifted(x, left, right):
    row = lax.broadcasted_iota(jnp.int32, (64, 1), 0)
    before = jnp.where(row == 0, left, pltpu.roll(x, 1, 0))
    after = jnp.where(row == 63, right, pltpu.roll(x, 63, 0))
    return before.astype(BF), x.astype(BF), after.astype(BF)


def conv(xs, w3):
    taps = [jnp.concatenate(shifted(*x), axis=1) for x in xs]
    taps = jnp.concatenate(taps, axis=0) if len(taps) > 1 else taps[0]
    whole = jnp.concatenate([x[0] for x in xs], axis=0) if len(xs) > 1 else xs[0][0]
    return whole + dot(taps, w3[...])


def conv_back(xs, w3):
    parts = [shifted(*x) for x in xs]
    cat = lambda i: jnp.concatenate([p[i] for p in parts], axis=0) if len(parts) > 1 else parts[0][i]
    whole = jnp.concatenate([x[0] for x in xs], axis=0) if len(xs) > 1 else xs[0][0]
    out = dot_nt(cat(0), w3[512:768, :])
    out = out + dot_nt(cat(1), w3[256:512, :])
    out = out + dot_nt(cat(2), w3[0:256, :])
    return whole + out


def put(ref, f, y):
    ref[f, 0:64, :] = y[:, :128].astype(ref.dtype)
    ref[f, 64:128, :] = y[:, 128:].astype(ref.dtype)


def edges_out(ref, f, edges, at):
    x = joined(ref, f)
    edges[0, pl.ds(at, 1), :] = x[63:64]
    edges[1, pl.ds(at, 1), :] = x[0:1]


def mask_edges(halo):
    x, nx = lax.axis_index("space"), lax.axis_size("space")
    halo[0] = jnp.where(x > 0, halo[0], 0.0)
    halo[1] = jnp.where(x < nx - 1, halo[1], 0.0)


def halo_rows(halo, f):
    return halo[0, pl.ds(f, 1), :], halo[1, pl.ds(f, 1), :]


def with_halo(ref, halo, f):
    return (joined(ref, f), *halo_rows(halo, f))


def cells(y):
    parts = []
    for i in range(y.shape[0] // 64):
        parts += [y[i * 64 : i * 64 + 64, :128], y[i * 64 : i * 64 + 64, 128:]]
    return jnp.concatenate(parts, axis=0)


def block_ones(rows, cols, rblock, cblock, value):
    r = lax.broadcasted_iota(jnp.int32, (rows, cols), 0) // rblock
    c = lax.broadcasted_iota(jnp.int32, (rows, cols), 1) // cblock
    return jnp.where(r == c, value, 0.0).astype(BF)


def kernel(
    lens_h, offs_h, lat_h, ct_h, cw_h, wq_h, wk_h, wv_h, wo_h, qg_h, kg_h, out_h, lg_h,
    lens, offs, starts, targets, slots, lastf,
    lat, ct, cw, wq, wk, wv, wo, qg, kg,
    w3, wqk, wvo, wqkt, wvot,
    hid, qs, un, sc, kk, vv, ga, gq, att, dk, dv, gh, base,
    edge_f, halo_f, ctx_f, rim_f, got_f, gotrim_f,
    edge_b, halo_b, edge_g, halo_g, ctx_b, rim_b, got_b, gotrim_b,
    out, lg, load_sem, store_sem, side_send, side_recv, clip_send, clip_recv,
):
    frames = lat.shape[0]
    t, nt = lax.axis_index("tm"), lax.axis_size("tm")
    first = t * frames
    last = first + frames - 1

    pairs = [
        (lens_h, lens), (offs_h, offs), (lat_h, lat), (cw_h, cw), (ct_h, ct), (wq_h, wq), (wk_h, wk),
        (wv_h, wv), (wo_h, wo), (qg_h, qg), (kg_h, kg),
    ]
    loads = [pltpu.make_async_copy(a, b, load_sem.at[i]) for i, (a, b) in enumerate(pairs)]
    for c in loads:
        c.start()
    sides, ups, downs = partners()
    barrier = pltpu.get_barrier_semaphore()
    for who, there in sides + ups + downs:

        @pl.when(there)
        def _(who=who):
            pl.semaphore_signal(barrier, inc=1, device_id=who, device_id_type=MESH)

    loads[0].wait()
    loads[1].wait()

    def scan(j, c):
        start, top, low, below, below_end, above = c
        length = lens[j]
        end = start + length
        target = start + lax.rem(offs[j], length)
        starts[j] = start
        targets[j] = target
        inside = (target >= first) & (target <= last)
        top = jnp.where(inside, target, top)
        low = jnp.where(inside, jnp.minimum(low, target), low)
        at_first = start <= first
        below = jnp.where(at_first, target, below)
        below_end = jnp.where(at_first, end, below_end)
        above = jnp.where(start <= last, target, above)
        return end, top, low, below, below_end, above

    init = (jnp.int32(0), first, last, first, first, last)
    _, top, low, below, below_end, above = lax.fori_loop(0, lens.shape[0], scan, init, unroll=4)
    top, low = top - first, low - first
    up_at = jnp.clip((first - below + frames - 1) // frames, 1, SPAN) - 1
    down_at = jnp.clip((above - first) // frames, 1, SPAN) - 1 + SPAN

    loads[2].wait()
    ctx_f[0] = lat[top]
    ctx_f[1] = lat[low]
    for f in range(frames):
        edges_out(lat, f, edge_f, f)
    pl.semaphore_wait(barrier, sum(there.astype(jnp.int32) for _, there in sides + ups + downs))

    halos_f = to_sides(edge_f, halo_f, side_send.at[0], side_recv.at[0])
    frames_f = to_clip(ctx_f.at[0], ctx_f.at[1], got_f, clip_send.at[0], clip_recv.at[0])
    rims_f = to_clip(rim_f.at[0], rim_f.at[1], gotrim_f, clip_send.at[1], clip_recv.at[1])
    for m in halos_f + frames_f:
        m.start()

    def scan2(j, c):
        slot, lastof, near = c
        start, target = starts[j], targets[j]
        at = target - first
        mine = jnp.where(at < 0, frames, jnp.where(at >= frames, frames + 1, at))
        end = jnp.minimum(start + lens[j] - 1, last) - first
        slot = [jnp.where(start - first <= f, mine, s) for f, s in enumerate(slot)]
        lastof = [jnp.where(at == f, end, s) for f, s in enumerate(lastof)]
        near = [
            jnp.where(start <= (first + k * frames if k > 0 else last + k * frames), target, s)
            for k, s in zip(HOPS, near)
        ]
        return slot, lastof, near

    zero = jnp.int32(0)
    slot, lastof, near = lax.fori_loop(
        0, lens.shape[0], scan2, ([zero] * frames, [zero - 1] * frames, [zero - 1] * len(HOPS)), unroll=2
    )
    for f in range(frames):
        slots[f] = slot[f]
        lastf[f] = lastof[f]
    lastf[frames] = jnp.where(below < first, jnp.minimum(below_end - 1, last) - first, -1)
    lastf[frames + 1] = jnp.where(above > last, frames - 1, -1)
    hits = [
        (near[i] >= first) & (near[i] <= last) & ((t + k < nt) if k > 0 else (t + k >= 0))
        for i, k in enumerate(HOPS)
    ]

    for c in loads[3:]:
        c.wait()
    build_conv(cw, w3)
    none = jnp.zeros((128, 128), BF)
    wqk[:, :128] = wq[...]
    wqk[:, 128:] = wk[...]
    wvo[:128, :128] = wv[...]
    wvo[:128, 128:] = none
    wvo[128:, :128] = none
    wvo[128:, 128:] = wo[...].astype(F32).T.astype(BF)
    wqkt[:128, :] = wq[...].astype(F32).T.astype(BF)
    wqkt[128:, :] = wk[...].astype(F32).T.astype(BF)
    wvot[:128, :128] = wv[...].astype(F32).T.astype(BF)
    wvot[:128, 128:] = none
    wvot[128:, :128] = none
    wvot[128:, 128:] = wo[...]
    mean4 = block_ones(256, 256, HEAD, HEAD, 1.0 / HEAD)
    ones2 = block_ones(256, 256, 128, 128, 1.0)
    spread = block_ones(128, 256, HEAD, 128, 1.0)
    gains = jnp.concatenate([qg[...], kg[...]], axis=1)
    head0 = lax.broadcasted_iota(jnp.int32, (1, 128), 1) < HEAD
    dk[0] = jnp.zeros((128, 128), F32)
    dv[0] = jnp.zeros((128, 128), F32)

    for m in halos_f:
        m.arrived()
    mask_edges(halo_f)
    for i, f in enumerate((top, low)):
        left, right = halo_rows(halo_f, f)
        rim_f[i, 0:1] = left
        rim_f[i, 1:2] = right
    for m in rims_f:
        m.start()

    def project(h, c, at, real):
        qk = dot(h, wqk[...])
        vg = dot(jnp.concatenate([h, c], axis=1), wvo[...])
        s = lax.rsqrt(dot((qk * qk).astype(BF), mean4) + EPS)
        u = qk * s
        y = u * gains
        for i in range(h.shape[0] // 128):
            rows = slice(i * 128, i * 128 + 128)
            f = at + i
            un[f] = u[rows]
            sc[f] = s[rows]
            key, val = y[rows, 128:], vg[rows, :128]
            kk[f, :128] = jnp.where(head0, key, 0.0).astype(BF)
            kk[f, 128:] = jnp.where(head0, 0.0, key).astype(BF)
            vv[f, :128] = jnp.where(head0, val, 0.0).astype(BF)
            vv[f, 128:] = jnp.where(head0, 0.0, val).astype(BF)
            if real:
                qs[f] = y[rows, :128].astype(BF)
                ga[f] = vg[rows, 128:].astype(BF)

    @pl.loop(0, frames // 2)
    def _(g):
        h = cells(conv([with_halo(lat, halo_f, g * 2 + i) for i in range(2)], w3).astype(BF))
        at = pl.ds(g * 2, 2)
        hid[at] = h.reshape(2, 128, 128)
        project(h, ct[at].reshape(256, 128), g * 2, True)

    for m in frames_f + rims_f:
        m.arrived()
    below_there, above_there = t > 0, t < nt - 1
    far = []
    for at, there in ((up_at, below_there), (down_at, above_there)):
        x = jnp.where(there, joined(got_f, at), 0.0)
        rim = jnp.where(there, gotrim_f[at], 0.0)
        far.append((x, rim[0:1], rim[1:2]))
    both = cells(conv(far, w3).astype(BF))
    project(both, both, frames, False)

    @pl.loop(0, frames // GROUP)
    def _(g):
        at = [g * GROUP + i for i in range(GROUP)]
        slot = [slots[f] for f in at]
        same = [slots[jnp.maximum(f - 1, 0)] == s for f, s in zip(at, slot)]
        n = range(GROUP)
        raised = [jnp.exp(dot_nt(qs[at[i]], kk[slot[i]]) * 0.125) for i in n]
        total = [dot(r.astype(BF), ones2) for r in raised]
        prob = [raised[i] / total[i] for i in n]
        low_p = [p.astype(BF) for p in prob]
        o = [dot(low_p[i], vv[slot[i]]) for i in n]
        gp = [dot_nt(ga[at[i]], vv[slot[i]]) for i in n]
        for i in n:
            att[at[i]] = o[i].astype(BF)
        delta = [dot((o[i] * ga[at[i]].astype(F32)).astype(BF), spread) for i in n]
        ds = [(prob[i] * (gp[i] - delta[i]) * 0.125).astype(BF) for i in n]
        for i in n:
            gq[at[i]] = dot(ds[i], kk[slot[i]])
        kt = [dot_tn(qs[at[i]], ds[i]) for i in n]
        vt = [dot_tn(ga[at[i]], low_p[i]) for i in n]
        for acc, terms in ((dk, kt), (dv, vt)):
            run = acc[g * GROUP]
            for i in n:
                term = jnp.concatenate([terms[i][:64, :128], terms[i][64:, 128:]], axis=0)
                run = jnp.where(same[i], run, 0.0) + term
                acc[at[i] + 1] = run

    def finish(at, real):
        rows, vals = [], []
        for i in range(2):
            f = at + i
            left = gq[f] if real else jnp.zeros((128, 128), F32)
            until = jnp.clip(lastf[f] + 1, 0, frames)
            rows.append(jnp.concatenate([left, dk[until].T], axis=1))
            vals.append(dv[until].T)
        e = jnp.concatenate(rows, axis=0) * gains
        u = jnp.concatenate([un[at], un[at + 1]], axis=0)
        s = jnp.concatenate([sc[at], sc[at + 1]], axis=0)
        m = dot((e * u).astype(BF), mean4)
        raw = (s * (e - u * m)).astype(BF)
        val = jnp.concatenate(vals, axis=0).astype(BF)
        a = jnp.concatenate([att[at], att[at + 1]], axis=0) if real else val
        back = dot(raw, wqkt[...])
        vo = dot(jnp.concatenate([val, a], axis=1), wvot[...])
        return back + vo[:, :128], vo[:, 128:]

    def finish_local(g):
        back, o = finish(g * 2, True)
        at = pl.ds(g * 2, 2)
        out[at] = (hid[at].astype(F32) + o.reshape(2, 128, 128)).astype(BF)
        gh[at] = (ct[at].astype(F32) + back.reshape(2, 128, 128)).astype(BF)

    owed, _ = finish(frames, False)
    ctx_b[...] = owed.reshape(2, 128, 128).astype(BF)
    for i in range(2):
        edges_out(ctx_b, i, edge_g, i)
    frames_b = to_clip(ctx_b.at[1], ctx_b.at[0], got_b, clip_send.at[2], clip_recv.at[2])
    rims_b = to_clip(rim_b.at[1], rim_b.at[0], gotrim_b, clip_send.at[3], clip_recv.at[3])
    halos_g = to_sides(edge_g, halo_g, side_send.at[1], side_recv.at[1])
    halos_b = to_sides(edge_b, halo_b, side_send.at[2], side_recv.at[2])
    for m in halos_g + frames_b:
        m.start()
    pl.loop(0, frames // 2)(finish_local)
    stores = [pltpu.make_async_copy(out, out_h, store_sem.at[0])]
    stores[0].start()
    for f in range(frames):
        edges_out(gh, f, edge_b, f)
    for m in halos_b:
        m.start()
    for m in halos_g:
        m.arrived()
    mask_edges(halo_g)
    for i in range(2):
        left, right = halo_rows(halo_g, i)
        rim_b[i, 0:1] = left
        rim_b[i, 1:2] = right
    for m in rims_b:
        m.start()
    for m in halos_b:
        m.arrived()
    mask_edges(halo_b)

    @pl.loop(0, frames // GROUP)
    def _(g):
        y = conv_back([with_halo(gh, halo_b, g * GROUP + i) for i in range(GROUP)], w3)
        for i in range(GROUP):
            put(base, g * GROUP + i, y[i * 64 : i * 64 + 64])

    for m in frames_b + rims_b:
        m.arrived()
    sums = []
    for at in (SPAN, 0):
        x, rim = jnp.zeros((64, 256), F32), jnp.zeros((2, 256), F32)
        for k in range(SPAN):
            x += jnp.where(hits[at + k], joined(got_b, at + k), 0.0)
            rim += jnp.where(hits[at + k], gotrim_b[at + k], 0.0)
        sums.append((x, rim[0:1], rim[1:2]))
    pair = cells(conv_back(sums, w3))
    for_top, for_low = pair[:128], pair[128:]

    for g in range(frames // GROUP):
        for f in range(g * GROUP, g * GROUP + GROUP):
            y = base[f] + jnp.where(f == top, for_top, 0.0) + jnp.where(f == low, for_low, 0.0)
            lg[f] = y.astype(BF)
        at = pl.ds(g * GROUP, GROUP)
        stores.append(pltpu.make_async_copy(lg.at[at], lg_h.at[at], store_sem.at[g + 1]))
        stores[-1].start()
    for c in stores:
        c.wait()
    for m in halos_f + frames_f + rims_f + halos_g + frames_b + rims_b + halos_b:
        m.sent()


def per_device(
    latents, cotangent, clip_lengths, context_offset, conv_weight, w_query, w_key, w_value, w_out, query_gain, key_gain
):
    frames, rows, width, channels = latents.shape
    flat = (frames, rows * width, channels)
    one = (rows * width, channels)
    square = (channels, channels)
    slots = frames + 2
    clips = clip_lengths.shape[0]
    smem = lambda n: pltpu.SMEM((n,), jnp.int32)
    edge, few = VMEM((2, frames, 256), F32), VMEM((2, 8, 256), F32)
    comm = lambda: [VMEM((2, *one), BF), VMEM((2, 2, 256), F32), VMEM((2 * SPAN, *one), BF), VMEM((2 * SPAN, 2, 256), F32)]
    result = jax.ShapeDtypeStruct(flat, BF)
    out, lg = pl.pallas_call(
        kernel,
        name="tokenizer_block",
        out_shape=(result, result),
        in_specs=[pl.BlockSpec(memory_space=pltpu.HBM)] * 11,
        out_specs=(pl.BlockSpec(memory_space=pltpu.HBM),) * 2,
        scratch_shapes=[smem(clips)] * 4
        + [smem(frames), smem(slots)]
        + [VMEM(flat, BF), VMEM(flat, BF), VMEM(conv_weight.shape, BF)]
        + [VMEM(square, BF)] * 4
        + [VMEM((1, channels), F32)] * 2
        + [VMEM((768, 256), BF), VMEM((128, 256), BF), VMEM((256, 256), BF), VMEM((256, 128), BF), VMEM((256, 256), BF)]
        + [
            VMEM(flat, BF),
            VMEM(flat, BF),
            VMEM((slots, 128, 256), F32),
            VMEM((slots, 128, 256), F32),
            VMEM((slots, 256, 128), BF),
            VMEM((slots, 256, 128), BF),
            VMEM(flat, BF),
            VMEM(flat, F32),
            VMEM(flat, BF),
            VMEM((frames + 1, 128, 128), F32),
            VMEM((frames + 1, 128, 128), F32),
            VMEM(flat, BF),
            VMEM(flat, F32),
        ]
        + [edge, edge]
        + comm()
        + [edge, edge, few, few]
        + comm()
        + [
            VMEM(flat, BF),
            VMEM(flat, BF),
            pltpu.SemaphoreType.DMA((11,)),
            pltpu.SemaphoreType.DMA((1 + frames // GROUP,)),
            pltpu.SemaphoreType.DMA((3, 2)),
            pltpu.SemaphoreType.DMA((3, 2)),
            pltpu.SemaphoreType.DMA((4, 2 * SPAN)),
            pltpu.SemaphoreType.DMA((4, 2 * SPAN)),
        ],
        compiler_params=pltpu.CompilerParams(
            collective_id=0, has_side_effects=True, vmem_limit_bytes=60 << 20
        ),
    )(
        clip_lengths, context_offset, latents.reshape(flat), cotangent.reshape(flat), conv_weight,
        w_query, w_key, w_value, w_out, query_gain.reshape(1, channels), key_gain.reshape(1, channels),
    )
    return out.reshape(latents.shape), lg.reshape(latents.shape)


def solution(mesh):
    data = P("tm", None, "space", None)
    return jax.shard_map(
        per_device,
        mesh=mesh,
        in_specs=(data, data) + (P(),) * 9,
        out_specs=(data, data),
        check_vma=False,
    )
```

```python
import jax
import jax.numpy as jnp
from jax import lax
from jax.experimental import pallas as pl
from jax.experimental.pallas import tpu as pltpu
from jax.sharding import PartitionSpec as P

HEAD = 64
SPAN = 4
GROUP = 4
HOPS = (-1, -2, -3, -4, 1, 2, 3, 4)
EPS = 1e-6
MESH = pl.DeviceIdType.MESH
VMEM = pltpu.VMEM
BF = jnp.bfloat16
F32 = jnp.float32
NT = (((1,), (1,)), ((), ()))
TN = (((0,), (0,)), ((), ()))


def dot(a, b):
    return jnp.dot(a, b, preferred_element_type=F32)


def dot_nt(a, b):
    return lax.dot_general(a, b, NT, preferred_element_type=F32)


def dot_tn(a, b):
    return lax.dot_general(a, b, TN, preferred_element_type=F32)


def partners():
    x, t = lax.axis_index("space"), lax.axis_index("tm")
    nx, nt = lax.axis_size("space"), lax.axis_size("tm")
    sides = [({"space": lax.rem(x + 1, nx)}, x + 1 < nx), ({"space": lax.rem(x + nx - 1, nx)}, x >= 1)]
    ups = [({"tm": lax.rem(t + k, nt)}, t + k < nt) for k in range(1, SPAN + 1)]
    downs = [({"tm": lax.rem(t + nt - k, nt)}, t >= k) for k in range(1, SPAN + 1)]
    return sides, ups, downs


class Message:
    def __init__(self, src, dst, send, recv, to, source):
        self.copy = pltpu.make_async_remote_copy(
            src_ref=src, dst_ref=dst, send_sem=send, recv_sem=recv, device_id=to[0], device_id_type=MESH
        )
        self.to, self.source = to[1], source[1]

    def start(self):
        pl.when(self.to)(self.copy.start)

    def sent(self):
        pl.when(self.to)(self.copy.wait_send)

    def arrived(self):
        pl.when(self.source)(self.copy.wait_recv)


def to_sides(src, dst, send, recv):
    sides, _, _ = partners()
    return [Message(src.at[i], dst.at[i], send.at[i], recv.at[i], sides[i], sides[1 - i]) for i in range(2)]


def to_clip(rising, falling, dst, send, recv):
    _, ups, downs = partners()
    out = []
    for k in reversed(range(SPAN)):
        j = SPAN + k
        out.append(Message(rising, dst.at[k], send.at[k], recv.at[k], ups[k], downs[k]))
        out.append(Message(falling, dst.at[j], send.at[j], recv.at[j], downs[k], ups[k]))
    return out


def build_conv(cw_ref, w3):
    for b in range(3):
        for rin in range(2):
            for rout in range(2):
                w3[
                    b * 256 + rin * 128 : b * 256 + rin * 128 + 128, rout * 128 : rout * 128 + 128
                ] = cw_ref[rin - rout + 1, b]


def joined(ref, f):
    return jnp.concatenate([ref[f, 0:64, :], ref[f, 64:128, :]], axis=1).astype(F32)


def shifted(x, left, right):
    row = lax.broadcasted_iota(jnp.int32, (64, 1), 0)
    before = jnp.where(row == 0, left, pltpu.roll(x, 1, 0))
    after = jnp.where(row == 63, right, pltpu.roll(x, 63, 0))
    return before.astype(BF), x.astype(BF), after.astype(BF)


def conv(xs, w3):
    taps = [jnp.concatenate(shifted(*x), axis=1) for x in xs]
    taps = jnp.concatenate(taps, axis=0) if len(taps) > 1 else taps[0]
    whole = jnp.concatenate([x[0] for x in xs], axis=0) if len(xs) > 1 else xs[0][0]
    return whole + dot(taps, w3[...])


def conv_back(xs, w3):
    parts = [shifted(*x) for x in xs]
    cat = lambda i: jnp.concatenate([p[i] for p in parts], axis=0) if len(parts) > 1 else parts[0][i]
    whole = jnp.concatenate([x[0] for x in xs], axis=0) if len(xs) > 1 else xs[0][0]
    out = dot_nt(cat(0), w3[512:768, :])
    out = out + dot_nt(cat(1), w3[256:512, :])
    out = out + dot_nt(cat(2), w3[0:256, :])
    return whole + out


def put(ref, f, y):
    ref[f, 0:64, :] = y[:, :128].astype(ref.dtype)
    ref[f, 64:128, :] = y[:, 128:].astype(ref.dtype)


def edges_out(ref, f, edges, at):
    x = joined(ref, f)
    edges[0, pl.ds(at, 1), :] = x[63:64]
    edges[1, pl.ds(at, 1), :] = x[0:1]


def mask_edges(halo):
    x, nx = lax.axis_index("space"), lax.axis_size("space")
    halo[0] = jnp.where(x > 0, halo[0], 0.0)
    halo[1] = jnp.where(x < nx - 1, halo[1], 0.0)


def halo_rows(halo, f):
    return halo[0, pl.ds(f, 1), :], halo[1, pl.ds(f, 1), :]


def with_halo(ref, halo, f):
    return (joined(ref, f), *halo_rows(halo, f))


def cells(y):
    parts = []
    for i in range(y.shape[0] // 64):
        parts += [y[i * 64 : i * 64 + 64, :128], y[i * 64 : i * 64 + 64, 128:]]
    return jnp.concatenate(parts, axis=0)


def block_ones(rows, cols, rblock, cblock, value):
    r = lax.broadcasted_iota(jnp.int32, (rows, cols), 0) // rblock
    c = lax.broadcasted_iota(jnp.int32, (rows, cols), 1) // cblock
    return jnp.where(r == c, value, 0.0).astype(BF)


def kernel(
    lens_h, offs_h, lat_h, ct_h, cw_h, wq_h, wk_h, wv_h, wo_h, qg_h, kg_h, out_h, lg_h, pair_h, spot_h,
    lens, offs, starts, targets, slots, lastf,
    lat, ct, cw, wq, wk, wv, wo, qg, kg,
    w3, wqk, wvo, wqkt, wvt,
    hid, qs, un, sc, kk, vv, ga, gq, att, dk, dv, gh,
    edge_f, halo_f, ctx_f, rim_f, got_f, gotrim_f,
    edge_b, halo_b, edge_g, halo_g, ctx_b, rim_b, got_b, gotrim_b,
    conv_f, rims, out, lg, pair, spot, load_sem, store_sem, side_send, side_recv, clip_send, clip_recv,
):
    frames = lat.shape[0]
    t, nt = lax.axis_index("tm"), lax.axis_size("tm")
    first = t * frames
    last = first + frames - 1

    pairs = [
        (lens_h, lens), (offs_h, offs), (lat_h, lat), (cw_h, cw), (ct_h, ct), (wq_h, wq), (wk_h, wk),
        (wv_h, wv), (wo_h, wo), (qg_h, qg), (kg_h, kg),
    ]
    loads = [pltpu.make_async_copy(a, b, load_sem.at[i]) for i, (a, b) in enumerate(pairs)]
    for c in loads:
        c.start()
    sides, ups, downs = partners()
    barrier = pltpu.get_barrier_semaphore()
    for who, there in sides + ups + downs:

        @pl.when(there)
        def _(who=who):
            pl.semaphore_signal(barrier, inc=1, device_id=who, device_id_type=MESH)

    loads[0].wait()
    loads[1].wait()

    def scan(j, c):
        start, top, low, below, below_end, above = c
        length = lens[j]
        end = start + length
        target = start + lax.rem(offs[j], length)
        starts[j] = start
        targets[j] = target
        inside = (target >= first) & (target <= last)
        top = jnp.where(inside, target, top)
        low = jnp.where(inside, jnp.minimum(low, target), low)
        at_first = start <= first
        below = jnp.where(at_first, target, below)
        below_end = jnp.where(at_first, end, below_end)
        above = jnp.where(start <= last, target, above)
        return end, top, low, below, below_end, above

    init = (jnp.int32(0), first, last, first, first, last)
    _, top, low, below, below_end, above = lax.fori_loop(0, lens.shape[0], scan, init, unroll=4)
    top, low = top - first, low - first
    spot[0] = top
    spot[1] = low
    spots = pltpu.make_async_copy(spot, spot_h, store_sem.at[3])
    spots.start()
    up_at = jnp.clip((first - below + frames - 1) // frames, 1, SPAN) - 1
    down_at = jnp.clip((above - first) // frames, 1, SPAN) - 1 + SPAN

    loads[2].wait()
    ctx_f[0] = lat[top]
    ctx_f[1] = lat[low]
    for f in range(frames):
        edges_out(lat, f, edge_f, f)
    pl.semaphore_wait(barrier, sum(there.astype(jnp.int32) for _, there in sides + ups + downs))

    halos_f = to_sides(edge_f, halo_f, side_send.at[0], side_recv.at[0])
    frames_f = to_clip(ctx_f.at[0], ctx_f.at[1], got_f, clip_send.at[0], clip_recv.at[0])
    rims_f = to_clip(rim_f.at[0], rim_f.at[1], gotrim_f, clip_send.at[1], clip_recv.at[1])
    for m in halos_f + frames_f:
        m.start()

    def scan2(j, c):
        slot, lastof, near = c
        start, target = starts[j], targets[j]
        at = target - first
        mine = jnp.where(at < 0, frames, jnp.where(at >= frames, frames + 1, at))
        end = jnp.minimum(start + lens[j] - 1, last) - first
        slot = [jnp.where(start - first <= f, mine, s) for f, s in enumerate(slot)]
        lastof = [jnp.where(at == f, end, s) for f, s in enumerate(lastof)]
        near = [
            jnp.where(start <= (first + k * frames if k > 0 else last + k * frames), target, s)
            for k, s in zip(HOPS, near)
        ]
        return slot, lastof, near

    zero = jnp.int32(0)
    slot, lastof, near = lax.fori_loop(
        0, lens.shape[0], scan2, ([zero] * frames, [zero - 1] * frames, [zero - 1] * len(HOPS)), unroll=2
    )
    for f in range(frames):
        slots[f] = slot[f]
        lastf[f] = lastof[f]
    lastf[frames] = jnp.where(below < first, jnp.minimum(below_end - 1, last) - first, -1)
    lastf[frames + 1] = jnp.where(above > last, frames - 1, -1)
    hits = [
        (near[i] >= first) & (near[i] <= last) & ((t + k < nt) if k > 0 else (t + k >= 0))
        for i, k in enumerate(HOPS)
    ]

    for c in loads[3:]:
        c.wait()
    build_conv(cw, w3)
    none = jnp.zeros((128, 128), BF)
    wqk[:, :128] = wq[...]
    wqk[:, 128:] = wk[...]
    wvo[:128, :128] = wv[...]
    wvo[:128, 128:] = none
    wvo[128:, :128] = none
    wvo[128:, 128:] = wo[...].astype(F32).T.astype(BF)
    wqkt[:128, :] = wq[...].astype(F32).T.astype(BF)
    wqkt[128:, :] = wk[...].astype(F32).T.astype(BF)
    wvt[...] = wv[...].astype(F32).T.astype(BF)
    mean4 = block_ones(256, 256, HEAD, HEAD, 1.0 / HEAD)
    ones2 = block_ones(256, 256, 128, 128, 1.0)
    spread = block_ones(128, 256, HEAD, 128, 1.0)
    gains = jnp.concatenate([qg[...], kg[...]], axis=1)
    head0 = lax.broadcasted_iota(jnp.int32, (1, 128), 1) < HEAD
    dk[0] = jnp.zeros((128, 128), F32)
    dv[0] = jnp.zeros((128, 128), F32)

    edgeless = jnp.zeros((1, 256), F32)

    @pl.loop(0, frames // GROUP)
    def _(g):
        y = conv([(joined(lat, g * GROUP + i), edgeless, edgeless) for i in range(GROUP)], w3)
        for i in range(GROUP):
            conv_f[g * GROUP + i] = y[i * 64 : i * 64 + 64]

    for m in halos_f:
        m.arrived()
    mask_edges(halo_f)
    for i, f in enumerate((top, low)):
        left, right = halo_rows(halo_f, f)
        rim_f[i, 0:1] = left
        rim_f[i, 1:2] = right
    for m in rims_f:
        m.start()
    left = dot(halo_f[0].astype(BF), w3[0:256, :])
    right = dot(halo_f[1].astype(BF), w3[512:768, :])
    for f in range(frames):
        conv_f[f, 0:1, :] += left[f : f + 1]
        conv_f[f, 63:64, :] += right[f : f + 1]

    def project(h, c, at, real):
        qk = dot(h, wqk[...])
        vg = dot(jnp.concatenate([h, c], axis=1), wvo[...])
        s = lax.rsqrt(dot((qk * qk).astype(BF), mean4) + EPS)
        u = qk * s
        y = u * gains
        for i in range(h.shape[0] // 128):
            rows = slice(i * 128, i * 128 + 128)
            f = at + i
            un[f] = u[rows]
            sc[f] = s[rows]
            key, val = y[rows, 128:], vg[rows, :128]
            kk[f, :128] = jnp.where(head0, key, 0.0).astype(BF)
            kk[f, 128:] = jnp.where(head0, 0.0, key).astype(BF)
            vv[f, :128] = jnp.where(head0, val, 0.0).astype(BF)
            vv[f, 128:] = jnp.where(head0, 0.0, val).astype(BF)
            if real:
                qs[f] = y[rows, :128].astype(BF)
                ga[f] = vg[rows, 128:].astype(BF)

    @pl.loop(0, frames // 2)
    def _(g):
        h = cells(jnp.concatenate([conv_f[g * 2], conv_f[g * 2 + 1]], axis=0).astype(BF))
        at = pl.ds(g * 2, 2)
        hid[at] = h.reshape(2, 128, 128)
        project(h, ct[at].reshape(256, 128), g * 2, True)

    for m in frames_f + rims_f:
        m.arrived()
    below_there, above_there = t > 0, t < nt - 1
    far = []
    for at, there in ((up_at, below_there), (down_at, above_there)):
        x = jnp.where(there, joined(got_f, at), 0.0)
        rim = jnp.where(there, gotrim_f[at], 0.0)
        far.append((x, rim[0:1], rim[1:2]))
    both = cells(conv(far, w3).astype(BF))
    project(both, both, frames, False)

    @pl.loop(0, frames // GROUP)
    def _(g):
        at = [g * GROUP + i for i in range(GROUP)]
        slot = [slots[f] for f in at]
        same = [slots[jnp.maximum(f - 1, 0)] == s for f, s in zip(at, slot)]
        n = range(GROUP)
        raised = [jnp.exp(dot_nt(qs[at[i]], kk[slot[i]]) * 0.125) for i in n]
        total = [dot(r.astype(BF), ones2) for r in raised]
        prob = [raised[i] / total[i] for i in n]
        low_p = [p.astype(BF) for p in prob]
        o = [dot(low_p[i], vv[slot[i]]) for i in n]
        gp = [dot_nt(ga[at[i]], vv[slot[i]]) for i in n]
        for i in n:
            att[at[i]] = o[i].astype(BF)
        delta = [dot((o[i] * ga[at[i]].astype(F32)).astype(BF), spread) for i in n]
        ds = [(prob[i] * (gp[i] - delta[i]) * 0.125).astype(BF) for i in n]
        for i in n:
            gq[at[i]] = dot(ds[i], kk[slot[i]])
        kt = [dot_tn(qs[at[i]], ds[i]) for i in n]
        vt = [dot_tn(ga[at[i]], low_p[i]) for i in n]
        for acc, terms in ((dk, kt), (dv, vt)):
            run = acc[g * GROUP]
            for i in n:
                term = jnp.concatenate([terms[i][:64, :128], terms[i][64:, 128:]], axis=0)
                run = jnp.where(same[i], run, 0.0) + term
                acc[at[i] + 1] = run

    def finish(at, real):
        rows, vals = [], []
        for i in range(2):
            f = at + i
            left = gq[f] if real else jnp.zeros((128, 128), F32)
            until = jnp.clip(lastf[f] + 1, 0, frames)
            rows.append(jnp.concatenate([left, dk[until].T], axis=1))
            vals.append(dv[until].T)
        e = jnp.concatenate(rows, axis=0) * gains
        u = jnp.concatenate([un[at], un[at + 1]], axis=0)
        s = jnp.concatenate([sc[at], sc[at + 1]], axis=0)
        m = dot((e * u).astype(BF), mean4)
        raw = (s * (e - u * m)).astype(BF)
        val = jnp.concatenate(vals, axis=0).astype(BF)
        return dot(raw, wqkt[...]) + dot(val, wvt[...])

    def finish_local(g):
        at = pl.ds(g * 2, 2)
        gh[at] = (ct[at].astype(F32) + finish(g * 2, True).reshape(2, 128, 128)).astype(BF)

    ctx_b[...] = finish(frames, False).reshape(2, 128, 128).astype(BF)
    for i in range(2):
        edges_out(ctx_b, i, edge_g, i)
    frames_b = to_clip(ctx_b.at[1], ctx_b.at[0], got_b, clip_send.at[2], clip_recv.at[2])
    rims_b = to_clip(rim_b.at[1], rim_b.at[0], gotrim_b, clip_send.at[3], clip_recv.at[3])
    halos_g = to_sides(edge_g, halo_g, side_send.at[1], side_recv.at[1])
    halos_b = to_sides(edge_b, halo_b, side_send.at[2], side_recv.at[2])
    for m in halos_g + frames_b:
        m.start()
    pl.loop(0, frames // 2)(finish_local)
    for f in range(frames):
        edges_out(gh, f, edge_b, f)
    for m in halos_b:
        m.start()
    for m in halos_g:
        m.arrived()
    mask_edges(halo_g)
    for i in range(2):
        left, right = halo_rows(halo_g, i)
        rim_b[i, 0:1] = left
        rim_b[i, 1:2] = right
    for m in rims_b:
        m.start()

    @pl.loop(0, frames // GROUP)
    def _(g):
        at = pl.ds(g * GROUP, GROUP)
        o = dot(att[at].reshape(GROUP * 128, 128), wo[...])
        out[at] = (hid[at].astype(F32) + o.reshape(GROUP, 128, 128)).astype(BF)

    stores = [pltpu.make_async_copy(out, out_h, store_sem.at[0])]
    stores[0].start()

    @pl.loop(0, frames // GROUP)
    def _(g):
        y = conv_back([(joined(gh, g * GROUP + i), edgeless, edgeless) for i in range(GROUP)], w3)
        for i in range(GROUP):
            f = g * GROUP + i
            put(lg, f, y[i * 64 : i * 64 + 64])
            rims[0, pl.ds(f, 1), :] = y[i * 64 : i * 64 + 1]
            rims[1, pl.ds(f, 1), :] = y[i * 64 + 63 : i * 64 + 64]

    for m in halos_b:
        m.arrived()
    mask_edges(halo_b)
    rims[0] += dot_nt(halo_b[0].astype(BF), w3[512:768, :])
    rims[1] += dot_nt(halo_b[1].astype(BF), w3[0:256, :])
    row = lax.broadcasted_iota(jnp.int32, (16, 1), 0)

    @pl.loop(0, frames)
    def _(f):
        for side, start, at in ((0, 0, 0), (1, 48, 15)):
            edge = rims[side, pl.ds(f, 1), :]
            for r in range(2):
                rows = slice(r * 64 + start, r * 64 + start + 16)
                tile = jnp.where(row == at, edge[:, r * 128 : r * 128 + 128], lg[f, rows, :].astype(F32))
                lg[f, rows, :] = tile.astype(BF)

    stores.append(pltpu.make_async_copy(lg, lg_h, store_sem.at[1]))
    stores[1].start()
    for m in frames_b + rims_b:
        m.arrived()
    sums = []
    for at in (SPAN, 0):
        x, rim = jnp.zeros((64, 256), F32), jnp.zeros((2, 256), F32)
        for k in range(SPAN):
            x += jnp.where(hits[at + k], joined(got_b, at + k), 0.0)
            rim += jnp.where(hits[at + k], gotrim_b[at + k], 0.0)
        sums.append((x, rim[0:1], rim[1:2]))
    pair[...] = cells(conv_back(sums, w3)).reshape(2, 128, 128)
    stores.append(pltpu.make_async_copy(pair, pair_h, store_sem.at[2]))
    stores[2].start()
    for c in stores + [spots]:
        c.wait()
    for m in halos_f + frames_f + rims_f + halos_g + frames_b + rims_b + halos_b:
        m.sent()


def hand_over(out_k, lg_k, pair_k, spot_k, out_h, lg_h, out, lg, pair, spot, load, store):
    moves = ((out_k, out, out_h), (lg_k, lg, lg_h), (pair_k, pair, None), (spot_k, spot, None))
    loads = [pltpu.make_async_copy(a, b, load.at[i]) for i, (a, b, _) in enumerate(moves)]
    stores = [pltpu.make_async_copy(b, c, store.at[i]) for i, (_, b, c) in enumerate(moves[:2])]
    for c in loads:
        c.start()
    loads[0].wait()
    stores[0].start()
    for c in loads[1:]:
        c.wait()
    for i in range(2):
        at = spot[i]
        lg[at] = (lg[at].astype(F32) + pair[i]).astype(BF)
    stores[1].start()
    for c in stores:
        c.wait()


def per_device(
    latents, cotangent, clip_lengths, context_offset, conv_weight, w_query, w_key, w_value, w_out, query_gain, key_gain
):
    frames, rows, width, channels = latents.shape
    flat = (frames, rows * width, channels)
    one = (rows * width, channels)
    square = (channels, channels)
    slots = frames + 2
    clips = clip_lengths.shape[0]
    smem = lambda n: pltpu.SMEM((n,), jnp.int32)
    edge, few = VMEM((2, frames, 256), F32), VMEM((2, 8, 256), F32)
    comm = lambda: [VMEM((2, *one), BF), VMEM((2, 2, 256), F32), VMEM((2 * SPAN, *one), BF), VMEM((2 * SPAN, 2, 256), F32)]
    result = jax.ShapeDtypeStruct(flat, BF)
    out, lg, pair, spot = pl.pallas_call(
        kernel,
        name="tokenizer_block",
        out_shape=(result, result, jax.ShapeDtypeStruct((2, *one), F32), jax.ShapeDtypeStruct((2,), jnp.int32)),
        in_specs=[pl.BlockSpec(memory_space=pltpu.HBM)] * 11,
        out_specs=(pl.BlockSpec(memory_space=pltpu.HBM),) * 4,
        scratch_shapes=[smem(clips)] * 4
        + [smem(frames), smem(slots)]
        + [VMEM(flat, BF), VMEM(flat, BF), VMEM(conv_weight.shape, BF)]
        + [VMEM(square, BF)] * 4
        + [VMEM((1, channels), F32)] * 2
        + [VMEM((768, 256), BF), VMEM((128, 256), BF), VMEM((256, 256), BF), VMEM((256, 128), BF), VMEM((128, 128), BF)]
        + [
            VMEM(flat, BF),
            VMEM(flat, BF),
            VMEM((slots, 128, 256), F32),
            VMEM((slots, 128, 256), F32),
            VMEM((slots, 256, 128), BF),
            VMEM((slots, 256, 128), BF),
            VMEM(flat, BF),
            VMEM(flat, F32),
            VMEM(flat, BF),
            VMEM((frames + 1, 128, 128), F32),
            VMEM((frames + 1, 128, 128), F32),
            VMEM(flat, BF),
        ]
        + [edge, edge]
        + comm()
        + [edge, edge, few, few]
        + comm()
        + [
            VMEM((frames, 64, 256), F32),
            VMEM((2, frames, 256), F32),
            VMEM(flat, BF),
            VMEM(flat, BF),
            VMEM((2, *one), F32),
            smem(2),
            pltpu.SemaphoreType.DMA((11,)),
            pltpu.SemaphoreType.DMA((4,)),
            pltpu.SemaphoreType.DMA((3, 2)),
            pltpu.SemaphoreType.DMA((3, 2)),
            pltpu.SemaphoreType.DMA((4, 2 * SPAN)),
            pltpu.SemaphoreType.DMA((4, 2 * SPAN)),
        ],
        compiler_params=pltpu.CompilerParams(
            collective_id=0, has_side_effects=True, vmem_limit_bytes=60 << 20
        ),
    )(
        clip_lengths, context_offset, latents.reshape(flat), cotangent.reshape(flat), conv_weight,
        w_query, w_key, w_value, w_out, query_gain.reshape(1, channels), key_gain.reshape(1, channels),
    )
    out, lg = pl.pallas_call(
        hand_over,
        name="hand_over",
        out_shape=(result, result),
        in_specs=[pl.BlockSpec(memory_space=pl.ANY)] * 4,
        out_specs=(pl.BlockSpec(memory_space=pl.ANY),) * 2,
        scratch_shapes=[
            VMEM(flat, BF),
            VMEM(flat, BF),
            VMEM((2, *one), F32),
            smem(2),
            pltpu.SemaphoreType.DMA((4,)),
            pltpu.SemaphoreType.DMA((2,)),
        ],
        compiler_params=pltpu.CompilerParams(vmem_limit_bytes=60 << 20),
    )(out, lg, pair, spot)
    return out.reshape(latents.shape), lg.reshape(latents.shape)


def solution(mesh):
    data = P("tm", None, "space", None)
    return jax.shard_map(
        per_device,
        mesh=mesh,
        in_specs=(data, data) + (P(),) * 9,
        out_specs=(data, data),
        check_vma=False,
    )
```

```python
import jax
import jax.numpy as jnp
from jax import lax
from jax.experimental import pallas as pl
from jax.experimental.pallas import tpu as pltpu
from jax.sharding import PartitionSpec as P

HEAD = 64
SPAN = 4
GROUP = 4
HOPS = (-1, -2, -3, -4, 1, 2, 3, 4)
EPS = 1e-6
MESH = pl.DeviceIdType.MESH
VMEM = pltpu.VMEM
BF = jnp.bfloat16
F32 = jnp.float32
NT = (((1,), (1,)), ((), ()))
TN = (((0,), (0,)), ((), ()))


def dot(a, b):
    return jnp.dot(a, b, preferred_element_type=F32)


def dot_nt(a, b):
    return lax.dot_general(a, b, NT, preferred_element_type=F32)


def dot_tn(a, b):
    return lax.dot_general(a, b, TN, preferred_element_type=F32)


def partners():
    x, t = lax.axis_index("space"), lax.axis_index("tm")
    nx, nt = lax.axis_size("space"), lax.axis_size("tm")
    sides = [({"space": lax.rem(x + 1, nx)}, x + 1 < nx), ({"space": lax.rem(x + nx - 1, nx)}, x >= 1)]
    ups = [({"tm": lax.rem(t + k, nt)}, t + k < nt) for k in range(1, SPAN + 1)]
    downs = [({"tm": lax.rem(t + nt - k, nt)}, t >= k) for k in range(1, SPAN + 1)]
    return sides, ups, downs


class Message:
    def __init__(self, src, dst, send, recv, to, source):
        self.copy = pltpu.make_async_remote_copy(
            src_ref=src, dst_ref=dst, send_sem=send, recv_sem=recv, device_id=to[0], device_id_type=MESH
        )
        self.to, self.source = to[1], source[1]

    def start(self):
        pl.when(self.to)(self.copy.start)

    def sent(self):
        pl.when(self.to)(self.copy.wait_send)

    def arrived(self):
        pl.when(self.source)(self.copy.wait_recv)


def to_sides(src, dst, send, recv):
    sides, _, _ = partners()
    return [Message(src.at[i], dst.at[i], send.at[i], recv.at[i], sides[i], sides[1 - i]) for i in range(2)]


def to_clip(rising, falling, dst, send, recv):
    _, ups, downs = partners()
    out = []
    for k in reversed(range(SPAN)):
        j = SPAN + k
        out.append(Message(rising, dst.at[k], send.at[k], recv.at[k], ups[k], downs[k]))
        out.append(Message(falling, dst.at[j], send.at[j], recv.at[j], downs[k], ups[k]))
    return out


def build_conv(cw_ref, w3):
    for b in range(3):
        for rin in range(2):
            for rout in range(2):
                w3[
                    b * 256 + rin * 128 : b * 256 + rin * 128 + 128, rout * 128 : rout * 128 + 128
                ] = cw_ref[rin - rout + 1, b]


def joined(ref, f):
    return jnp.concatenate([ref[f, 0:64, :], ref[f, 64:128, :]], axis=1).astype(F32)


def shifted(x, left, right):
    row = lax.broadcasted_iota(jnp.int32, (64, 1), 0)
    before = jnp.where(row == 0, left, pltpu.roll(x, 1, 0))
    after = jnp.where(row == 63, right, pltpu.roll(x, 63, 0))
    return before.astype(BF), x.astype(BF), after.astype(BF)


def conv(xs, w3):
    taps = [jnp.concatenate(shifted(*x), axis=1) for x in xs]
    taps = jnp.concatenate(taps, axis=0) if len(taps) > 1 else taps[0]
    whole = jnp.concatenate([x[0] for x in xs], axis=0) if len(xs) > 1 else xs[0][0]
    return whole + dot(taps, w3[...])


def conv_back(xs, w3):
    parts = [shifted(*x) for x in xs]
    cat = lambda i: jnp.concatenate([p[i] for p in parts], axis=0) if len(parts) > 1 else parts[0][i]
    whole = jnp.concatenate([x[0] for x in xs], axis=0) if len(xs) > 1 else xs[0][0]
    out = dot_nt(cat(0), w3[512:768, :])
    out = out + dot_nt(cat(1), w3[256:512, :])
    out = out + dot_nt(cat(2), w3[0:256, :])
    return whole + out


def put(ref, f, y):
    ref[f, 0:64, :] = y[:, :128].astype(ref.dtype)
    ref[f, 64:128, :] = y[:, 128:].astype(ref.dtype)


def edges_out(ref, f, edges, at):
    x = joined(ref, f)
    edges[0, pl.ds(at, 1), :] = x[63:64]
    edges[1, pl.ds(at, 1), :] = x[0:1]


def mask_edges(halo):
    x, nx = lax.axis_index("space"), lax.axis_size("space")
    halo[0] = jnp.where(x > 0, halo[0], 0.0)
    halo[1] = jnp.where(x < nx - 1, halo[1], 0.0)


def halo_rows(halo, f):
    return halo[0, pl.ds(f, 1), :], halo[1, pl.ds(f, 1), :]


def with_halo(ref, halo, f):
    return (joined(ref, f), *halo_rows(halo, f))


def cells(y):
    parts = []
    for i in range(y.shape[0] // 64):
        parts += [y[i * 64 : i * 64 + 64, :128], y[i * 64 : i * 64 + 64, 128:]]
    return jnp.concatenate(parts, axis=0)


def block_ones(rows, cols, rblock, cblock, value):
    r = lax.broadcasted_iota(jnp.int32, (rows, cols), 0) // rblock
    c = lax.broadcasted_iota(jnp.int32, (rows, cols), 1) // cblock
    return jnp.where(r == c, value, 0.0).astype(BF)


def kernel(
    lens_h, offs_h, lat_h, ct_h, cw_h, wq_h, wk_h, wv_h, wo_h, qg_h, kg_h, out_h, lg_h, pair_h, spot_h,
    lens, offs, starts, targets, slots, lastf,
    lat, ct, cw, wq, wk, wv, wo, qg, kg,
    w3, stack, wcat, wot, gainq, gaink,
    hid, un, sc, qq, gg, kvt, kv, gq, att, dk, dv, gh,
    edge_f, halo_f, ctx_f, rim_f, got_f, gotrim_f,
    edge_b, halo_b, edge_g, halo_g, ctx_b, rim_b, got_b, gotrim_b,
    conv_f, rims, out, lg, pair, spot, load_sem, store_sem, side_send, side_recv, clip_send, clip_recv,
):
    frames = lat.shape[0]
    t, nt = lax.axis_index("tm"), lax.axis_size("tm")
    first = t * frames
    last = first + frames - 1

    pairs = [
        (lens_h, lens), (offs_h, offs), (lat_h, lat), (cw_h, cw), (ct_h, ct), (wq_h, wq), (wk_h, wk),
        (wv_h, wv), (wo_h, wo), (qg_h, qg), (kg_h, kg),
    ]
    loads = [pltpu.make_async_copy(a, b, load_sem.at[i]) for i, (a, b) in enumerate(pairs)]
    for c in loads:
        c.start()
    sides, ups, downs = partners()
    barrier = pltpu.get_barrier_semaphore()
    for who, there in sides + ups + downs:

        @pl.when(there)
        def _(who=who):
            pl.semaphore_signal(barrier, inc=1, device_id=who, device_id_type=MESH)

    loads[0].wait()
    loads[1].wait()

    def scan(j, c):
        start, top, low, below, below_end, above = c
        length = lens[j]
        end = start + length
        target = start + lax.rem(offs[j], length)
        starts[j] = start
        targets[j] = target
        inside = (target >= first) & (target <= last)
        top = jnp.where(inside, target, top)
        low = jnp.where(inside, jnp.minimum(low, target), low)
        at_first = start <= first
        below = jnp.where(at_first, target, below)
        below_end = jnp.where(at_first, end, below_end)
        above = jnp.where(start <= last, target, above)
        return end, top, low, below, below_end, above

    init = (jnp.int32(0), first, last, first, first, last)
    _, top, low, below, below_end, above = lax.fori_loop(0, lens.shape[0], scan, init, unroll=4)
    top, low = top - first, low - first
    spot[0] = top
    spot[1] = low
    spots = pltpu.make_async_copy(spot, spot_h, store_sem.at[3])
    spots.start()
    up_at = jnp.clip((first - below + frames - 1) // frames, 1, SPAN) - 1
    down_at = jnp.clip((above - first) // frames, 1, SPAN) - 1 + SPAN

    loads[2].wait()
    ctx_f[0] = lat[top]
    ctx_f[1] = lat[low]
    for f in range(frames):
        edges_out(lat, f, edge_f, f)
    pl.semaphore_wait(barrier, sum(there.astype(jnp.int32) for _, there in sides + ups + downs))

    halos_f = to_sides(edge_f, halo_f, side_send.at[0], side_recv.at[0])
    frames_f = to_clip(ctx_f.at[0], ctx_f.at[1], got_f, clip_send.at[0], clip_recv.at[0])
    rims_f = to_clip(rim_f.at[0], rim_f.at[1], gotrim_f, clip_send.at[1], clip_recv.at[1])
    for m in halos_f + frames_f:
        m.start()

    def scan2(j, c):
        slot, lastof, near = c
        start, target = starts[j], targets[j]
        at = target - first
        mine = jnp.where(at < 0, frames, jnp.where(at >= frames, frames + 1, at))
        end = jnp.minimum(start + lens[j] - 1, last) - first
        slot = [jnp.where(start - first <= f, mine, s) for f, s in enumerate(slot)]
        lastof = [jnp.where(at == f, end, s) for f, s in enumerate(lastof)]
        near = [
            jnp.where(start <= (first + k * frames if k > 0 else last + k * frames), target, s)
            for k, s in zip(HOPS, near)
        ]
        return slot, lastof, near

    zero = jnp.int32(0)
    slot, lastof, near = lax.fori_loop(
        0, lens.shape[0], scan2, ([zero] * frames, [zero - 1] * frames, [zero - 1] * len(HOPS)), unroll=2
    )
    for f in range(frames):
        slots[f] = slot[f]
        lastf[f] = lastof[f]
    lastf[frames] = jnp.where(below < first, jnp.minimum(below_end - 1, last) - first, -1)
    lastf[frames + 1] = jnp.where(above > last, frames - 1, -1)
    hits = [
        (near[i] >= first) & (near[i] <= last) & ((t + k < nt) if k > 0 else (t + k >= 0))
        for i, k in enumerate(HOPS)
    ]

    for c in loads[3:]:
        c.wait()
    build_conv(cw, w3)
    stack[...] = jnp.zeros_like(stack)
    for i, w in enumerate((wq, wk, wv)):
        stack[i * 128 : i * 128 + 128, :128] = w[...].astype(F32).T.astype(BF)
        wcat[:, i * 128 : i * 128 + 128] = w[...]
    stack[384:512, 128:] = wo[...]
    wot[...] = wo[...].astype(F32).T.astype(BF)
    gainq[...] = jnp.broadcast_to(qg[...], (128, 128)).T
    gaink[...] = jnp.broadcast_to(kg[...], (128, 128)).T
    one = block_ones(128, 128, 1, 1, 1.0)
    qq[...] = jnp.zeros_like(qq)
    gg[...] = jnp.zeros_like(gg)
    dk[0] = jnp.zeros((128, 128), F32)
    dv[0] = jnp.zeros((128, 128), F32)

    edgeless = jnp.zeros((1, 256), F32)

    @pl.loop(0, frames // GROUP)
    def _(g):
        y = conv([(joined(lat, g * GROUP + i), edgeless, edgeless) for i in range(GROUP)], w3)
        for i in range(GROUP):
            conv_f[g * GROUP + i] = y[i * 64 : i * 64 + 64]

    for m in halos_f:
        m.arrived()
    mask_edges(halo_f)
    for i, f in enumerate((top, low)):
        left, right = halo_rows(halo_f, f)
        rim_f[i, 0:1] = left
        rim_f[i, 1:2] = right
    for m in rims_f:
        m.start()
    left = dot(halo_f[0].astype(BF), w3[0:256, :])
    right = dot(halo_f[1].astype(BF), w3[512:768, :])
    for f in range(frames):
        conv_f[f, 0:1, :] += left[f : f + 1]
        conv_f[f, 63:64, :] += right[f : f + 1]

    def diagonal(ref, f, x):
        ref[f, :64, :128] = x[:64].astype(BF)
        ref[f, 64:, 128:] = x[64:].astype(BF)

    def per_head(x):
        return [jnp.sum(x[h * HEAD : h * HEAD + HEAD], axis=0, keepdims=True) for h in range(2)]

    def normed(x, gain, f, at):
        rows = []
        for h, total in enumerate(per_head(x * x)):
            s = lax.rsqrt(total * (1.0 / HEAD) + EPS)
            u = x[h * HEAD : h * HEAD + HEAD] * s
            un[f, at * 128 + h * HEAD : at * 128 + h * HEAD + HEAD] = u
            sc[f, at * 2 + h : at * 2 + h + 1] = s
            rows.append(u * gain[h * HEAD : h * HEAD + HEAD])
        return jnp.concatenate(rows, axis=0)

    def project(h, c, at, real):
        y = dot_nt(stack[...] if real else stack[:384], jnp.concatenate([h, c], axis=1))
        for i in range(2):
            cols = slice(i * 128, i * 128 + 128)
            f = at + i
            if real:
                diagonal(qq, f, normed(y[:128, cols], gainq[...], f, 0))
                diagonal(gg, f, y[384:, cols])
            pair_t = jnp.concatenate([normed(y[128:256, cols], gaink[...], f, 1), y[256:384, cols]], axis=0).astype(BF)
            kvt[f] = pair_t
            kv[f] = dot_nt(one, pair_t).astype(BF)

    @pl.loop(0, frames // GROUP)
    def _(g):
        for half in range(GROUP // 2):
            f = g * GROUP + half * 2
            h = cells(jnp.concatenate([conv_f[f], conv_f[f + 1]], axis=0).astype(BF))
            at = pl.ds(f, 2)
            hid[at] = h.reshape(2, 128, 128)
            project(h, ct[at].reshape(256, 128), f, True)

    for m in frames_f + rims_f:
        m.arrived()
    below_there, above_there = t > 0, t < nt - 1
    far = []
    for at, there in ((up_at, below_there), (down_at, above_there)):
        x = jnp.where(there, joined(got_f, at), 0.0)
        rim = jnp.where(there, gotrim_f[at], 0.0)
        far.append((x, rim[0:1], rim[1:2]))
    both = cells(conv(far, w3).astype(BF))
    project(both, both, frames, False)

    def own_head(x):
        return jnp.concatenate([x[:64, :128], x[64:, 128:]], axis=0)

    @pl.loop(0, frames // GROUP)
    def _(g):
        at = [g * GROUP + i for i in range(GROUP)]
        slot = [slots[f] for f in at]
        same = [slots[jnp.maximum(f - 1, 0)] == s for f, s in zip(at, slot)]
        n = range(GROUP)
        raised = [jnp.exp(dot(kv[slot[i], :, :128], qq[at[i]]) * 0.125) for i in n]
        prob = [r * (1.0 / jnp.sum(r, axis=0, keepdims=True)) for r in raised]
        low_p = [p.astype(BF) for p in prob]
        gp = [dot(kv[slot[i], :, 128:], gg[at[i]]) for i in n]
        o = [own_head(dot(kvt[slot[i], 128:], low_p[i])) for i in n]
        for i in n:
            att[at[i]] = o[i].astype(BF)
        delta = [jnp.concatenate(per_head(o[i] * own_head(gg[at[i]].astype(F32))), axis=1) for i in n]
        ds = [(prob[i] * (gp[i] - delta[i])).astype(BF) for i in n]
        for i in n:
            gq[at[i]] = own_head(dot(kvt[slot[i], :128], ds[i]))
        for acc, left, right in ((dk, qq, ds), (dv, gg, low_p)):
            terms = [dot_nt(left[at[i]], right[i]) for i in n]
            run = acc[g * GROUP]
            for i in n:
                run = jnp.where(same[i], run, 0.0) + terms[i]
                acc[at[i] + 1] = run

    def norm_back(e, gain, f, at):
        e = e * (gain * 0.125)
        u = un[f, at * 128 : at * 128 + 128]
        rows = []
        for h, total in enumerate(per_head(e * u)):
            r = slice(h * HEAD, h * HEAD + HEAD)
            s = sc[f, at * 2 + h : at * 2 + h + 1]
            rows.append(s * (e[r] - u[r] * (total * (1.0 / HEAD))))
        return jnp.concatenate(rows, axis=0).astype(BF)

    def finish(at, real):
        cols = []
        for i in range(2):
            f = at + i
            until = jnp.clip(lastf[f] + 1, 0, frames)
            left = [norm_back(gq[f], gainq[...], f, 0)] if real else []
            cols.append(
                jnp.concatenate(left + [norm_back(dk[until], gaink[...], f, 1), dv[until].astype(BF)], axis=0)
            )
        y = dot(wcat[...] if real else wcat[:, 128:], jnp.concatenate(cols, axis=1)).astype(BF)
        return jnp.concatenate([dot_nt(one, y[:, :128]), dot_nt(one, y[:, 128:])], axis=0)

    def finish_local(g):
        at = pl.ds(g * 2, 2)
        gh[at] = (ct[at].astype(F32) + finish(g * 2, True).reshape(2, 128, 128)).astype(BF)

    ctx_b[...] = finish(frames, False).reshape(2, 128, 128).astype(BF)
    for i in range(2):
        edges_out(ctx_b, i, edge_g, i)
    frames_b = to_clip(ctx_b.at[1], ctx_b.at[0], got_b, clip_send.at[2], clip_recv.at[2])
    rims_b = to_clip(rim_b.at[1], rim_b.at[0], gotrim_b, clip_send.at[3], clip_recv.at[3])
    halos_g = to_sides(edge_g, halo_g, side_send.at[1], side_recv.at[1])
    halos_b = to_sides(edge_b, halo_b, side_send.at[2], side_recv.at[2])
    for m in halos_g + frames_b:
        m.start()
    pl.loop(0, frames // 2 - 2)(finish_local)
    for m in halos_g:
        m.arrived()
    mask_edges(halo_g)
    for i in range(2):
        left, right = halo_rows(halo_g, i)
        rim_b[i, 0:1] = left
        rim_b[i, 1:2] = right
    for m in rims_b:
        m.start()
    pl.loop(frames // 2 - 2, frames // 2)(finish_local)
    for f in range(frames):
        edges_out(gh, f, edge_b, f)
    for m in halos_b:
        m.start()

    @pl.loop(0, frames // GROUP)
    def _(g):
        for i in range(0, GROUP, 2):
            f = g * GROUP + i
            y = dot(wot[...], jnp.concatenate([att[f], att[f + 1]], axis=1)).astype(BF)
            out[f] = (hid[f].astype(F32) + dot_nt(one, y[:, :128])).astype(BF)
            out[f + 1] = (hid[f + 1].astype(F32) + dot_nt(one, y[:, 128:])).astype(BF)

    stores = [pltpu.make_async_copy(out, out_h, store_sem.at[0])]
    stores[0].start()

    @pl.loop(0, frames // GROUP)
    def _(g):
        y = conv_back([(joined(gh, g * GROUP + i), edgeless, edgeless) for i in range(GROUP)], w3)
        for i in range(GROUP):
            f = g * GROUP + i
            put(lg, f, y[i * 64 : i * 64 + 64])
            rims[0, pl.ds(f, 1), :] = y[i * 64 : i * 64 + 1]
            rims[1, pl.ds(f, 1), :] = y[i * 64 + 63 : i * 64 + 64]

    for m in halos_b:
        m.arrived()
    mask_edges(halo_b)
    rims[0] += dot_nt(halo_b[0].astype(BF), w3[512:768, :])
    rims[1] += dot_nt(halo_b[1].astype(BF), w3[0:256, :])
    row = lax.broadcasted_iota(jnp.int32, (16, 1), 0)

    @pl.loop(0, frames)
    def _(f):
        for side, start, at in ((0, 0, 0), (1, 48, 15)):
            edge = rims[side, pl.ds(f, 1), :]
            for r in range(2):
                rows = slice(r * 64 + start, r * 64 + start + 16)
                tile = jnp.where(row == at, edge[:, r * 128 : r * 128 + 128], lg[f, rows, :].astype(F32))
                lg[f, rows, :] = tile.astype(BF)

    stores.append(pltpu.make_async_copy(lg, lg_h, store_sem.at[1]))
    stores[1].start()
    for m in frames_b + rims_b:
        m.arrived()
    sums = []
    for at in (SPAN, 0):
        x, rim = jnp.zeros((64, 256), F32), jnp.zeros((2, 256), F32)
        for k in range(SPAN):
            x += jnp.where(hits[at + k], joined(got_b, at + k), 0.0)
            rim += jnp.where(hits[at + k], gotrim_b[at + k], 0.0)
        sums.append((x, rim[0:1], rim[1:2]))
    pair[...] = cells(conv_back(sums, w3)).reshape(2, 128, 128)
    stores.append(pltpu.make_async_copy(pair, pair_h, store_sem.at[2]))
    stores[2].start()
    for c in stores + [spots]:
        c.wait()
    for m in halos_f + frames_f + rims_f + halos_g + frames_b + rims_b + halos_b:
        m.sent()


def hand_over(out_k, lg_k, pair_k, spot_k, out_h, lg_h, out, lg, pair, spot, load, store):
    moves = ((out_k, out, out_h), (lg_k, lg, lg_h), (pair_k, pair, None), (spot_k, spot, None))
    loads = [pltpu.make_async_copy(a, b, load.at[i]) for i, (a, b, _) in enumerate(moves)]
    stores = [pltpu.make_async_copy(b, c, store.at[i]) for i, (_, b, c) in enumerate(moves[:2])]
    for c in loads:
        c.start()
    loads[0].wait()
    stores[0].start()
    for c in loads[1:]:
        c.wait()
    for i in range(2):
        at = spot[i]
        lg[at] = (lg[at].astype(F32) + pair[i]).astype(BF)
    stores[1].start()
    for c in stores:
        c.wait()


def per_device(
    latents, cotangent, clip_lengths, context_offset, conv_weight, w_query, w_key, w_value, w_out, query_gain, key_gain
):
    frames, rows, width, channels = latents.shape
    flat = (frames, rows * width, channels)
    one = (rows * width, channels)
    square = (channels, channels)
    slots = frames + 2
    clips = clip_lengths.shape[0]
    smem = lambda n: pltpu.SMEM((n,), jnp.int32)
    edge, few = VMEM((2, frames, 256), F32), VMEM((2, 8, 256), F32)
    comm = lambda: [VMEM((2, *one), BF), VMEM((2, 2, 256), F32), VMEM((2 * SPAN, *one), BF), VMEM((2 * SPAN, 2, 256), F32)]
    result = jax.ShapeDtypeStruct(flat, BF)
    out, lg, pair, spot = pl.pallas_call(
        kernel,
        name="tokenizer_block",
        out_shape=(result, result, jax.ShapeDtypeStruct((2, *one), F32), jax.ShapeDtypeStruct((2,), jnp.int32)),
        in_specs=[pl.BlockSpec(memory_space=pltpu.HBM)] * 11,
        out_specs=(pl.BlockSpec(memory_space=pltpu.HBM),) * 4,
        scratch_shapes=[smem(clips)] * 4
        + [smem(frames), smem(slots)]
        + [VMEM(flat, BF), VMEM(flat, BF), VMEM(conv_weight.shape, BF)]
        + [VMEM(square, BF)] * 4
        + [VMEM((1, channels), F32)] * 2
        + [VMEM((768, 256), BF), VMEM((512, 256), BF), VMEM((128, 384), BF), VMEM(square, BF)]
        + [VMEM(square, F32)] * 2
        + [
            VMEM(flat, BF),
            VMEM((slots, 256, 128), F32),
            VMEM((slots, 8, 128), F32),
            VMEM((frames, 128, 256), BF),
            VMEM((frames, 128, 256), BF),
            VMEM((slots, 256, 128), BF),
            VMEM((slots, 128, 256), BF),
            VMEM(flat, F32),
            VMEM(flat, BF),
            VMEM((frames + 1, 128, 128), F32),
            VMEM((frames + 1, 128, 128), F32),
            VMEM(flat, BF),
        ]
        + [edge, edge]
        + comm()
        + [edge, edge, few, few]
        + comm()
        + [
            VMEM((frames, 64, 256), F32),
            VMEM((2, frames, 256), F32),
            VMEM(flat, BF),
            VMEM(flat, BF),
            VMEM((2, *one), F32),
            smem(2),
            pltpu.SemaphoreType.DMA((11,)),
            pltpu.SemaphoreType.DMA((4,)),
            pltpu.SemaphoreType.DMA((3, 2)),
            pltpu.SemaphoreType.DMA((3, 2)),
            pltpu.SemaphoreType.DMA((4, 2 * SPAN)),
            pltpu.SemaphoreType.DMA((4, 2 * SPAN)),
        ],
        compiler_params=pltpu.CompilerParams(
            collective_id=0, has_side_effects=True, vmem_limit_bytes=60 << 20
        ),
    )(
        clip_lengths, context_offset, latents.reshape(flat), cotangent.reshape(flat), conv_weight,
        w_query, w_key, w_value, w_out, query_gain.reshape(1, channels), key_gain.reshape(1, channels),
    )
    out, lg = pl.pallas_call(
        hand_over,
        name="hand_over",
        out_shape=(result, result),
        in_specs=[pl.BlockSpec(memory_space=pl.ANY)] * 4,
        out_specs=(pl.BlockSpec(memory_space=pl.ANY),) * 2,
        scratch_shapes=[
            VMEM(flat, BF),
            VMEM(flat, BF),
            VMEM((2, *one), F32),
            smem(2),
            pltpu.SemaphoreType.DMA((4,)),
            pltpu.SemaphoreType.DMA((2,)),
        ],
        compiler_params=pltpu.CompilerParams(vmem_limit_bytes=60 << 20),
    )(out, lg, pair, spot)
    return out.reshape(latents.shape), lg.reshape(latents.shape)


def solution(mesh):
    data = P("tm", None, "space", None)
    return jax.shard_map(
        per_device,
        mesh=mesh,
        in_specs=(data, data) + (P(),) * 9,
        out_specs=(data, data),
        check_vma=False,
    )
```

```python
import jax
import jax.numpy as jnp
from jax import lax
from jax.experimental import pallas as pl
from jax.experimental.pallas import tpu as pltpu
from jax.sharding import PartitionSpec as P

HEAD = 64
SPAN = 4
GROUP = 8
HOPS = (-1, -2, -3, -4, 1, 2, 3, 4)
EPS = 1e-6
MESH = pl.DeviceIdType.MESH
VMEM = pltpu.VMEM
BF = jnp.bfloat16
F32 = jnp.float32
NT = (((1,), (1,)), ((), ()))
TN = (((0,), (0,)), ((), ()))


def dot(a, b):
    return jnp.dot(a, b, preferred_element_type=F32)


def dot_nt(a, b):
    return lax.dot_general(a, b, NT, preferred_element_type=F32)


def dot_tn(a, b):
    return lax.dot_general(a, b, TN, preferred_element_type=F32)


def partners():
    x, t = lax.axis_index("space"), lax.axis_index("tm")
    nx, nt = lax.axis_size("space"), lax.axis_size("tm")
    sides = [({"space": lax.rem(x + 1, nx)}, x + 1 < nx), ({"space": lax.rem(x + nx - 1, nx)}, x >= 1)]
    ups = [({"tm": lax.rem(t + k, nt)}, t + k < nt) for k in range(1, SPAN + 1)]
    downs = [({"tm": lax.rem(t + nt - k, nt)}, t >= k) for k in range(1, SPAN + 1)]
    return sides, ups, downs


class Message:
    def __init__(self, src, dst, send, recv, to, source):
        self.copy = pltpu.make_async_remote_copy(
            src_ref=src, dst_ref=dst, send_sem=send, recv_sem=recv, device_id=to[0], device_id_type=MESH
        )
        self.to, self.source = to[1], source[1]

    def start(self):
        pl.when(self.to)(self.copy.start)

    def sent(self):
        pl.when(self.to)(self.copy.wait_send)

    def arrived(self):
        pl.when(self.source)(self.copy.wait_recv)


def to_sides(src, dst, send, recv):
    sides, _, _ = partners()
    return [Message(src.at[i], dst.at[i], send.at[i], recv.at[i], sides[i], sides[1 - i]) for i in range(2)]


def to_clip(rising, falling, dst, send, recv):
    _, ups, downs = partners()
    out = []
    for k in reversed(range(SPAN)):
        j = SPAN + k
        out.append(Message(rising, dst.at[k], send.at[k], recv.at[k], ups[k], downs[k]))
        out.append(Message(falling, dst.at[j], send.at[j], recv.at[j], downs[k], ups[k]))
    return out


def build_conv(cw_ref, w3):
    for b in range(3):
        for rin in range(2):
            for rout in range(2):
                w3[
                    b * 256 + rin * 128 : b * 256 + rin * 128 + 128, rout * 128 : rout * 128 + 128
                ] = cw_ref[rin - rout + 1, b]


def joined(ref, f):
    return jnp.concatenate([ref[f, 0:64, :], ref[f, 64:128, :]], axis=1).astype(F32)


def shifted(x, left, right):
    row = lax.broadcasted_iota(jnp.int32, (64, 1), 0)
    before = jnp.where(row == 0, left, pltpu.roll(x, 1, 0))
    after = jnp.where(row == 63, right, pltpu.roll(x, 63, 0))
    return before.astype(BF), x.astype(BF), after.astype(BF)


def conv(xs, w3):
    taps = [jnp.concatenate(shifted(*x), axis=1) for x in xs]
    taps = jnp.concatenate(taps, axis=0) if len(taps) > 1 else taps[0]
    whole = jnp.concatenate([x[0] for x in xs], axis=0) if len(xs) > 1 else xs[0][0]
    return whole + dot(taps, w3[...])


def conv_back(xs, w3):
    parts = [shifted(*x) for x in xs]
    cat = lambda i: jnp.concatenate([p[i] for p in parts], axis=0) if len(parts) > 1 else parts[0][i]
    whole = jnp.concatenate([x[0] for x in xs], axis=0) if len(xs) > 1 else xs[0][0]
    out = dot_nt(cat(0), w3[512:768, :])
    out = out + dot_nt(cat(1), w3[256:512, :])
    out = out + dot_nt(cat(2), w3[0:256, :])
    return whole + out


def put(ref, f, y):
    ref[f, 0:64, :] = y[:, :128].astype(ref.dtype)
    ref[f, 64:128, :] = y[:, 128:].astype(ref.dtype)


def edges_out(ref, f, edges, at):
    x = joined(ref, f)
    edges[0, pl.ds(at, 1), :] = x[63:64]
    edges[1, pl.ds(at, 1), :] = x[0:1]


def mask_edges(halo):
    x, nx = lax.axis_index("space"), lax.axis_size("space")
    halo[0] = jnp.where(x > 0, halo[0], 0.0)
    halo[1] = jnp.where(x < nx - 1, halo[1], 0.0)


def halo_rows(halo, f):
    return halo[0, pl.ds(f, 1), :], halo[1, pl.ds(f, 1), :]


def with_halo(ref, halo, f):
    return (joined(ref, f), *halo_rows(halo, f))


def cells(y):
    parts = []
    for i in range(y.shape[0] // 64):
        parts += [y[i * 64 : i * 64 + 64, :128], y[i * 64 : i * 64 + 64, 128:]]
    return jnp.concatenate(parts, axis=0)


def kernel(
    lens_h, offs_h, lat_h, ct_h, cw_h, wq_h, wk_h, wv_h, wo_h, qg_h, kg_h, out_h, lg_h, pair_h, spot_h,
    lens, offs, starts, targets, slots, lastf,
    lat, ct, cw, wq, wk, wv, wo, qg, kg,
    w3, stack, wcat, wot, gainq, gaink,
    hid, un, sc, qq, gg, kvt, kv, gq, att, dk, dv, gh,
    edge_f, halo_f, ctx_f, rim_f, got_f, gotrim_f,
    edge_b, halo_b, edge_g, halo_g, ctx_b, rim_b, got_b, gotrim_b,
    conv_f, rims, out, lg, pair, spot, load_sem, store_sem, side_send, side_recv, clip_send, clip_recv,
):
    frames = lat.shape[0]
    t, nt = lax.axis_index("tm"), lax.axis_size("tm")
    first = t * frames
    last = first + frames - 1

    pairs = [
        (lens_h, lens), (offs_h, offs), (lat_h, lat), (cw_h, cw), (ct_h, ct), (wq_h, wq), (wk_h, wk),
        (wv_h, wv), (wo_h, wo), (qg_h, qg), (kg_h, kg),
    ]
    loads = [pltpu.make_async_copy(a, b, load_sem.at[i]) for i, (a, b) in enumerate(pairs)]
    for c in loads:
        c.start()
    sides, ups, downs = partners()
    barrier = pltpu.get_barrier_semaphore()
    for who, there in sides + ups + downs:

        @pl.when(there)
        def _(who=who):
            pl.semaphore_signal(barrier, inc=1, device_id=who, device_id_type=MESH)

    loads[0].wait()
    loads[1].wait()

    def scan(j, c):
        start, top, low, below, below_end, above = c
        length = lens[j]
        end = start + length
        target = start + lax.rem(offs[j], length)
        starts[j] = start
        targets[j] = target
        inside = (target >= first) & (target <= last)
        top = jnp.where(inside, target, top)
        low = jnp.where(inside, jnp.minimum(low, target), low)
        at_first = start <= first
        below = jnp.where(at_first, target, below)
        below_end = jnp.where(at_first, end, below_end)
        above = jnp.where(start <= last, target, above)
        return end, top, low, below, below_end, above

    init = (jnp.int32(0), first, last, first, first, last)
    _, top, low, below, below_end, above = lax.fori_loop(0, lens.shape[0], scan, init, unroll=4)
    top, low = top - first, low - first
    spot[0] = top
    spot[1] = low
    spots = pltpu.make_async_copy(spot, spot_h, store_sem.at[3])
    spots.start()
    up_at = jnp.clip((first - below + frames - 1) // frames, 1, SPAN) - 1
    down_at = jnp.clip((above - first) // frames, 1, SPAN) - 1 + SPAN

    loads[2].wait()
    ctx_f[0] = lat[top]
    ctx_f[1] = lat[low]
    for f in range(frames):
        edges_out(lat, f, edge_f, f)
    pl.semaphore_wait(barrier, sum(there.astype(jnp.int32) for _, there in sides + ups + downs))

    halos_f = to_sides(edge_f, halo_f, side_send.at[0], side_recv.at[0])
    frames_f = to_clip(ctx_f.at[0], ctx_f.at[1], got_f, clip_send.at[0], clip_recv.at[0])
    rims_f = to_clip(rim_f.at[0], rim_f.at[1], gotrim_f, clip_send.at[1], clip_recv.at[1])
    for m in halos_f + frames_f:
        m.start()

    def scan2(j, c):
        slot, lastof, near = c
        start, target = starts[j], targets[j]
        at = target - first
        mine = jnp.where(at < 0, frames, jnp.where(at >= frames, frames + 1, at))
        end = jnp.minimum(start + lens[j] - 1, last) - first
        slot = [jnp.where(start - first <= f, mine, s) for f, s in enumerate(slot)]
        lastof = [jnp.where(at == f, end, s) for f, s in enumerate(lastof)]
        near = [
            jnp.where(start <= (first + k * frames if k > 0 else last + k * frames), target, s)
            for k, s in zip(HOPS, near)
        ]
        return slot, lastof, near

    zero = jnp.int32(0)
    slot, lastof, near = lax.fori_loop(
        0, lens.shape[0], scan2, ([zero] * frames, [zero - 1] * frames, [zero - 1] * len(HOPS)), unroll=2
    )
    for f in range(frames):
        slots[f] = slot[f]
        lastf[f] = lastof[f]
    lastf[frames] = jnp.where(below < first, jnp.minimum(below_end - 1, last) - first, -1)
    lastf[frames + 1] = jnp.where(above > last, frames - 1, -1)
    hits = [
        (near[i] >= first) & (near[i] <= last) & ((t + k < nt) if k > 0 else (t + k >= 0))
        for i, k in enumerate(HOPS)
    ]

    for c in loads[3:]:
        c.wait()
    build_conv(cw, w3)
    stack[...] = jnp.zeros_like(stack)
    for i, w in enumerate((wq, wk, wv)):
        stack[i * 128 : i * 128 + 128, :128] = w[...].astype(F32).T.astype(BF)
        wcat[:, i * 128 : i * 128 + 128] = w[...]
    stack[384:512, 128:] = wo[...]
    wot[...] = wo[...].astype(F32).T.astype(BF)
    gainq[...] = jnp.broadcast_to(qg[...], (128, 128)).T
    gaink[...] = jnp.broadcast_to(kg[...], (128, 128)).T
    qq[...] = jnp.zeros_like(qq)
    gg[...] = jnp.zeros_like(gg)
    dk[0] = jnp.zeros((128, 128), F32)
    dv[0] = jnp.zeros((128, 128), F32)

    edgeless = jnp.zeros((1, 256), F32)

    @pl.loop(0, frames // GROUP)
    def _(g):
        y = conv([(joined(lat, g * GROUP + i), edgeless, edgeless) for i in range(GROUP)], w3)
        for i in range(GROUP):
            conv_f[g * GROUP + i] = y[i * 64 : i * 64 + 64]

    for m in halos_f:
        m.arrived()
    mask_edges(halo_f)
    for i, f in enumerate((top, low)):
        left, right = halo_rows(halo_f, f)
        rim_f[i, 0:1] = left
        rim_f[i, 1:2] = right
    for m in rims_f:
        m.start()
    left = dot(halo_f[0].astype(BF), w3[0:256, :])
    right = dot(halo_f[1].astype(BF), w3[512:768, :])
    for f in range(frames):
        conv_f[f, 0:1, :] += left[f : f + 1]
        conv_f[f, 63:64, :] += right[f : f + 1]

    def diagonal(ref, f, x):
        ref[f, :64, :128] = x[:64].astype(BF)
        ref[f, 64:, 128:] = x[64:].astype(BF)

    def per_head(x):
        return [jnp.sum(x[h * HEAD : h * HEAD + HEAD], axis=0, keepdims=True) for h in range(2)]

    def normed(x, gain, f, at):
        rows = []
        for h, total in enumerate(per_head(x * x)):
            s = lax.rsqrt(total * (1.0 / HEAD) + EPS)
            u = x[h * HEAD : h * HEAD + HEAD] * s
            un[f, at * 128 + h * HEAD : at * 128 + h * HEAD + HEAD] = u
            sc[f, at * 2 + h : at * 2 + h + 1] = s
            rows.append(u * gain[h * HEAD : h * HEAD + HEAD])
        return jnp.concatenate(rows, axis=0)

    def project(h, c, at, real):
        y = dot_nt(stack[...] if real else stack[:384], jnp.concatenate([h, c], axis=1))
        for i in range(2):
            cols = slice(i * 128, i * 128 + 128)
            f = at + i
            if real:
                diagonal(qq, f, normed(y[:128, cols], gainq[...], f, 0))
                diagonal(gg, f, y[384:, cols])
            pair_t = jnp.concatenate([normed(y[128:256, cols], gaink[...], f, 1), y[256:384, cols]], axis=0).astype(BF)
            kvt[f] = pair_t
            kv[f, :, :128] = pair_t[:128].T
            kv[f, :, 128:] = pair_t[128:].T

    @pl.loop(0, frames // GROUP)
    def _(g):
        for half in range(GROUP // 2):
            f = g * GROUP + half * 2
            h = cells(jnp.concatenate([conv_f[f], conv_f[f + 1]], axis=0).astype(BF))
            at = pl.ds(f, 2)
            hid[at] = h.reshape(2, 128, 128)
            project(h, ct[at].reshape(256, 128), f, True)

    for m in frames_f + rims_f:
        m.arrived()
    below_there, above_there = t > 0, t < nt - 1
    far = []
    for at, there in ((up_at, below_there), (down_at, above_there)):
        x = jnp.where(there, joined(got_f, at), 0.0)
        rim = jnp.where(there, gotrim_f[at], 0.0)
        far.append((x, rim[0:1], rim[1:2]))
    both = cells(conv(far, w3).astype(BF))
    project(both, both, frames, False)

    def own_head(x):
        return jnp.concatenate([x[:64, :128], x[64:, 128:]], axis=0)

    @pl.loop(0, frames // GROUP)
    def _(g):
        at = [g * GROUP + i for i in range(GROUP)]
        slot = [slots[f] for f in at]
        same = [slots[jnp.maximum(f - 1, 0)] == s for f, s in zip(at, slot)]
        n = range(GROUP)
        raised = [jnp.exp(dot(kv[slot[i], :, :128], qq[at[i]]) * 0.125) for i in n]
        prob = [r * (1.0 / jnp.sum(r, axis=0, keepdims=True)) for r in raised]
        low_p = [p.astype(BF) for p in prob]
        gp = [dot(kv[slot[i], :, 128:], gg[at[i]]) for i in n]
        o = [own_head(dot(kvt[slot[i], 128:], low_p[i])) for i in n]
        for i in n:
            att[at[i]] = o[i].astype(BF)
        delta = [jnp.concatenate(per_head(o[i] * own_head(gg[at[i]].astype(F32))), axis=1) for i in n]
        ds = [(prob[i] * (gp[i] - delta[i])).astype(BF) for i in n]
        for i in n:
            gq[at[i]] = own_head(dot(kvt[slot[i], :128], ds[i]))
        for acc, left, right in ((dk, qq, ds), (dv, gg, low_p)):
            terms = [dot_nt(left[at[i]], right[i]) for i in n]
            run = acc[g * GROUP]
            for i in n:
                run = jnp.where(same[i], run, 0.0) + terms[i]
                acc[at[i] + 1] = run

    def norm_back(e, gain, f, at):
        e = e * (gain * 0.125)
        u = un[f, at * 128 : at * 128 + 128]
        rows = []
        for h, total in enumerate(per_head(e * u)):
            r = slice(h * HEAD, h * HEAD + HEAD)
            s = sc[f, at * 2 + h : at * 2 + h + 1]
            rows.append(s * (e[r] - u[r] * (total * (1.0 / HEAD))))
        return jnp.concatenate(rows, axis=0).astype(BF)

    def finish(at, real):
        cols = []
        for i in range(2):
            f = at + i
            until = jnp.clip(lastf[f] + 1, 0, frames)
            left = [norm_back(gq[f], gainq[...], f, 0)] if real else []
            cols.append(
                jnp.concatenate(left + [norm_back(dk[until], gaink[...], f, 1), dv[until].astype(BF)], axis=0)
            )
        y = dot(wcat[...] if real else wcat[:, 128:], jnp.concatenate(cols, axis=1))
        return jnp.stack([y[:, :128].T, y[:, 128:].T])

    def finish_local(g):
        for i in range(0, GROUP, 2):
            at = pl.ds(g * GROUP + i, 2)
            gh[at] = (ct[at].astype(F32) + finish(g * GROUP + i, True)).astype(BF)

    ctx_b[...] = finish(frames, False).astype(BF)
    for i in range(2):
        edges_out(ctx_b, i, edge_g, i)
    frames_b = to_clip(ctx_b.at[1], ctx_b.at[0], got_b, clip_send.at[2], clip_recv.at[2])
    rims_b = to_clip(rim_b.at[1], rim_b.at[0], gotrim_b, clip_send.at[3], clip_recv.at[3])
    halos_g = to_sides(edge_g, halo_g, side_send.at[1], side_recv.at[1])
    halos_b = to_sides(edge_b, halo_b, side_send.at[2], side_recv.at[2])
    for m in halos_g + frames_b:
        m.start()
    early = frames // GROUP // 2
    pl.loop(0, early)(finish_local)
    for m in halos_g:
        m.arrived()
    mask_edges(halo_g)
    for i in range(2):
        left, right = halo_rows(halo_g, i)
        rim_b[i, 0:1] = left
        rim_b[i, 1:2] = right
    for m in rims_b:
        m.start()
    pl.loop(early, frames // GROUP)(finish_local)
    for f in range(frames):
        edges_out(gh, f, edge_b, f)
    for m in halos_b:
        m.start()

    @pl.loop(0, frames // GROUP)
    def _(g):
        for i in range(0, GROUP, 2):
            f = g * GROUP + i
            y = dot(wot[...], jnp.concatenate([att[f], att[f + 1]], axis=1))
            out[f] = (hid[f].astype(F32) + y[:, :128].T).astype(BF)
            out[f + 1] = (hid[f + 1].astype(F32) + y[:, 128:].T).astype(BF)

    stores = [pltpu.make_async_copy(out, out_h, store_sem.at[0])]
    stores[0].start()

    @pl.loop(0, frames // GROUP)
    def _(g):
        y = conv_back([(joined(gh, g * GROUP + i), edgeless, edgeless) for i in range(GROUP)], w3)
        for i in range(GROUP):
            f = g * GROUP + i
            put(lg, f, y[i * 64 : i * 64 + 64])
            rims[0, pl.ds(f, 1), :] = y[i * 64 : i * 64 + 1]
            rims[1, pl.ds(f, 1), :] = y[i * 64 + 63 : i * 64 + 64]

    for m in halos_b:
        m.arrived()
    mask_edges(halo_b)
    rims[0] += dot_nt(halo_b[0].astype(BF), w3[512:768, :])
    rims[1] += dot_nt(halo_b[1].astype(BF), w3[0:256, :])
    row = lax.broadcasted_iota(jnp.int32, (16, 1), 0)

    @pl.loop(0, frames)
    def _(f):
        for side, start, at in ((0, 0, 0), (1, 48, 15)):
            edge = rims[side, pl.ds(f, 1), :]
            for r in range(2):
                rows = slice(r * 64 + start, r * 64 + start + 16)
                tile = jnp.where(row == at, edge[:, r * 128 : r * 128 + 128], lg[f, rows, :].astype(F32))
                lg[f, rows, :] = tile.astype(BF)

    stores.append(pltpu.make_async_copy(lg, lg_h, store_sem.at[1]))
    stores[1].start()
    for m in frames_b + rims_b:
        m.arrived()
    sums = []
    for at in (SPAN, 0):
        x, rim = jnp.zeros((64, 256), F32), jnp.zeros((2, 256), F32)
        for k in range(SPAN):
            x += jnp.where(hits[at + k], joined(got_b, at + k), 0.0)
            rim += jnp.where(hits[at + k], gotrim_b[at + k], 0.0)
        sums.append((x, rim[0:1], rim[1:2]))
    pair[...] = cells(conv_back(sums, w3)).reshape(2, 128, 128)
    stores.append(pltpu.make_async_copy(pair, pair_h, store_sem.at[2]))
    stores[2].start()
    for c in stores + [spots]:
        c.wait()
    for m in halos_f + frames_f + rims_f + halos_g + frames_b + rims_b + halos_b:
        m.sent()


def hand_over(out_k, lg_k, pair_k, spot_k, out_h, lg_h, out, lg, pair, spot, load, store):
    moves = ((out_k, out, out_h), (lg_k, lg, lg_h), (pair_k, pair, None), (spot_k, spot, None))
    loads = [pltpu.make_async_copy(a, b, load.at[i]) for i, (a, b, _) in enumerate(moves)]
    stores = [pltpu.make_async_copy(b, c, store.at[i]) for i, (_, b, c) in enumerate(moves[:2])]
    for c in loads:
        c.start()
    loads[0].wait()
    stores[0].start()
    for c in loads[1:]:
        c.wait()
    for i in range(2):
        at = spot[i]
        lg[at] = (lg[at].astype(F32) + pair[i]).astype(BF)
    stores[1].start()
    for c in stores:
        c.wait()


def per_device(
    latents, cotangent, clip_lengths, context_offset, conv_weight, w_query, w_key, w_value, w_out, query_gain, key_gain
):
    frames, rows, width, channels = latents.shape
    flat = (frames, rows * width, channels)
    one = (rows * width, channels)
    square = (channels, channels)
    slots = frames + 2
    clips = clip_lengths.shape[0]
    smem = lambda n: pltpu.SMEM((n,), jnp.int32)
    edge, few = VMEM((2, frames, 256), F32), VMEM((2, 8, 256), F32)
    comm = lambda: [VMEM((2, *one), BF), VMEM((2, 2, 256), F32), VMEM((2 * SPAN, *one), BF), VMEM((2 * SPAN, 2, 256), F32)]
    result = jax.ShapeDtypeStruct(flat, BF)
    out, lg, pair, spot = pl.pallas_call(
        kernel,
        name="tokenizer_block",
        out_shape=(result, result, jax.ShapeDtypeStruct((2, *one), F32), jax.ShapeDtypeStruct((2,), jnp.int32)),
        in_specs=[pl.BlockSpec(memory_space=pltpu.HBM)] * 11,
        out_specs=(pl.BlockSpec(memory_space=pltpu.HBM),) * 4,
        scratch_shapes=[smem(clips)] * 4
        + [smem(frames), smem(slots)]
        + [VMEM(flat, BF), VMEM(flat, BF), VMEM(conv_weight.shape, BF)]
        + [VMEM(square, BF)] * 4
        + [VMEM((1, channels), F32)] * 2
        + [VMEM((768, 256), BF), VMEM((512, 256), BF), VMEM((128, 384), BF), VMEM(square, BF)]
        + [VMEM(square, F32)] * 2
        + [
            VMEM(flat, BF),
            VMEM((slots, 256, 128), F32),
            VMEM((slots, 8, 128), F32),
            VMEM((frames, 128, 256), BF),
            VMEM((frames, 128, 256), BF),
            VMEM((slots, 256, 128), BF),
            VMEM((slots, 128, 256), BF),
            VMEM(flat, F32),
            VMEM(flat, BF),
            VMEM((frames + 1, 128, 128), F32),
            VMEM((frames + 1, 128, 128), F32),
            VMEM(flat, BF),
        ]
        + [edge, edge]
        + comm()
        + [edge, edge, few, few]
        + comm()
        + [
            VMEM((frames, 64, 256), F32),
            VMEM((2, frames, 256), F32),
            VMEM(flat, BF),
            VMEM(flat, BF),
            VMEM((2, *one), F32),
            smem(2),
            pltpu.SemaphoreType.DMA((11,)),
            pltpu.SemaphoreType.DMA((4,)),
            pltpu.SemaphoreType.DMA((3, 2)),
            pltpu.SemaphoreType.DMA((3, 2)),
            pltpu.SemaphoreType.DMA((4, 2 * SPAN)),
            pltpu.SemaphoreType.DMA((4, 2 * SPAN)),
        ],
        compiler_params=pltpu.CompilerParams(
            collective_id=0, has_side_effects=True, vmem_limit_bytes=60 << 20
        ),
    )(
        clip_lengths, context_offset, latents.reshape(flat), cotangent.reshape(flat), conv_weight,
        w_query, w_key, w_value, w_out, query_gain.reshape(1, channels), key_gain.reshape(1, channels),
    )
    out, lg = pl.pallas_call(
        hand_over,
        name="hand_over",
        out_shape=(result, result),
        in_specs=[pl.BlockSpec(memory_space=pl.ANY)] * 4,
        out_specs=(pl.BlockSpec(memory_space=pl.ANY),) * 2,
        scratch_shapes=[
            VMEM(flat, BF),
            VMEM(flat, BF),
            VMEM((2, *one), F32),
            smem(2),
            pltpu.SemaphoreType.DMA((4,)),
            pltpu.SemaphoreType.DMA((2,)),
        ],
        compiler_params=pltpu.CompilerParams(vmem_limit_bytes=60 << 20),
    )(out, lg, pair, spot)
    return out.reshape(latents.shape), lg.reshape(latents.shape)


def solution(mesh):
    data = P("tm", None, "space", None)
    return jax.shard_map(
        per_device,
        mesh=mesh,
        in_specs=(data, data) + (P(),) * 9,
        out_specs=(data, data),
        check_vma=False,
    )
```

```python
import jax
import jax.numpy as jnp
from jax import lax
from jax.experimental import pallas as pl
from jax.experimental.pallas import tpu as pltpu
from jax.sharding import PartitionSpec as P

HEAD = 64
SPAN = 4
GROUP = 8
HOPS = (-1, -2, -3, -4, 1, 2, 3, 4)
EPS = 1e-6
MESH = pl.DeviceIdType.MESH
VMEM = pltpu.VMEM
BF = jnp.bfloat16
F32 = jnp.float32
NT = (((1,), (1,)), ((), ()))
TN = (((0,), (0,)), ((), ()))


def dot(a, b):
    return jnp.dot(a, b, preferred_element_type=F32)


def dot_nt(a, b):
    return lax.dot_general(a, b, NT, preferred_element_type=F32)


def dot_tn(a, b):
    return lax.dot_general(a, b, TN, preferred_element_type=F32)


def partners():
    x, t = lax.axis_index("space"), lax.axis_index("tm")
    nx, nt = lax.axis_size("space"), lax.axis_size("tm")
    sides = [({"space": lax.rem(x + 1, nx)}, x + 1 < nx), ({"space": lax.rem(x + nx - 1, nx)}, x >= 1)]
    ups = [({"tm": lax.rem(t + k, nt)}, t + k < nt) for k in range(1, SPAN + 1)]
    downs = [({"tm": lax.rem(t + nt - k, nt)}, t >= k) for k in range(1, SPAN + 1)]
    return sides, ups, downs


class Message:
    def __init__(self, src, dst, send, recv, to, source):
        self.copy = pltpu.make_async_remote_copy(
            src_ref=src, dst_ref=dst, send_sem=send, recv_sem=recv, device_id=to[0], device_id_type=MESH
        )
        self.to, self.source = to[1], source[1]

    def start(self):
        pl.when(self.to)(self.copy.start)

    def sent(self):
        pl.when(self.to)(self.copy.wait_send)

    def arrived(self):
        pl.when(self.source)(self.copy.wait_recv)


def to_sides(src, dst, send, recv):
    sides, _, _ = partners()
    return [Message(src.at[i], dst.at[i], send.at[i], recv.at[i], sides[i], sides[1 - i]) for i in range(2)]


def to_clip(rising, falling, dst, send, recv):
    _, ups, downs = partners()
    out = []
    for k in reversed(range(SPAN)):
        j = SPAN + k
        out.append(Message(rising, dst.at[k], send.at[k], recv.at[k], ups[k], downs[k]))
        out.append(Message(falling, dst.at[j], send.at[j], recv.at[j], downs[k], ups[k]))
    return out


def build_conv(cw_ref, w3):
    for b in range(3):
        for rin in range(2):
            for rout in range(2):
                w3[
                    b * 256 + rin * 128 : b * 256 + rin * 128 + 128, rout * 128 : rout * 128 + 128
                ] = cw_ref[rin - rout + 1, b]


def joined(ref, f):
    return jnp.concatenate([ref[f, 0:64, :], ref[f, 64:128, :]], axis=1).astype(F32)


def shifted(x, left, right):
    row = lax.broadcasted_iota(jnp.int32, (64, 1), 0)
    before = jnp.where(row == 0, left, pltpu.roll(x, 1, 0))
    after = jnp.where(row == 63, right, pltpu.roll(x, 63, 0))
    return before.astype(BF), x.astype(BF), after.astype(BF)


def conv(xs, w3):
    taps = [jnp.concatenate(shifted(*x), axis=1) for x in xs]
    taps = jnp.concatenate(taps, axis=0) if len(taps) > 1 else taps[0]
    whole = jnp.concatenate([x[0] for x in xs], axis=0) if len(xs) > 1 else xs[0][0]
    return whole + dot(taps, w3[...])


def conv_back(xs, w3):
    parts = [shifted(*x) for x in xs]
    cat = lambda i: jnp.concatenate([p[i] for p in parts], axis=0) if len(parts) > 1 else parts[0][i]
    whole = jnp.concatenate([x[0] for x in xs], axis=0) if len(xs) > 1 else xs[0][0]
    out = dot_nt(cat(0), w3[512:768, :])
    out = out + dot_nt(cat(1), w3[256:512, :])
    out = out + dot_nt(cat(2), w3[0:256, :])
    return whole + out


def put(ref, f, y):
    ref[f, 0:64, :] = y[:, :128].astype(ref.dtype)
    ref[f, 64:128, :] = y[:, 128:].astype(ref.dtype)


def edges_out(ref, f, edges, at):
    x = joined(ref, f)
    edges[0, pl.ds(at, 1), :] = x[63:64]
    edges[1, pl.ds(at, 1), :] = x[0:1]


def mask_edges(halo):
    x, nx = lax.axis_index("space"), lax.axis_size("space")
    halo[0] = jnp.where(x > 0, halo[0], 0.0)
    halo[1] = jnp.where(x < nx - 1, halo[1], 0.0)


def halo_rows(halo, f):
    return halo[0, pl.ds(f, 1), :], halo[1, pl.ds(f, 1), :]


def with_halo(ref, halo, f):
    return (joined(ref, f), *halo_rows(halo, f))


def cells(y):
    parts = []
    for i in range(y.shape[0] // 64):
        parts += [y[i * 64 : i * 64 + 64, :128], y[i * 64 : i * 64 + 64, 128:]]
    return jnp.concatenate(parts, axis=0)


def kernel(
    lens_h, offs_h, lat_h, ct_h, cw_h, wq_h, wk_h, wv_h, wo_h, qg_h, kg_h, out_h, lg_h, pair_h, spot_h,
    lens, offs, starts, targets, slots, lastf,
    lat, ct, cw, wq, wk, wv, wo, qg, kg,
    w3, stack, wcat, wot, gainq, gaink,
    hid, un, sc, qq, gg, kvt, kv, weights, grads, dk, dv, gh,
    edge_f, halo_f, ctx_f, rim_f, got_f, gotrim_f,
    edge_b, halo_b, edge_g, halo_g, ctx_b, rim_b, got_b, gotrim_b,
    conv_f, rims, out, lg, pair, spot, load_sem, store_sem, side_send, side_recv, clip_send, clip_recv,
):
    frames = lat.shape[0]
    t, nt = lax.axis_index("tm"), lax.axis_size("tm")
    first = t * frames
    last = first + frames - 1

    pairs = [
        (lens_h, lens), (offs_h, offs), (lat_h, lat), (cw_h, cw), (ct_h, ct), (wq_h, wq), (wk_h, wk),
        (wv_h, wv), (wo_h, wo), (qg_h, qg), (kg_h, kg),
    ]
    loads = [pltpu.make_async_copy(a, b, load_sem.at[i]) for i, (a, b) in enumerate(pairs)]
    for c in loads:
        c.start()
    sides, ups, downs = partners()
    barrier = pltpu.get_barrier_semaphore()
    for who, there in sides + ups + downs:

        @pl.when(there)
        def _(who=who):
            pl.semaphore_signal(barrier, inc=1, device_id=who, device_id_type=MESH)

    loads[0].wait()
    loads[1].wait()

    def scan(j, c):
        start, top, low, below, below_end, above = c
        length = lens[j]
        end = start + length
        target = start + lax.rem(offs[j], length)
        starts[j] = start
        targets[j] = target
        inside = (target >= first) & (target <= last)
        top = jnp.where(inside, target, top)
        low = jnp.where(inside, jnp.minimum(low, target), low)
        at_first = start <= first
        below = jnp.where(at_first, target, below)
        below_end = jnp.where(at_first, end, below_end)
        above = jnp.where(start <= last, target, above)
        return end, top, low, below, below_end, above

    init = (jnp.int32(0), first, last, first, first, last)
    _, top, low, below, below_end, above = lax.fori_loop(0, lens.shape[0], scan, init, unroll=4)
    top, low = top - first, low - first
    spot[0] = top
    spot[1] = low
    spots = pltpu.make_async_copy(spot, spot_h, store_sem.at[3])
    spots.start()
    up_at = jnp.clip((first - below + frames - 1) // frames, 1, SPAN) - 1
    down_at = jnp.clip((above - first) // frames, 1, SPAN) - 1 + SPAN

    loads[2].wait()
    ctx_f[0] = lat[top]
    ctx_f[1] = lat[low]
    for f in range(frames):
        edges_out(lat, f, edge_f, f)
    pl.semaphore_wait(barrier, sum(there.astype(jnp.int32) for _, there in sides + ups + downs))

    halos_f = to_sides(edge_f, halo_f, side_send.at[0], side_recv.at[0])
    frames_f = to_clip(ctx_f.at[0], ctx_f.at[1], got_f, clip_send.at[0], clip_recv.at[0])
    rims_f = to_clip(rim_f.at[0], rim_f.at[1], gotrim_f, clip_send.at[1], clip_recv.at[1])
    for m in halos_f + frames_f:
        m.start()

    def scan2(j, c):
        slot, lastof, near = c
        start, target = starts[j], targets[j]
        at = target - first
        mine = jnp.where(at < 0, frames, jnp.where(at >= frames, frames + 1, at))
        end = jnp.minimum(start + lens[j] - 1, last) - first
        slot = [jnp.where(start - first <= f, mine, s) for f, s in enumerate(slot)]
        lastof = [jnp.where(at == f, end, s) for f, s in enumerate(lastof)]
        near = [
            jnp.where(start <= (first + k * frames if k > 0 else last + k * frames), target, s)
            for k, s in zip(HOPS, near)
        ]
        return slot, lastof, near

    zero = jnp.int32(0)
    slot, lastof, near = lax.fori_loop(
        0, lens.shape[0], scan2, ([zero] * frames, [zero - 1] * frames, [zero - 1] * len(HOPS)), unroll=2
    )
    for f in range(frames):
        slots[f] = slot[f]
        lastf[f] = lastof[f]
    lastf[frames] = jnp.where(below < first, jnp.minimum(below_end - 1, last) - first, -1)
    lastf[frames + 1] = jnp.where(above > last, frames - 1, -1)
    hits = [
        (near[i] >= first) & (near[i] <= last) & ((t + k < nt) if k > 0 else (t + k >= 0))
        for i, k in enumerate(HOPS)
    ]

    for c in loads[3:]:
        c.wait()
    build_conv(cw, w3)
    stack[...] = jnp.zeros_like(stack)
    for i, w in enumerate((wq, wk, wv)):
        stack[i * 128 : i * 128 + 128, :128] = w[...].astype(F32).T.astype(BF)
        wcat[:, i * 128 : i * 128 + 128] = w[...]
    stack[384:512, 128:] = wo[...]
    wot[...] = wo[...].astype(F32).T.astype(BF)
    gainq[...] = jnp.broadcast_to(qg[...], (128, 128)).T
    gaink[...] = jnp.broadcast_to(kg[...], (128, 128)).T
    qq[...] = jnp.zeros_like(qq)
    gg[...] = jnp.zeros_like(gg)
    dk[0] = jnp.zeros((128, 128), F32)
    dv[0] = jnp.zeros((128, 128), F32)

    edgeless = jnp.zeros((1, 256), F32)

    @pl.loop(0, frames // GROUP)
    def _(g):
        y = conv([(joined(lat, g * GROUP + i), edgeless, edgeless) for i in range(GROUP)], w3)
        for i in range(GROUP):
            conv_f[g * GROUP + i] = y[i * 64 : i * 64 + 64]

    for m in halos_f:
        m.arrived()
    mask_edges(halo_f)
    for i, f in enumerate((top, low)):
        left, right = halo_rows(halo_f, f)
        rim_f[i, 0:1] = left
        rim_f[i, 1:2] = right
    for m in rims_f:
        m.start()
    left = dot(halo_f[0].astype(BF), w3[0:256, :])
    right = dot(halo_f[1].astype(BF), w3[512:768, :])
    for f in range(frames):
        conv_f[f, 0:1, :] += left[f : f + 1]
        conv_f[f, 63:64, :] += right[f : f + 1]

    def diagonal(ref, f, x):
        ref[f, :64, :128] = x[:64].astype(BF)
        ref[f, 64:, 128:] = x[64:].astype(BF)

    def per_head(x):
        return [jnp.sum(x[h * HEAD : h * HEAD + HEAD], axis=0, keepdims=True) for h in range(2)]

    def normed(x, gain, f, at):
        rows = []
        for h, total in enumerate(per_head(x * x)):
            s = lax.rsqrt(total * (1.0 / HEAD) + EPS)
            u = x[h * HEAD : h * HEAD + HEAD] * s
            un[f, at * 128 + h * HEAD : at * 128 + h * HEAD + HEAD] = u
            sc[f, at * 2 + h : at * 2 + h + 1] = s
            rows.append(u * gain[h * HEAD : h * HEAD + HEAD])
        return jnp.concatenate(rows, axis=0)

    def project(h, c, at, real):
        y = dot_nt(stack[...] if real else stack[:384], jnp.concatenate([h, c], axis=1))
        for i in range(2):
            cols = slice(i * 128, i * 128 + 128)
            f = at + i
            if real:
                diagonal(qq, f, normed(y[:128, cols], gainq[...], f, 0))
                diagonal(gg, f, y[384:, cols])
            pair_t = jnp.concatenate([normed(y[128:256, cols], gaink[...], f, 1), y[256:384, cols]], axis=0).astype(BF)
            kvt[f] = pair_t
            kv[f, :, :128] = pair_t[:128].T
            kv[f, :, 128:] = pair_t[128:].T

    @pl.loop(0, frames // GROUP)
    def _(g):
        for half in range(GROUP // 2):
            f = g * GROUP + half * 2
            h = cells(jnp.concatenate([conv_f[f], conv_f[f + 1]], axis=0).astype(BF))
            at = pl.ds(f, 2)
            hid[at] = h.reshape(2, 128, 128)
            project(h, ct[at].reshape(256, 128), f, True)

    for m in frames_f + rims_f:
        m.arrived()
    below_there, above_there = t > 0, t < nt - 1
    far = []
    for at, there in ((up_at, below_there), (down_at, above_there)):
        x = jnp.where(there, joined(got_f, at), 0.0)
        rim = jnp.where(there, gotrim_f[at], 0.0)
        far.append((x, rim[0:1], rim[1:2]))
    both = cells(conv(far, w3).astype(BF))
    project(both, both, frames, False)

    def own_head(x):
        return jnp.concatenate([x[:64, :128], x[64:, 128:]], axis=0)

    @pl.loop(0, frames // GROUP)
    def _(g):
        at = [g * GROUP + i for i in range(GROUP)]
        slot = [slots[f] for f in at]
        same = [slots[jnp.maximum(f - 1, 0)] == s for f, s in zip(at, slot)]
        n = range(GROUP)
        raised = [jnp.exp(dot(kv[slot[i], :, :128], qq[at[i]]) * 0.125) for i in n]
        prob = [r * (1.0 / jnp.sum(r, axis=0, keepdims=True)) for r in raised]
        low_p = [p.astype(BF) for p in prob]
        gp = [dot(kv[slot[i], :, 128:], gg[at[i]]) for i in n]
        delta = [jnp.sum(gp[i] * prob[i], axis=0, keepdims=True) for i in n]
        ds = [(prob[i] * (gp[i] - delta[i])).astype(BF) for i in n]
        for i in n:
            weights[at[i]] = low_p[i]
            grads[at[i]] = ds[i]
        for acc, left, right in ((dk, qq, ds), (dv, gg, low_p)):
            terms = [dot_nt(left[at[i]], right[i]) for i in n]
            run = acc[g * GROUP]
            for i in n:
                run = jnp.where(same[i], run, 0.0) + terms[i]
                acc[at[i] + 1] = run

    def norm_back(e, gain, f, at):
        e = e * (gain * 0.125)
        u = un[f, at * 128 : at * 128 + 128]
        rows = []
        for h, total in enumerate(per_head(e * u)):
            r = slice(h * HEAD, h * HEAD + HEAD)
            s = sc[f, at * 2 + h : at * 2 + h + 1]
            rows.append(s * (e[r] - u[r] * (total * (1.0 / HEAD))))
        return jnp.concatenate(rows, axis=0).astype(BF)

    def finish(at, real):
        cols = []
        for i in range(2):
            f = at + i
            until = jnp.clip(lastf[f] + 1, 0, frames)
            left = []
            if real:
                gq = own_head(dot(kvt[slots[f], :128], grads[f]))
                left = [norm_back(gq, gainq[...], f, 0)]
            cols.append(
                jnp.concatenate(left + [norm_back(dk[until], gaink[...], f, 1), dv[until].astype(BF)], axis=0)
            )
        y = dot(wcat[...] if real else wcat[:, 128:], jnp.concatenate(cols, axis=1))
        return jnp.stack([y[:, :128].T, y[:, 128:].T])

    def finish_local(g):
        for i in range(0, GROUP, 2):
            at = pl.ds(g * GROUP + i, 2)
            gh[at] = (ct[at].astype(F32) + finish(g * GROUP + i, True)).astype(BF)

    ctx_b[...] = finish(frames, False).astype(BF)
    for i in range(2):
        edges_out(ctx_b, i, edge_g, i)
    frames_b = to_clip(ctx_b.at[1], ctx_b.at[0], got_b, clip_send.at[2], clip_recv.at[2])
    rims_b = to_clip(rim_b.at[1], rim_b.at[0], gotrim_b, clip_send.at[3], clip_recv.at[3])
    halos_g = to_sides(edge_g, halo_g, side_send.at[1], side_recv.at[1])
    halos_b = to_sides(edge_b, halo_b, side_send.at[2], side_recv.at[2])
    for m in halos_g + frames_b:
        m.start()
    early = frames // GROUP // 2
    pl.loop(0, early)(finish_local)
    for m in halos_g:
        m.arrived()
    mask_edges(halo_g)
    for i in range(2):
        left, right = halo_rows(halo_g, i)
        rim_b[i, 0:1] = left
        rim_b[i, 1:2] = right
    for m in rims_b:
        m.start()
    pl.loop(early, frames // GROUP)(finish_local)
    for f in range(frames):
        edges_out(gh, f, edge_b, f)
    for m in halos_b:
        m.start()

    @pl.loop(0, frames // GROUP)
    def _(g):
        for i in range(0, GROUP, 2):
            f = g * GROUP + i
            att = [own_head(dot(kvt[slots[e], 128:], weights[e])).astype(BF) for e in (f, f + 1)]
            y = dot(wot[...], jnp.concatenate(att, axis=1))
            out[f] = (hid[f].astype(F32) + y[:, :128].T).astype(BF)
            out[f + 1] = (hid[f + 1].astype(F32) + y[:, 128:].T).astype(BF)

    stores = [pltpu.make_async_copy(out, out_h, store_sem.at[0])]
    stores[0].start()

    @pl.loop(0, frames // GROUP)
    def _(g):
        y = conv_back([(joined(gh, g * GROUP + i), edgeless, edgeless) for i in range(GROUP)], w3)
        for i in range(GROUP):
            f = g * GROUP + i
            put(lg, f, y[i * 64 : i * 64 + 64])
            rims[0, pl.ds(f, 1), :] = y[i * 64 : i * 64 + 1]
            rims[1, pl.ds(f, 1), :] = y[i * 64 + 63 : i * 64 + 64]

    for m in halos_b:
        m.arrived()
    mask_edges(halo_b)
    rims[0] += dot_nt(halo_b[0].astype(BF), w3[512:768, :])
    rims[1] += dot_nt(halo_b[1].astype(BF), w3[0:256, :])
    row = lax.broadcasted_iota(jnp.int32, (16, 1), 0)

    @pl.loop(0, frames)
    def _(f):
        for side, start, at in ((0, 0, 0), (1, 48, 15)):
            edge = rims[side, pl.ds(f, 1), :]
            for r in range(2):
                rows = slice(r * 64 + start, r * 64 + start + 16)
                tile = jnp.where(row == at, edge[:, r * 128 : r * 128 + 128], lg[f, rows, :].astype(F32))
                lg[f, rows, :] = tile.astype(BF)

    stores.append(pltpu.make_async_copy(lg, lg_h, store_sem.at[1]))
    stores[1].start()
    for m in frames_b + rims_b:
        m.arrived()
    sums = []
    for at in (SPAN, 0):
        x, rim = jnp.zeros((64, 256), F32), jnp.zeros((2, 256), F32)
        for k in range(SPAN):
            x += jnp.where(hits[at + k], joined(got_b, at + k), 0.0)
            rim += jnp.where(hits[at + k], gotrim_b[at + k], 0.0)
        sums.append((x, rim[0:1], rim[1:2]))
    pair[...] = cells(conv_back(sums, w3)).reshape(2, 128, 128)
    stores.append(pltpu.make_async_copy(pair, pair_h, store_sem.at[2]))
    stores[2].start()
    for c in stores + [spots]:
        c.wait()
    for m in halos_f + frames_f + rims_f + halos_g + frames_b + rims_b + halos_b:
        m.sent()


def hand_over(out_k, lg_k, pair_k, spot_k, out_h, lg_h, out, lg, pair, spot, load, store):
    moves = ((out_k, out, out_h), (lg_k, lg, lg_h), (pair_k, pair, None), (spot_k, spot, None))
    loads = [pltpu.make_async_copy(a, b, load.at[i]) for i, (a, b, _) in enumerate(moves)]
    stores = [pltpu.make_async_copy(b, c, store.at[i]) for i, (_, b, c) in enumerate(moves[:2])]
    for c in loads:
        c.start()
    loads[0].wait()
    stores[0].start()
    for c in loads[1:]:
        c.wait()
    for i in range(2):
        at = spot[i]
        lg[at] = (lg[at].astype(F32) + pair[i]).astype(BF)
    stores[1].start()
    for c in stores:
        c.wait()


def per_device(
    latents, cotangent, clip_lengths, context_offset, conv_weight, w_query, w_key, w_value, w_out, query_gain, key_gain
):
    frames, rows, width, channels = latents.shape
    flat = (frames, rows * width, channels)
    one = (rows * width, channels)
    square = (channels, channels)
    slots = frames + 2
    clips = clip_lengths.shape[0]
    smem = lambda n: pltpu.SMEM((n,), jnp.int32)
    edge, few = VMEM((2, frames, 256), F32), VMEM((2, 8, 256), F32)
    comm = lambda: [VMEM((2, *one), BF), VMEM((2, 2, 256), F32), VMEM((2 * SPAN, *one), BF), VMEM((2 * SPAN, 2, 256), F32)]
    result = jax.ShapeDtypeStruct(flat, BF)
    out, lg, pair, spot = pl.pallas_call(
        kernel,
        name="tokenizer_block",
        out_shape=(result, result, jax.ShapeDtypeStruct((2, *one), F32), jax.ShapeDtypeStruct((2,), jnp.int32)),
        in_specs=[pl.BlockSpec(memory_space=pltpu.HBM)] * 11,
        out_specs=(pl.BlockSpec(memory_space=pltpu.HBM),) * 4,
        scratch_shapes=[smem(clips)] * 4
        + [smem(frames), smem(slots)]
        + [VMEM(flat, BF), VMEM(flat, BF), VMEM(conv_weight.shape, BF)]
        + [VMEM(square, BF)] * 4
        + [VMEM((1, channels), F32)] * 2
        + [VMEM((768, 256), BF), VMEM((512, 256), BF), VMEM((128, 384), BF), VMEM(square, BF)]
        + [VMEM(square, F32)] * 2
        + [
            VMEM(flat, BF),
            VMEM((slots, 256, 128), F32),
            VMEM((slots, 8, 128), F32),
            VMEM((frames, 128, 256), BF),
            VMEM((frames, 128, 256), BF),
            VMEM((slots, 256, 128), BF),
            VMEM((slots, 128, 256), BF),
            VMEM((frames, 128, 256), BF),
            VMEM((frames, 128, 256), BF),
            VMEM((frames + 1, 128, 128), F32),
            VMEM((frames + 1, 128, 128), F32),
            VMEM(flat, BF),
        ]
        + [edge, edge]
        + comm()
        + [edge, edge, few, few]
        + comm()
        + [
            VMEM((frames, 64, 256), F32),
            VMEM((2, frames, 256), F32),
            VMEM(flat, BF),
            VMEM(flat, BF),
            VMEM((2, *one), F32),
            smem(2),
            pltpu.SemaphoreType.DMA((11,)),
            pltpu.SemaphoreType.DMA((4,)),
            pltpu.SemaphoreType.DMA((3, 2)),
            pltpu.SemaphoreType.DMA((3, 2)),
            pltpu.SemaphoreType.DMA((4, 2 * SPAN)),
            pltpu.SemaphoreType.DMA((4, 2 * SPAN)),
        ],
        compiler_params=pltpu.CompilerParams(
            collective_id=0, has_side_effects=True, vmem_limit_bytes=60 << 20
        ),
    )(
        clip_lengths, context_offset, latents.reshape(flat), cotangent.reshape(flat), conv_weight,
        w_query, w_key, w_value, w_out, query_gain.reshape(1, channels), key_gain.reshape(1, channels),
    )
    out, lg = pl.pallas_call(
        hand_over,
        name="hand_over",
        out_shape=(result, result),
        in_specs=[pl.BlockSpec(memory_space=pl.ANY)] * 4,
        out_specs=(pl.BlockSpec(memory_space=pl.ANY),) * 2,
        scratch_shapes=[
            VMEM(flat, BF),
            VMEM(flat, BF),
            VMEM((2, *one), F32),
            smem(2),
            pltpu.SemaphoreType.DMA((4,)),
            pltpu.SemaphoreType.DMA((2,)),
        ],
        compiler_params=pltpu.CompilerParams(vmem_limit_bytes=60 << 20),
    )(out, lg, pair, spot)
    return out.reshape(latents.shape), lg.reshape(latents.shape)


def solution(mesh):
    data = P("tm", None, "space", None)
    return jax.shard_map(
        per_device,
        mesh=mesh,
        in_specs=(data, data) + (P(),) * 9,
        out_specs=(data, data),
        check_vma=False,
    )
```

```python
import jax
import jax.numpy as jnp
from jax import lax
from jax.experimental import pallas as pl
from jax.experimental.pallas import tpu as pltpu
from jax.sharding import PartitionSpec as P

HEAD = 64
SPAN = 4
GROUP = 8
STEP = 16
LOG2E = 1.4426950408889634
HOPS = (-1, -2, -3, -4, 1, 2, 3, 4)
EPS = 1e-6
MESH = pl.DeviceIdType.MESH
VMEM = pltpu.VMEM
BF = jnp.bfloat16
F32 = jnp.float32
NT = (((1,), (1,)), ((), ()))
TN = (((0,), (0,)), ((), ()))


def dot(a, b):
    return jnp.dot(a, b, preferred_element_type=F32)


def dot_nt(a, b):
    return lax.dot_general(a, b, NT, preferred_element_type=F32)


def dot_tn(a, b):
    return lax.dot_general(a, b, TN, preferred_element_type=F32)


def partners():
    x, t = lax.axis_index("space"), lax.axis_index("tm")
    nx, nt = lax.axis_size("space"), lax.axis_size("tm")
    sides = [({"space": lax.rem(x + 1, nx)}, x + 1 < nx), ({"space": lax.rem(x + nx - 1, nx)}, x >= 1)]
    ups = [({"tm": lax.rem(t + k, nt)}, t + k < nt) for k in range(1, SPAN + 1)]
    downs = [({"tm": lax.rem(t + nt - k, nt)}, t >= k) for k in range(1, SPAN + 1)]
    return sides, ups, downs


class Message:
    def __init__(self, src, dst, send, recv, to, source):
        self.copy = pltpu.make_async_remote_copy(
            src_ref=src, dst_ref=dst, send_sem=send, recv_sem=recv, device_id=to[0], device_id_type=MESH
        )
        self.to, self.source = to[1], source[1]

    def start(self):
        pl.when(self.to)(self.copy.start)

    def sent(self):
        pl.when(self.to)(self.copy.wait_send)

    def arrived(self):
        pl.when(self.source)(self.copy.wait_recv)


def to_sides(src, dst, send, recv):
    sides, _, _ = partners()
    return [Message(src.at[i], dst.at[i], send.at[i], recv.at[i], sides[i], sides[1 - i]) for i in range(2)]


def to_clip(rising, falling, dst, send, recv):
    _, ups, downs = partners()
    out = []
    for k in reversed(range(SPAN)):
        j = SPAN + k
        out.append(Message(rising, dst.at[k], send.at[k], recv.at[k], ups[k], downs[k]))
        out.append(Message(falling, dst.at[j], send.at[j], recv.at[j], downs[k], ups[k]))
    return out


def build_conv(cw_ref, w3):
    for b in range(3):
        for rin in range(2):
            for rout in range(2):
                w3[
                    b * 256 + rin * 128 : b * 256 + rin * 128 + 128, rout * 128 : rout * 128 + 128
                ] = cw_ref[rin - rout + 1, b]


def joined(ref, f):
    return jnp.concatenate([ref[f, 0:64, :], ref[f, 64:128, :]], axis=1).astype(F32)


def shifted(x, left, right):
    row = lax.broadcasted_iota(jnp.int32, (64, 1), 0)
    before = jnp.where(row == 0, left, pltpu.roll(x, 1, 0))
    after = jnp.where(row == 63, right, pltpu.roll(x, 63, 0))
    return before.astype(BF), x.astype(BF), after.astype(BF)


def conv(xs, w3):
    taps = [jnp.concatenate(shifted(*x), axis=1) for x in xs]
    taps = jnp.concatenate(taps, axis=0) if len(taps) > 1 else taps[0]
    whole = jnp.concatenate([x[0] for x in xs], axis=0) if len(xs) > 1 else xs[0][0]
    return whole + dot(taps, w3[...])


def conv_back(xs, w3):
    parts = [shifted(*x) for x in xs]
    cat = lambda i: jnp.concatenate([p[i] for p in parts], axis=0) if len(parts) > 1 else parts[0][i]
    whole = jnp.concatenate([x[0] for x in xs], axis=0) if len(xs) > 1 else xs[0][0]
    out = dot_nt(cat(0), w3[512:768, :])
    out = out + dot_nt(cat(1), w3[256:512, :])
    out = out + dot_nt(cat(2), w3[0:256, :])
    return whole + out


def put(ref, f, y):
    ref[f, 0:64, :] = y[:, :128].astype(ref.dtype)
    ref[f, 64:128, :] = y[:, 128:].astype(ref.dtype)


def edges_out(ref, f, edges, at):
    x = joined(ref, f)
    edges[0, pl.ds(at, 1), :] = x[63:64]
    edges[1, pl.ds(at, 1), :] = x[0:1]


def mask_edges(halo):
    x, nx = lax.axis_index("space"), lax.axis_size("space")
    halo[0] = jnp.where(x > 0, halo[0], 0.0)
    halo[1] = jnp.where(x < nx - 1, halo[1], 0.0)


def halo_rows(halo, f):
    return halo[0, pl.ds(f, 1), :], halo[1, pl.ds(f, 1), :]


def with_halo(ref, halo, f):
    return (joined(ref, f), *halo_rows(halo, f))


def cells(y):
    parts = []
    for i in range(y.shape[0] // 64):
        parts += [y[i * 64 : i * 64 + 64, :128], y[i * 64 : i * 64 + 64, 128:]]
    return jnp.concatenate(parts, axis=0)


def kernel(
    lens_h, offs_h, lat_h, ct_h, cw_h, wq_h, wk_h, wv_h, wo_h, qg_h, kg_h, out_h, lg_h, pair_h, spot_h,
    lens, offs, starts, targets, slots, lastf,
    lat, ct, cw, wq, wk, wv, wo, qg, kg,
    w3, stack, wcat, wot, gainq, gaink,
    hid, un, sc, qq, gg, kvt, kv, weights, grads, dk, dv, gh,
    edge_f, halo_f, ctx_f, rim_f, got_f, gotrim_f,
    edge_b, halo_b, edge_g, halo_g, ctx_b, rim_b, got_b, gotrim_b,
    conv_f, rims, out, lg, pair, spot, load_sem, store_sem, side_send, side_recv, clip_send, clip_recv,
):
    frames = lat.shape[0]
    t, nt = lax.axis_index("tm"), lax.axis_size("tm")
    first = t * frames
    last = first + frames - 1

    pairs = [
        (lens_h, lens), (offs_h, offs), (lat_h, lat), (cw_h, cw), (ct_h, ct), (wq_h, wq), (wk_h, wk),
        (wv_h, wv), (wo_h, wo), (qg_h, qg), (kg_h, kg),
    ]
    loads = [pltpu.make_async_copy(a, b, load_sem.at[i]) for i, (a, b) in enumerate(pairs)]
    for c in loads:
        c.start()
    sides, ups, downs = partners()
    barrier = pltpu.get_barrier_semaphore()
    for who, there in sides + ups + downs:

        @pl.when(there)
        def _(who=who):
            pl.semaphore_signal(barrier, inc=1, device_id=who, device_id_type=MESH)

    loads[0].wait()
    loads[1].wait()

    def scan(j, c):
        start, top, low, below, below_end, above = c
        length = lens[j]
        end = start + length
        target = start + lax.rem(offs[j], length)
        starts[j] = start
        targets[j] = target
        inside = (target >= first) & (target <= last)
        top = jnp.where(inside, target, top)
        low = jnp.where(inside, jnp.minimum(low, target), low)
        at_first = start <= first
        below = jnp.where(at_first, target, below)
        below_end = jnp.where(at_first, end, below_end)
        above = jnp.where(start <= last, target, above)
        return end, top, low, below, below_end, above

    init = (jnp.int32(0), first, last, first, first, last)
    _, top, low, below, below_end, above = lax.fori_loop(0, lens.shape[0], scan, init, unroll=4)
    top, low = top - first, low - first
    spot[0] = top
    spot[1] = low
    spots = pltpu.make_async_copy(spot, spot_h, store_sem.at[3])
    spots.start()
    up_at = jnp.clip((first - below + frames - 1) // frames, 1, SPAN) - 1
    down_at = jnp.clip((above - first) // frames, 1, SPAN) - 1 + SPAN

    loads[2].wait()
    ctx_f[0] = lat[top]
    ctx_f[1] = lat[low]
    for f in range(frames):
        edges_out(lat, f, edge_f, f)
    pl.semaphore_wait(barrier, sum(there.astype(jnp.int32) for _, there in sides + ups + downs))

    halos_f = to_sides(edge_f, halo_f, side_send.at[0], side_recv.at[0])
    frames_f = to_clip(ctx_f.at[0], ctx_f.at[1], got_f, clip_send.at[0], clip_recv.at[0])
    rims_f = to_clip(rim_f.at[0], rim_f.at[1], gotrim_f, clip_send.at[1], clip_recv.at[1])
    for m in halos_f + frames_f:
        m.start()

    def scan2(j, c):
        slot, lastof, near = c
        start, target = starts[j], targets[j]
        at = target - first
        mine = jnp.where(at < 0, frames, jnp.where(at >= frames, frames + 1, at))
        end = jnp.minimum(start + lens[j] - 1, last) - first
        slot = [jnp.where(start - first <= f, mine, s) for f, s in enumerate(slot)]
        lastof = [jnp.where(at == f, end, s) for f, s in enumerate(lastof)]
        near = [
            jnp.where(start <= (first + k * frames if k > 0 else last + k * frames), target, s)
            for k, s in zip(HOPS, near)
        ]
        return slot, lastof, near

    zero = jnp.int32(0)
    slot, lastof, near = lax.fori_loop(
        0, lens.shape[0], scan2, ([zero] * frames, [zero - 1] * frames, [zero - 1] * len(HOPS)), unroll=2
    )
    for f in range(frames):
        slots[f] = slot[f]
        lastf[f] = lastof[f]
    lastf[frames] = jnp.where(below < first, jnp.minimum(below_end - 1, last) - first, -1)
    lastf[frames + 1] = jnp.where(above > last, frames - 1, -1)
    hits = [
        (near[i] >= first) & (near[i] <= last) & ((t + k < nt) if k > 0 else (t + k >= 0))
        for i, k in enumerate(HOPS)
    ]

    for c in loads[3:]:
        c.wait()
    build_conv(cw, w3)
    stack[...] = jnp.zeros_like(stack)
    for i, w in enumerate((wq, wk, wv)):
        stack[i * 128 : i * 128 + 128, :128] = w[...].astype(F32).T.astype(BF)
        wcat[:, i * 128 : i * 128 + 128] = w[...]
    stack[384:512, 128:] = wo[...]
    wot[...] = wo[...].astype(F32).T.astype(BF)
    gainq[...] = jnp.broadcast_to(qg[...], (128, 128)).T
    gaink[...] = jnp.broadcast_to(kg[...], (128, 128)).T
    qq[...] = jnp.zeros_like(qq)
    gg[...] = jnp.zeros_like(gg)
    dk[0] = jnp.zeros((128, 128), F32)
    dv[0] = jnp.zeros((128, 128), F32)

    edgeless = jnp.zeros((1, 256), F32)

    @pl.loop(0, frames // GROUP)
    def _(g):
        y = conv([(joined(lat, g * GROUP + i), edgeless, edgeless) for i in range(GROUP)], w3)
        for i in range(GROUP):
            conv_f[g * GROUP + i] = y[i * 64 : i * 64 + 64]

    for m in halos_f:
        m.arrived()
    mask_edges(halo_f)
    for i, f in enumerate((top, low)):
        left, right = halo_rows(halo_f, f)
        rim_f[i, 0:1] = left
        rim_f[i, 1:2] = right
    for m in rims_f:
        m.start()
    left = dot(halo_f[0].astype(BF), w3[0:256, :])
    right = dot(halo_f[1].astype(BF), w3[512:768, :])
    for f in range(frames):
        conv_f[f, 0:1, :] += left[f : f + 1]
        conv_f[f, 63:64, :] += right[f : f + 1]

    def diagonal(ref, f, x):
        ref[f, :64, :128] = x[:64].astype(BF)
        ref[f, 64:, 128:] = x[64:].astype(BF)

    def per_head(x):
        return [jnp.sum(x[h * HEAD : h * HEAD + HEAD], axis=0, keepdims=True) for h in range(2)]

    def normed(x, gain, f, at):
        rows = []
        for h, total in enumerate(per_head(x * x)):
            s = lax.rsqrt(total * (1.0 / HEAD) + EPS)
            u = x[h * HEAD : h * HEAD + HEAD] * s
            un[f, at * 128 + h * HEAD : at * 128 + h * HEAD + HEAD] = u
            sc[f, at * 2 + h : at * 2 + h + 1] = s
            rows.append(u * gain[h * HEAD : h * HEAD + HEAD])
        return jnp.concatenate(rows, axis=0)

    def project(h, c, at, real):
        y = dot_nt(stack[...] if real else stack[:384], jnp.concatenate([h, c], axis=1))
        for i in range(2):
            cols = slice(i * 128, i * 128 + 128)
            f = at + i
            if real:
                diagonal(qq, f, normed(y[:128, cols], gainq[...], f, 0))
                diagonal(gg, f, y[384:, cols])
            pair_t = jnp.concatenate([normed(y[128:256, cols], gaink[...], f, 1), y[256:384, cols]], axis=0).astype(BF)
            kvt[f] = pair_t
            kv[f, :, :128] = pair_t[:128].T
            kv[f, :, 128:] = pair_t[128:].T

    @pl.loop(0, frames // GROUP)
    def _(g):
        for half in range(GROUP // 2):
            f = g * GROUP + half * 2
            h = cells(jnp.concatenate([conv_f[f], conv_f[f + 1]], axis=0).astype(BF))
            at = pl.ds(f, 2)
            hid[at] = h.reshape(2, 128, 128)
            project(h, ct[at].reshape(256, 128), f, True)

    for m in frames_f + rims_f:
        m.arrived()
    below_there, above_there = t > 0, t < nt - 1
    far = []
    for at, there in ((up_at, below_there), (down_at, above_there)):
        x = jnp.where(there, joined(got_f, at), 0.0)
        rim = jnp.where(there, gotrim_f[at], 0.0)
        far.append((x, rim[0:1], rim[1:2]))
    both = cells(conv(far, w3).astype(BF))
    project(both, both, frames, False)

    def own_head(x):
        return jnp.concatenate([x[:64, :128], x[64:, 128:]], axis=0)

    @pl.loop(0, frames // STEP)
    def _(g):
        at = [g * STEP + i for i in range(STEP)]
        slot = [slots[f] for f in at]
        same = [slots[jnp.maximum(f - 1, 0)] == s for f, s in zip(at, slot)]
        n = range(STEP)
        raised = [jnp.exp2(dot(kv[slot[i], :, :128], qq[at[i]]) * (0.125 * LOG2E)) for i in n]
        prob = [r * (1.0 / jnp.sum(r, axis=0, keepdims=True)) for r in raised]
        low_p = [p.astype(BF) for p in prob]
        gp = [dot(kv[slot[i], :, 128:], gg[at[i]]) for i in n]
        delta = [jnp.sum(gp[i] * prob[i], axis=0, keepdims=True) for i in n]
        ds = [(prob[i] * (gp[i] - delta[i])).astype(BF) for i in n]
        for i in n:
            weights[at[i]] = low_p[i]
            grads[at[i]] = ds[i]
        for acc, left, right in ((dk, qq, ds), (dv, gg, low_p)):
            terms = [dot_nt(left[at[i]], right[i]) for i in n]
            run = acc[g * STEP]
            for i in n:
                run = jnp.where(same[i], run, 0.0) + terms[i]
                acc[at[i] + 1] = run

    def norm_back(e, gain, f, at):
        e = e * (gain * 0.125)
        u = un[f, at * 128 : at * 128 + 128]
        rows = []
        for h, total in enumerate(per_head(e * u)):
            r = slice(h * HEAD, h * HEAD + HEAD)
            s = sc[f, at * 2 + h : at * 2 + h + 1]
            rows.append(s * (e[r] - u[r] * (total * (1.0 / HEAD))))
        return jnp.concatenate(rows, axis=0).astype(BF)

    def finish(at, real):
        cols = []
        for i in range(2):
            f = at + i
            until = jnp.clip(lastf[f] + 1, 0, frames)
            left = []
            if real:
                gq = own_head(dot(kvt[slots[f], :128], grads[f]))
                left = [norm_back(gq, gainq[...], f, 0)]
            cols.append(
                jnp.concatenate(left + [norm_back(dk[until], gaink[...], f, 1), dv[until].astype(BF)], axis=0)
            )
        y = dot(wcat[...] if real else wcat[:, 128:], jnp.concatenate(cols, axis=1))
        return jnp.stack([y[:, :128].T, y[:, 128:].T])

    def finish_local(g):
        for i in range(0, GROUP, 2):
            at = pl.ds(g * GROUP + i, 2)
            gh[at] = (ct[at].astype(F32) + finish(g * GROUP + i, True)).astype(BF)

    ctx_b[...] = finish(frames, False).astype(BF)
    for i in range(2):
        edges_out(ctx_b, i, edge_g, i)
    frames_b = to_clip(ctx_b.at[1], ctx_b.at[0], got_b, clip_send.at[2], clip_recv.at[2])
    rims_b = to_clip(rim_b.at[1], rim_b.at[0], gotrim_b, clip_send.at[3], clip_recv.at[3])
    halos_g = to_sides(edge_g, halo_g, side_send.at[1], side_recv.at[1])
    halos_b = to_sides(edge_b, halo_b, side_send.at[2], side_recv.at[2])
    for m in halos_g + frames_b:
        m.start()
    early = frames // GROUP // 2
    pl.loop(0, early)(finish_local)
    for m in halos_g:
        m.arrived()
    mask_edges(halo_g)
    for i in range(2):
        left, right = halo_rows(halo_g, i)
        rim_b[i, 0:1] = left
        rim_b[i, 1:2] = right
    for m in rims_b:
        m.start()
    pl.loop(early, frames // GROUP)(finish_local)
    for f in range(frames):
        edges_out(gh, f, edge_b, f)
    for m in halos_b:
        m.start()

    @pl.loop(0, frames // GROUP)
    def _(g):
        for i in range(0, GROUP, 2):
            f = g * GROUP + i
            att = [own_head(dot(kvt[slots[e], 128:], weights[e])).astype(BF) for e in (f, f + 1)]
            y = dot(wot[...], jnp.concatenate(att, axis=1))
            out[f] = (hid[f].astype(F32) + y[:, :128].T).astype(BF)
            out[f + 1] = (hid[f + 1].astype(F32) + y[:, 128:].T).astype(BF)

    stores = [pltpu.make_async_copy(out, out_h, store_sem.at[0])]
    stores[0].start()

    @pl.loop(0, frames // GROUP)
    def _(g):
        y = conv_back([(joined(gh, g * GROUP + i), edgeless, edgeless) for i in range(GROUP)], w3)
        for i in range(GROUP):
            f = g * GROUP + i
            put(lg, f, y[i * 64 : i * 64 + 64])
            rims[0, pl.ds(f, 1), :] = y[i * 64 : i * 64 + 1]
            rims[1, pl.ds(f, 1), :] = y[i * 64 + 63 : i * 64 + 64]

    for m in halos_b:
        m.arrived()
    mask_edges(halo_b)
    rims[0] += dot_nt(halo_b[0].astype(BF), w3[512:768, :])
    rims[1] += dot_nt(halo_b[1].astype(BF), w3[0:256, :])
    row = lax.broadcasted_iota(jnp.int32, (16, 1), 0)

    @pl.loop(0, frames)
    def _(f):
        for side, start, at in ((0, 0, 0), (1, 48, 15)):
            edge = rims[side, pl.ds(f, 1), :]
            for r in range(2):
                rows = slice(r * 64 + start, r * 64 + start + 16)
                tile = jnp.where(row == at, edge[:, r * 128 : r * 128 + 128], lg[f, rows, :].astype(F32))
                lg[f, rows, :] = tile.astype(BF)

    stores.append(pltpu.make_async_copy(lg, lg_h, store_sem.at[1]))
    stores[1].start()
    for m in frames_b + rims_b:
        m.arrived()
    sums = []
    for at in (SPAN, 0):
        x, rim = jnp.zeros((64, 256), F32), jnp.zeros((2, 256), F32)
        for k in range(SPAN):
            x += jnp.where(hits[at + k], joined(got_b, at + k), 0.0)
            rim += jnp.where(hits[at + k], gotrim_b[at + k], 0.0)
        sums.append((x, rim[0:1], rim[1:2]))
    pair[...] = cells(conv_back(sums, w3)).reshape(2, 128, 128)
    stores.append(pltpu.make_async_copy(pair, pair_h, store_sem.at[2]))
    stores[2].start()
    for c in stores + [spots]:
        c.wait()
    for m in halos_f + frames_f + rims_f + halos_g + frames_b + rims_b + halos_b:
        m.sent()


def hand_over(out_k, lg_k, pair_k, spot_k, out_h, lg_h, out, lg, pair, spot, load, store):
    moves = ((lg_k, lg, lg_h), (out_k, out, out_h), (pair_k, pair, None), (spot_k, spot, None))
    loads = [pltpu.make_async_copy(a, b, load.at[i]) for i, (a, b, _) in enumerate(moves)]
    stores = [pltpu.make_async_copy(b, c, store.at[i]) for i, (_, b, c) in enumerate(moves[:2])]
    for i in (2, 3, 0, 1):
        loads[i].start()
    for i in (2, 3, 0):
        loads[i].wait()
    for i in range(2):
        at = spot[i]
        lg[at] = (lg[at].astype(F32) + pair[i]).astype(BF)
    stores[0].start()
    loads[1].wait()
    stores[1].start()
    for c in stores:
        c.wait()


def per_device(
    latents, cotangent, clip_lengths, context_offset, conv_weight, w_query, w_key, w_value, w_out, query_gain, key_gain
):
    frames, rows, width, channels = latents.shape
    flat = (frames, rows * width, channels)
    one = (rows * width, channels)
    square = (channels, channels)
    slots = frames + 2
    clips = clip_lengths.shape[0]
    smem = lambda n: pltpu.SMEM((n,), jnp.int32)
    edge, few = VMEM((2, frames, 256), F32), VMEM((2, 8, 256), F32)
    comm = lambda: [VMEM((2, *one), BF), VMEM((2, 2, 256), F32), VMEM((2 * SPAN, *one), BF), VMEM((2 * SPAN, 2, 256), F32)]
    result = jax.ShapeDtypeStruct(flat, BF)
    out, lg, pair, spot = pl.pallas_call(
        kernel,
        name="tokenizer_block",
        out_shape=(result, result, jax.ShapeDtypeStruct((2, *one), F32), jax.ShapeDtypeStruct((2,), jnp.int32)),
        in_specs=[pl.BlockSpec(memory_space=pltpu.HBM)] * 11,
        out_specs=(pl.BlockSpec(memory_space=pltpu.HBM),) * 4,
        scratch_shapes=[smem(clips)] * 4
        + [smem(frames), smem(slots)]
        + [VMEM(flat, BF), VMEM(flat, BF), VMEM(conv_weight.shape, BF)]
        + [VMEM(square, BF)] * 4
        + [VMEM((1, channels), F32)] * 2
        + [VMEM((768, 256), BF), VMEM((512, 256), BF), VMEM((128, 384), BF), VMEM(square, BF)]
        + [VMEM(square, F32)] * 2
        + [
            VMEM(flat, BF),
            VMEM((slots, 256, 128), F32),
            VMEM((slots, 8, 128), F32),
            VMEM((frames, 128, 256), BF),
            VMEM((frames, 128, 256), BF),
            VMEM((slots, 256, 128), BF),
            VMEM((slots, 128, 256), BF),
            VMEM((frames, 128, 256), BF),
            VMEM((frames, 128, 256), BF),
            VMEM((frames + 1, 128, 128), F32),
            VMEM((frames + 1, 128, 128), F32),
            VMEM(flat, BF),
        ]
        + [edge, edge]
        + comm()
        + [edge, edge, few, few]
        + comm()
        + [
            VMEM((frames, 64, 256), F32),
            VMEM((2, frames, 256), F32),
            VMEM(flat, BF),
            VMEM(flat, BF),
            VMEM((2, *one), F32),
            smem(2),
            pltpu.SemaphoreType.DMA((11,)),
            pltpu.SemaphoreType.DMA((4,)),
            pltpu.SemaphoreType.DMA((3, 2)),
            pltpu.SemaphoreType.DMA((3, 2)),
            pltpu.SemaphoreType.DMA((4, 2 * SPAN)),
            pltpu.SemaphoreType.DMA((4, 2 * SPAN)),
        ],
        compiler_params=pltpu.CompilerParams(
            collective_id=0, has_side_effects=True, vmem_limit_bytes=60 << 20
        ),
    )(
        clip_lengths, context_offset, latents.reshape(flat), cotangent.reshape(flat), conv_weight,
        w_query, w_key, w_value, w_out, query_gain.reshape(1, channels), key_gain.reshape(1, channels),
    )
    out, lg = pl.pallas_call(
        hand_over,
        name="hand_over",
        out_shape=(result, result),
        in_specs=[pl.BlockSpec(memory_space=pl.ANY)] * 4,
        out_specs=(pl.BlockSpec(memory_space=pl.ANY),) * 2,
        scratch_shapes=[
            VMEM(flat, BF),
            VMEM(flat, BF),
            VMEM((2, *one), F32),
            smem(2),
            pltpu.SemaphoreType.DMA((4,)),
            pltpu.SemaphoreType.DMA((2,)),
        ],
        compiler_params=pltpu.CompilerParams(vmem_limit_bytes=60 << 20),
    )(out, lg, pair, spot)
    return out.reshape(latents.shape), lg.reshape(latents.shape)


def solution(mesh):
    data = P("tm", None, "space", None)
    return jax.shard_map(
        per_device,
        mesh=mesh,
        in_specs=(data, data) + (P(),) * 9,
        out_specs=(data, data),
        check_vma=False,
    )
```

```python
import jax
import jax.numpy as jnp
from jax import lax
from jax.experimental import pallas as pl
from jax.experimental.pallas import tpu as pltpu
from jax.sharding import PartitionSpec as P

HEAD = 64
SPAN = 4
GROUP = 8
HOPS = (-1, -2, -3, -4, 1, 2, 3, 4)
EPS = 1e-6
MESH = pl.DeviceIdType.MESH
VMEM = pltpu.VMEM
BF = jnp.bfloat16
F32 = jnp.float32
NT = (((1,), (1,)), ((), ()))
TN = (((0,), (0,)), ((), ()))


def dot(a, b):
    return jnp.dot(a, b, preferred_element_type=F32)


def dot_nt(a, b):
    return lax.dot_general(a, b, NT, preferred_element_type=F32)


def dot_tn(a, b):
    return lax.dot_general(a, b, TN, preferred_element_type=F32)


def partners():
    x, t = lax.axis_index("space"), lax.axis_index("tm")
    nx, nt = lax.axis_size("space"), lax.axis_size("tm")
    sides = [({"space": lax.rem(x + 1, nx)}, x + 1 < nx), ({"space": lax.rem(x + nx - 1, nx)}, x >= 1)]
    ups = [({"tm": lax.rem(t + k, nt)}, t + k < nt) for k in range(1, SPAN + 1)]
    downs = [({"tm": lax.rem(t + nt - k, nt)}, t >= k) for k in range(1, SPAN + 1)]
    return sides, ups, downs


class Message:
    def __init__(self, src, dst, send, recv, to, source):
        self.copy = pltpu.make_async_remote_copy(
            src_ref=src, dst_ref=dst, send_sem=send, recv_sem=recv, device_id=to[0], device_id_type=MESH
        )
        self.to, self.source = to[1], source[1]

    def start(self):
        pl.when(self.to)(self.copy.start)

    def sent(self):
        pl.when(self.to)(self.copy.wait_send)

    def arrived(self):
        pl.when(self.source)(self.copy.wait_recv)


def to_sides(src, dst, send, recv):
    sides, _, _ = partners()
    return [Message(src.at[i], dst.at[i], send.at[i], recv.at[i], sides[i], sides[1 - i]) for i in range(2)]


def to_clip(rising, falling, dst, send, recv):
    _, ups, downs = partners()
    out = []
    for k in reversed(range(SPAN)):
        j = SPAN + k
        out.append(Message(rising, dst.at[k], send.at[k], recv.at[k], ups[k], downs[k]))
        out.append(Message(falling, dst.at[j], send.at[j], recv.at[j], downs[k], ups[k]))
    return out


def build_conv(cw_ref, w3):
    for b in range(3):
        for rin in range(2):
            for rout in range(2):
                w3[
                    b * 256 + rin * 128 : b * 256 + rin * 128 + 128, rout * 128 : rout * 128 + 128
                ] = cw_ref[rin - rout + 1, b]


def joined(ref, f):
    return jnp.concatenate([ref[f, 0:64, :], ref[f, 64:128, :]], axis=1).astype(F32)


def shifted(x, left, right):
    row = lax.broadcasted_iota(jnp.int32, (64, 1), 0)
    before = jnp.where(row == 0, left, pltpu.roll(x, 1, 0))
    after = jnp.where(row == 63, right, pltpu.roll(x, 63, 0))
    return before.astype(BF), x.astype(BF), after.astype(BF)


def conv(xs, w3):
    taps = [jnp.concatenate(shifted(*x), axis=1) for x in xs]
    taps = jnp.concatenate(taps, axis=0) if len(taps) > 1 else taps[0]
    whole = jnp.concatenate([x[0] for x in xs], axis=0) if len(xs) > 1 else xs[0][0]
    return whole + dot(taps, w3[...])


def conv_back(xs, w3):
    parts = [shifted(*x) for x in xs]
    cat = lambda i: jnp.concatenate([p[i] for p in parts], axis=0) if len(parts) > 1 else parts[0][i]
    whole = jnp.concatenate([x[0] for x in xs], axis=0) if len(xs) > 1 else xs[0][0]
    out = dot_nt(cat(0), w3[512:768, :])
    out = out + dot_nt(cat(1), w3[256:512, :])
    out = out + dot_nt(cat(2), w3[0:256, :])
    return whole + out


def put(ref, f, y):
    ref[f, 0:64, :] = y[:, :128].astype(ref.dtype)
    ref[f, 64:128, :] = y[:, 128:].astype(ref.dtype)


def edges_out(ref, f, edges, at):
    x = joined(ref, f)
    edges[0, pl.ds(at, 1), :] = x[63:64]
    edges[1, pl.ds(at, 1), :] = x[0:1]


def mask_edges(halo):
    x, nx = lax.axis_index("space"), lax.axis_size("space")
    halo[0] = jnp.where(x > 0, halo[0], 0.0)
    halo[1] = jnp.where(x < nx - 1, halo[1], 0.0)


def halo_rows(halo, f):
    return halo[0, pl.ds(f, 1), :], halo[1, pl.ds(f, 1), :]


def with_halo(ref, halo, f):
    return (joined(ref, f), *halo_rows(halo, f))


def cells(y):
    parts = []
    for i in range(y.shape[0] // 64):
        parts += [y[i * 64 : i * 64 + 64, :128], y[i * 64 : i * 64 + 64, 128:]]
    return jnp.concatenate(parts, axis=0)


def kernel(
    lens_h, offs_h, lat_h, ct_h, cw_h, wq_h, wk_h, wv_h, wo_h, qg_h, kg_h, out_h, lg_h, pair_h, spot_h,
    lens, offs, starts, targets, slots, lastf,
    lat, ct, cw, wq, wk, wv, wo, qg, kg,
    w3, stack, wcat, wot, gainq, gaink,
    hid, un, sc, qq, gg, kvt, kv, weights, grads, dk, dv, gh,
    edge_f, halo_f, ctx_f, rim_f, got_f, gotrim_f,
    edge_b, halo_b, edge_g, halo_g, ctx_b, rim_b, got_b, gotrim_b,
    conv_f, rims, out, lg, pair, spot, load_sem, store_sem, side_send, side_recv, clip_send, clip_recv,
):
    frames = lat.shape[0]
    t, nt = lax.axis_index("tm"), lax.axis_size("tm")
    first = t * frames
    last = first + frames - 1

    pairs = [
        (lens_h, lens), (offs_h, offs), (lat_h, lat), (cw_h, cw), (ct_h, ct), (wq_h, wq), (wk_h, wk),
        (wv_h, wv), (wo_h, wo), (qg_h, qg), (kg_h, kg),
    ]
    loads = [pltpu.make_async_copy(a, b, load_sem.at[i]) for i, (a, b) in enumerate(pairs)]
    for c in loads:
        c.start()
    sides, ups, downs = partners()
    barrier = pltpu.get_barrier_semaphore()
    for who, there in sides + ups + downs:

        @pl.when(there)
        def _(who=who):
            pl.semaphore_signal(barrier, inc=1, device_id=who, device_id_type=MESH)

    loads[0].wait()
    loads[1].wait()

    def scan(j, c):
        start, top, low, below, below_end, above = c
        length = lens[j]
        end = start + length
        target = start + lax.rem(offs[j], length)
        starts[j] = start
        targets[j] = target
        inside = (target >= first) & (target <= last)
        top = jnp.where(inside, target, top)
        low = jnp.where(inside, jnp.minimum(low, target), low)
        at_first = start <= first
        below = jnp.where(at_first, target, below)
        below_end = jnp.where(at_first, end, below_end)
        above = jnp.where(start <= last, target, above)
        return end, top, low, below, below_end, above

    init = (jnp.int32(0), first, last, first, first, last)
    _, top, low, below, below_end, above = lax.fori_loop(0, lens.shape[0], scan, init, unroll=4)
    top, low = top - first, low - first
    spot[0] = top
    spot[1] = low
    spots = pltpu.make_async_copy(spot, spot_h, store_sem.at[3])
    spots.start()
    up_at = jnp.clip((first - below + frames - 1) // frames, 1, SPAN) - 1
    down_at = jnp.clip((above - first) // frames, 1, SPAN) - 1 + SPAN

    loads[2].wait()
    ctx_f[0] = lat[top]
    ctx_f[1] = lat[low]
    for f in range(frames):
        edges_out(lat, f, edge_f, f)
    pl.semaphore_wait(barrier, sum(there.astype(jnp.int32) for _, there in sides + ups + downs))

    halos_f = to_sides(edge_f, halo_f, side_send.at[0], side_recv.at[0])
    frames_f = to_clip(ctx_f.at[0], ctx_f.at[1], got_f, clip_send.at[0], clip_recv.at[0])
    rims_f = to_clip(rim_f.at[0], rim_f.at[1], gotrim_f, clip_send.at[1], clip_recv.at[1])
    for m in halos_f + frames_f:
        m.start()

    def scan2(j, c):
        slot, lastof, near = c
        start, target = starts[j], targets[j]
        at = target - first
        mine = jnp.where(at < 0, frames, jnp.where(at >= frames, frames + 1, at))
        end = jnp.minimum(start + lens[j] - 1, last) - first
        slot = [jnp.where(start - first <= f, mine, s) for f, s in enumerate(slot)]
        lastof = [jnp.where(at == f, end, s) for f, s in enumerate(lastof)]
        near = [
            jnp.where(start <= (first + k * frames if k > 0 else last + k * frames), target, s)
            for k, s in zip(HOPS, near)
        ]
        return slot, lastof, near

    zero = jnp.int32(0)
    slot, lastof, near = lax.fori_loop(
        0, lens.shape[0], scan2, ([zero] * frames, [zero - 1] * frames, [zero - 1] * len(HOPS)), unroll=2
    )
    for f in range(frames):
        slots[f] = slot[f]
        lastf[f] = lastof[f]
    lastf[frames] = jnp.where(below < first, jnp.minimum(below_end - 1, last) - first, -1)
    lastf[frames + 1] = jnp.where(above > last, frames - 1, -1)
    hits = [
        (near[i] >= first) & (near[i] <= last) & ((t + k < nt) if k > 0 else (t + k >= 0))
        for i, k in enumerate(HOPS)
    ]

    for c in loads[3:]:
        c.wait()
    build_conv(cw, w3)
    stack[...] = jnp.zeros_like(stack)
    for i, w in enumerate((wq, wk, wv)):
        stack[i * 128 : i * 128 + 128, :128] = w[...].astype(F32).T.astype(BF)
        wcat[:, i * 128 : i * 128 + 128] = w[...]
    stack[384:512, 128:] = wo[...]
    wot[...] = wo[...].astype(F32).T.astype(BF)
    gainq[...] = jnp.broadcast_to(qg[...], (128, 128)).T
    gaink[...] = jnp.broadcast_to(kg[...], (128, 128)).T
    qq[...] = jnp.zeros_like(qq)
    gg[...] = jnp.zeros_like(gg)
    dk[0] = jnp.zeros((128, 128), F32)
    dv[0] = jnp.zeros((128, 128), F32)

    edgeless = jnp.zeros((1, 256), F32)

    @pl.loop(0, frames // GROUP)
    def _(g):
        y = conv([(joined(lat, g * GROUP + i), edgeless, edgeless) for i in range(GROUP)], w3)
        for i in range(GROUP):
            conv_f[g * GROUP + i] = y[i * 64 : i * 64 + 64]

    for m in halos_f:
        m.arrived()
    mask_edges(halo_f)
    for i, f in enumerate((top, low)):
        left, right = halo_rows(halo_f, f)
        rim_f[i, 0:1] = left
        rim_f[i, 1:2] = right
    for m in rims_f:
        m.start()
    left = dot(halo_f[0].astype(BF), w3[0:256, :])
    right = dot(halo_f[1].astype(BF), w3[512:768, :])
    for f in range(frames):
        conv_f[f, 0:1, :] += left[f : f + 1]
        conv_f[f, 63:64, :] += right[f : f + 1]

    def diagonal(ref, f, x):
        ref[f, :64, :128] = x[:64].astype(BF)
        ref[f, 64:, 128:] = x[64:].astype(BF)

    def per_head(x):
        return [jnp.sum(x[h * HEAD : h * HEAD + HEAD], axis=0, keepdims=True) for h in range(2)]

    def normed(x, gain, f, at):
        rows = []
        for h, total in enumerate(per_head(x * x)):
            s = lax.rsqrt(total * (1.0 / HEAD) + EPS)
            u = x[h * HEAD : h * HEAD + HEAD] * s
            un[f, at * 128 + h * HEAD : at * 128 + h * HEAD + HEAD] = u
            sc[f, at * 2 + h : at * 2 + h + 1] = s
            rows.append(u * gain[h * HEAD : h * HEAD + HEAD])
        return jnp.concatenate(rows, axis=0)

    def project(h, c, at, real):
        y = dot_nt(stack[...] if real else stack[:384], jnp.concatenate([h, c], axis=1))
        for i in range(2):
            cols = slice(i * 128, i * 128 + 128)
            f = at + i
            if real:
                diagonal(qq, f, normed(y[:128, cols], gainq[...], f, 0))
                diagonal(gg, f, y[384:, cols])
            pair_t = jnp.concatenate([normed(y[128:256, cols], gaink[...], f, 1), y[256:384, cols]], axis=0).astype(BF)
            kvt[f] = pair_t
            kv[f, :, :128] = pair_t[:128].T
            kv[f, :, 128:] = pair_t[128:].T

    @pl.loop(0, frames // GROUP)
    def _(g):
        for half in range(GROUP // 2):
            f = g * GROUP + half * 2
            h = cells(jnp.concatenate([conv_f[f], conv_f[f + 1]], axis=0).astype(BF))
            at = pl.ds(f, 2)
            hid[at] = h.reshape(2, 128, 128)
            project(h, ct[at].reshape(256, 128), f, True)

    for m in frames_f + rims_f:
        m.arrived()
    below_there, above_there = t > 0, t < nt - 1
    far = []
    for at, there in ((up_at, below_there), (down_at, above_there)):
        x = jnp.where(there, joined(got_f, at), 0.0)
        rim = jnp.where(there, gotrim_f[at], 0.0)
        far.append((x, rim[0:1], rim[1:2]))
    both = cells(conv(far, w3).astype(BF))
    project(both, both, frames, False)

    def own_head(x):
        return jnp.concatenate([x[:64, :128], x[64:, 128:]], axis=0)

    @pl.loop(0, frames // GROUP)
    def _(g):
        at = [g * GROUP + i for i in range(GROUP)]
        slot = [slots[f] for f in at]
        same = [slots[jnp.maximum(f - 1, 0)] == s for f, s in zip(at, slot)]
        n = range(GROUP)
        raised = [jnp.exp(dot(kv[slot[i], :, :128], qq[at[i]]) * 0.125) for i in n]
        prob = [r * (1.0 / jnp.sum(r, axis=0, keepdims=True)) for r in raised]
        low_p = [p.astype(BF) for p in prob]
        gp = [dot(kv[slot[i], :, 128:], gg[at[i]]) for i in n]
        delta = [jnp.sum(gp[i] * prob[i], axis=0, keepdims=True) for i in n]
        ds = [(prob[i] * (gp[i] - delta[i])).astype(BF) for i in n]
        for i in n:
            weights[at[i]] = low_p[i]
            grads[at[i]] = ds[i]
        for acc, left, right in ((dk, qq, ds), (dv, gg, low_p)):
            terms = [dot_nt(left[at[i]], right[i]) for i in n]
            run = acc[g * GROUP]
            for i in n:
                run = jnp.where(same[i], run, 0.0) + terms[i]
                acc[at[i] + 1] = run

    def norm_back(e, gain, f, at):
        e = e * (gain * 0.125)
        u = un[f, at * 128 : at * 128 + 128]
        rows = []
        for h, total in enumerate(per_head(e * u)):
            r = slice(h * HEAD, h * HEAD + HEAD)
            s = sc[f, at * 2 + h : at * 2 + h + 1]
            rows.append(s * (e[r] - u[r] * (total * (1.0 / HEAD))))
        return jnp.concatenate(rows, axis=0).astype(BF)

    def finish(at, real):
        cols = []
        for i in range(2):
            f = at + i
            until = jnp.clip(lastf[f] + 1, 0, frames)
            left = []
            if real:
                gq = own_head(dot(kvt[slots[f], :128], grads[f]))
                left = [norm_back(gq, gainq[...], f, 0)]
            cols.append(
                jnp.concatenate(left + [norm_back(dk[until], gaink[...], f, 1), dv[until].astype(BF)], axis=0)
            )
        y = dot(wcat[...] if real else wcat[:, 128:], jnp.concatenate(cols, axis=1))
        return jnp.stack([y[:, :128].T, y[:, 128:].T])

    def finish_local(g):
        for i in range(0, GROUP, 2):
            at = pl.ds(g * GROUP + i, 2)
            gh[at] = (ct[at].astype(F32) + finish(g * GROUP + i, True)).astype(BF)

    ctx_b[...] = finish(frames, False).astype(BF)
    frames_b = to_clip(ctx_b.at[1], ctx_b.at[0], got_b, clip_send.at[2], clip_recv.at[2])
    for m in frames_b:
        m.start()
    for i in range(2):
        edges_out(ctx_b, i, edge_g, i)
    rims_b = to_clip(rim_b.at[1], rim_b.at[0], gotrim_b, clip_send.at[3], clip_recv.at[3])
    halos_g = to_sides(edge_g, halo_g, side_send.at[1], side_recv.at[1])
    halos_b = to_sides(edge_b, halo_b, side_send.at[2], side_recv.at[2])
    for m in halos_g:
        m.start()
    early = frames // GROUP // 2
    pl.loop(0, early)(finish_local)
    for m in halos_g:
        m.arrived()
    mask_edges(halo_g)
    for i in range(2):
        left, right = halo_rows(halo_g, i)
        rim_b[i, 0:1] = left
        rim_b[i, 1:2] = right
    for m in rims_b:
        m.start()
    pl.loop(early, frames // GROUP)(finish_local)
    for f in range(frames):
        edges_out(gh, f, edge_b, f)
    for m in halos_b:
        m.start()

    @pl.loop(0, frames // GROUP)
    def _(g):
        for i in range(0, GROUP, 2):
            f = g * GROUP + i
            att = [own_head(dot(kvt[slots[e], 128:], weights[e])).astype(BF) for e in (f, f + 1)]
            y = dot(wot[...], jnp.concatenate(att, axis=1))
            out[f] = (hid[f].astype(F32) + y[:, :128].T).astype(BF)
            out[f + 1] = (hid[f + 1].astype(F32) + y[:, 128:].T).astype(BF)

    stores = [pltpu.make_async_copy(out, out_h, store_sem.at[0])]
    stores[0].start()

    @pl.loop(0, frames // GROUP)
    def _(g):
        y = conv_back([(joined(gh, g * GROUP + i), edgeless, edgeless) for i in range(GROUP)], w3)
        for i in range(GROUP):
            f = g * GROUP + i
            put(lg, f, y[i * 64 : i * 64 + 64])
            rims[0, pl.ds(f, 1), :] = y[i * 64 : i * 64 + 1]
            rims[1, pl.ds(f, 1), :] = y[i * 64 + 63 : i * 64 + 64]

    for m in halos_b:
        m.arrived()
    mask_edges(halo_b)
    rims[0] += dot_nt(halo_b[0].astype(BF), w3[512:768, :])
    rims[1] += dot_nt(halo_b[1].astype(BF), w3[0:256, :])
    row = lax.broadcasted_iota(jnp.int32, (16, 1), 0)

    @pl.loop(0, frames)
    def _(f):
        for side, start, at in ((0, 0, 0), (1, 48, 15)):
            edge = rims[side, pl.ds(f, 1), :]
            for r in range(2):
                rows = slice(r * 64 + start, r * 64 + start + 16)
                tile = jnp.where(row == at, edge[:, r * 128 : r * 128 + 128], lg[f, rows, :].astype(F32))
                lg[f, rows, :] = tile.astype(BF)

    stores.append(pltpu.make_async_copy(lg, lg_h, store_sem.at[1]))
    stores[1].start()
    for m in frames_b + rims_b:
        m.arrived()
    sums = []
    for at in (SPAN, 0):
        x, rim = jnp.zeros((64, 256), F32), jnp.zeros((2, 256), F32)
        for k in range(SPAN):
            x += jnp.where(hits[at + k], joined(got_b, at + k), 0.0)
            rim += jnp.where(hits[at + k], gotrim_b[at + k], 0.0)
        sums.append((x, rim[0:1], rim[1:2]))
    pair[...] = cells(conv_back(sums, w3)).reshape(2, 128, 128)
    stores.append(pltpu.make_async_copy(pair, pair_h, store_sem.at[2]))
    stores[2].start()
    for c in stores + [spots]:
        c.wait()
    for m in halos_f + frames_f + rims_f + halos_g + frames_b + rims_b + halos_b:
        m.sent()


def hand_over(out_k, lg_k, pair_k, spot_k, out_h, lg_h, out, lg, pair, spot, load, store):
    moves = ((out_k, out, out_h), (lg_k, lg, lg_h), (pair_k, pair, None), (spot_k, spot, None))
    loads = [pltpu.make_async_copy(a, b, load.at[i]) for i, (a, b, _) in enumerate(moves)]
    stores = [pltpu.make_async_copy(b, c, store.at[i]) for i, (_, b, c) in enumerate(moves[:2])]
    for c in loads:
        c.start()
    loads[0].wait()
    stores[0].start()
    for c in loads[1:]:
        c.wait()
    for i in range(2):
        at = spot[i]
        lg[at] = (lg[at].astype(F32) + pair[i]).astype(BF)
    stores[1].start()
    for c in stores:
        c.wait()


def per_device(
    latents, cotangent, clip_lengths, context_offset, conv_weight, w_query, w_key, w_value, w_out, query_gain, key_gain
):
    frames, rows, width, channels = latents.shape
    flat = (frames, rows * width, channels)
    one = (rows * width, channels)
    square = (channels, channels)
    slots = frames + 2
    clips = clip_lengths.shape[0]
    smem = lambda n: pltpu.SMEM((n,), jnp.int32)
    edge, few = VMEM((2, frames, 256), F32), VMEM((2, 8, 256), F32)
    comm = lambda: [VMEM((2, *one), BF), VMEM((2, 2, 256), F32), VMEM((2 * SPAN, *one), BF), VMEM((2 * SPAN, 2, 256), F32)]
    result = jax.ShapeDtypeStruct(flat, BF)
    out, lg, pair, spot = pl.pallas_call(
        kernel,
        name="tokenizer_block",
        out_shape=(result, result, jax.ShapeDtypeStruct((2, *one), F32), jax.ShapeDtypeStruct((2,), jnp.int32)),
        in_specs=[pl.BlockSpec(memory_space=pltpu.HBM)] * 11,
        out_specs=(pl.BlockSpec(memory_space=pltpu.HBM),) * 4,
        scratch_shapes=[smem(clips)] * 4
        + [smem(frames), smem(slots)]
        + [VMEM(flat, BF), VMEM(flat, BF), VMEM(conv_weight.shape, BF)]
        + [VMEM(square, BF)] * 4
        + [VMEM((1, channels), F32)] * 2
        + [VMEM((768, 256), BF), VMEM((512, 256), BF), VMEM((128, 384), BF), VMEM(square, BF)]
        + [VMEM(square, F32)] * 2
        + [
            VMEM(flat, BF),
            VMEM((slots, 256, 128), F32),
            VMEM((slots, 8, 128), F32),
            VMEM((frames, 128, 256), BF),
            VMEM((frames, 128, 256), BF),
            VMEM((slots, 256, 128), BF),
            VMEM((slots, 128, 256), BF),
            VMEM((frames, 128, 256), BF),
            VMEM((frames, 128, 256), BF),
            VMEM((frames + 1, 128, 128), F32),
            VMEM((frames + 1, 128, 128), F32),
            VMEM(flat, BF),
        ]
        + [edge, edge]
        + comm()
        + [edge, edge, few, few]
        + comm()
        + [
            VMEM((frames, 64, 256), F32),
            VMEM((2, frames, 256), F32),
            VMEM(flat, BF),
            VMEM(flat, BF),
            VMEM((2, *one), F32),
            smem(2),
            pltpu.SemaphoreType.DMA((11,)),
            pltpu.SemaphoreType.DMA((4,)),
            pltpu.SemaphoreType.DMA((3, 2)),
            pltpu.SemaphoreType.DMA((3, 2)),
            pltpu.SemaphoreType.DMA((4, 2 * SPAN)),
            pltpu.SemaphoreType.DMA((4, 2 * SPAN)),
        ],
        compiler_params=pltpu.CompilerParams(
            collective_id=0, has_side_effects=True, vmem_limit_bytes=60 << 20
        ),
    )(
        clip_lengths, context_offset, latents.reshape(flat), cotangent.reshape(flat), conv_weight,
        w_query, w_key, w_value, w_out, query_gain.reshape(1, channels), key_gain.reshape(1, channels),
    )
    out, lg = pl.pallas_call(
        hand_over,
        name="hand_over",
        out_shape=(result, result),
        in_specs=[pl.BlockSpec(memory_space=pl.ANY)] * 4,
        out_specs=(pl.BlockSpec(memory_space=pl.ANY),) * 2,
        scratch_shapes=[
            VMEM(flat, BF),
            VMEM(flat, BF),
            VMEM((2, *one), F32),
            smem(2),
            pltpu.SemaphoreType.DMA((4,)),
            pltpu.SemaphoreType.DMA((2,)),
        ],
        compiler_params=pltpu.CompilerParams(vmem_limit_bytes=60 << 20),
    )(out, lg, pair, spot)
    return out.reshape(latents.shape), lg.reshape(latents.shape)


def solution(mesh):
    data = P("tm", None, "space", None)
    return jax.shard_map(
        per_device,
        mesh=mesh,
        in_specs=(data, data) + (P(),) * 9,
        out_specs=(data, data),
        check_vma=False,
    )
```
